32 devices in a mesh: dp: 2 (over core), seq: 16 (over z, y, x).
Axes of the slice: x: 2, y: 2, z: 4, core: 2. Of those that a mesh axis runs over, the one named last changes fastest.
Arguments:
- byte_ids: int32 [32, 4096], P('dp', 'seq'), may hold values from 0 to 255
- lengths: int32 [32], P('dp'), may hold values from 1024 to 4096, as said below
- embedding: float32 [256, 768], replicated, may hold values from -6 to 6
- conv_weight: float32 [4, 768], replicated, may hold values from -3 to 3
- conv_bias: float32 [768], replicated, may hold values from -3 to 3
- score_weight: float32 [768], replicated, may hold values from -0.5 to 0.5
- cotangent: float32 [32, 2048, 768], P('dp', 'seq'), may hold values from -6 to 6
Outputs:
- latent: float32 [32, 2048, 768], P('dp', 'seq')
- grad_embedding: float32 [256, 768], replicated
- grad_conv_weight: float32 [4, 768], replicated
- grad_conv_bias: float32 [768], replicated
- grad_score_weight: float32 [768], replicated
The draws below stay inside these ranges and needn't reach their ends.
Inputs may be any that keep to these rules, and one draw needn't show every extreme that they name: `lengths`: among the 16 rows of each index of dp one has length 4096 and one has length 1024, which ones drawn from the seed.
All inputs are finite; a program needn't handle non-finite values.
Results may differ from the reference program's by a relative error of at most 0.0003.
Values sent between devices are 32-bit elements; how exact they have to be, the bound alone decides.
No kernel may reach another device: no remote copies, remote signals or barrier semaphores. Data moves between devices by JAX's collectives and lax.ppermute only.
A program may use at most 448 MiB of HBM per device.

```python
import math
import jax
import jax.numpy as jnp
import numpy as np
from jax import lax

D = 768
VOCAB = 256
KERNEL = 4
BLOCKS = 4
LEN = 4096
ROWS_DEV = 16
ROWS = 32
HALF = 2048


def draw_lengths(key, part):
    key = jax.random.fold_in(key, 11)
    key_full, key_short, key_rest = jax.random.split(key, 3)
    groups = ROWS // ROWS_DEV
    full = jax.random.randint(key_full, (groups, 1), 0, ROWS_DEV)
    short = (full + jax.random.randint(key_short, (groups, 1), 1, ROWS_DEV)) % ROWS_DEV
    rest = jax.random.randint(key_rest, (groups, ROWS_DEV), LEN // 4, LEN + 1)
    slot = jnp.arange(ROWS_DEV)[None, :]
    values = jnp.where(slot == full, LEN, jnp.where(slot == short, LEN // 4, rest))
    return values.reshape(ROWS).astype(jnp.int32)


def place_ends(array, key, smallest, largest):
    longest = array.shape.index(max(array.shape))
    spots = []
    for shift in (0, 1):
        where = [jax.random.randint(jax.random.fold_in(key, axis), (), 0, length) for axis, length in enumerate(array.shape)]
        where[longest] = (where[longest] + shift) % array.shape[longest]
        spots.append(tuple(where))
    return array.at[spots[0]].set(smallest).at[spots[1]].set(largest)


def levels(key, extent, cuts, smallest, high):
    factor_of, own = 1.0, jax.random.fold_in(key, 6)
    for dim, blocks in cuts:
        draws = jnp.exp(jax.random.uniform(jax.random.fold_in(own, dim), (blocks,), jnp.float32, smallest / len(cuts), high / len(cuts)))
        factor_of = factor_of * jnp.repeat(draws, extent[dim] // blocks).reshape([-1 if axis == dim else 1 for axis in range(len(extent))])
    return factor_of


def rank_bounds(count, skew):
    portions = [(1 << 20) // math.isqrt(rank ** skew) + 1 for rank in range(1, count + 1)]
    spread = 1 + sum(portions) // (1 << 30)
    return np.cumsum(np.array([max(1, weight // spread) for weight in portions]))


def ranked_ids(own_key, dims, number_of, slope):
    listing = rank_bounds(number_of, slope)
    lot = jax.random.randint(jax.random.fold_in(own_key, 1), dims, 0, int(listing[number_of - 1]))
    grade = jnp.searchsorted(jnp.asarray(listing, jnp.int32), lot, side="right")
    return jax.random.permutation(jax.random.fold_in(own_key, 2), number_of)[grade].astype(jnp.int32)


def normal_values(key, shape, deviation, limit, cuts=(), kind=jnp.bfloat16):
    entries = deviation * jax.random.normal(key, shape, jnp.float32)
    if cuts:
        entries = entries * levels(key, shape, cuts, -0.22, 0.18)
    return jnp.clip(entries, -limit, limit).astype(kind)


def setup_inputs(seed: int = 0) -> dict:
    keys = jax.random.split(jax.random.key(seed), 8)
    byte_ids = place_ends(ranked_ids(keys[0], (ROWS, LEN), VOCAB, 1), jax.random.fold_in(keys[0], 3), 0, VOCAB - 1).astype(jnp.int32)
    lengths = draw_lengths(jax.random.fold_in(keys[7], 71), 0)
    embedding = normal_values(keys[2], (VOCAB, D), 1.0, 6.0, (), jnp.float32)
    conv_weight = normal_values(keys[3], (KERNEL, D), KERNEL ** -0.5, 3.0, (), jnp.float32)
    conv_bias = normal_values(keys[4], (D,), 0.5, 3.0, (), jnp.float32)
    score_weight = normal_values(keys[5], (D,), 0.08, 0.5, (), jnp.float32)
    cotangent = normal_values(keys[6], (ROWS, HALF, D), 1.0, 6.0, ((0, 2), (1, 16)), jnp.float32)
    return {"byte_ids": byte_ids, "lengths": lengths, "embedding": embedding, "conv_weight": conv_weight, "conv_bias": conv_bias, "score_weight": score_weight, "cotangent": cotangent}


@jax.custom_vjp
def low(v):
    return lax.optimization_barrier(v.astype(jnp.bfloat16)).astype(jnp.float32)

@jax.custom_vjp
def low_back(v):
    return v

def low_keep(v):
    return (low(v), None)

def low_pass(kept, grad):
    return (grad,)

def back_keep(v):
    return (v, None)

def back_low(kept, grad):
    return (low(grad),)
low.defvjp(low_keep, low_pass)
low_back.defvjp(back_keep, back_low)

def forward_row(table, weight, bias, scorer, ids, length):
    positions = jnp.arange(LEN)
    live = (positions < length).astype(jnp.float32)[:, None]
    embedded = jnp.take(table, ids, axis=0) * live
    padded = jnp.pad(embedded, ((2, 1), (0, 0)))
    conv = bias[None, :] + sum((weight[k][None, :] * padded[k:k + LEN] for k in range(KERNEL)))
    conv = conv * live
    pooled = []
    for size in range(1, BLOCKS + 1):
        total = -(-LEN // size) * size
        wide = jnp.pad(conv, ((0, total - LEN), (0, 0)))
        means = lax.optimization_barrier(jnp.mean(wide.reshape(total // size, size, D), axis=1))
        pooled.append(jnp.repeat(means, size, axis=0)[:LEN])
    stack = jnp.stack(pooled)
    scores = jnp.dot(stack, scorer, precision=lax.Precision.HIGHEST)
    weights = jax.nn.softmax(scores, axis=0)
    mixed = lax.optimization_barrier(jnp.sum(weights[:, :, None] * stack, axis=0))
    return lax.optimization_barrier(jnp.mean(mixed.reshape(HALF, 2, D), axis=1))

def reference(byte_ids, lengths, embedding, conv_weight, conv_bias, score_weight, cotangent):

    def step(carry, item):
        ids, length, grad_out = item

        def forward(table, weight, bias, scorer):
            return forward_row(table, weight, bias, scorer, ids, length)
        out, back = jax.vjp(forward, embedding, conv_weight, conv_bias, score_weight)
        grads = back(grad_out)
        carry = tuple((c + g for c, g in zip(carry, grads)))
        return (carry, out)
    init = (jnp.zeros((VOCAB, D), jnp.float32), jnp.zeros((KERNEL, D), jnp.float32), jnp.zeros((D,), jnp.float32), jnp.zeros((D,), jnp.float32))
    grads, latent = lax.scan(step, init, (byte_ids, lengths, cotangent))
    return (latent, grads[0], grads[1], grads[2], grads[3])
```

```python
import functools

import jax
import jax.numpy as jnp
from jax import lax
from jax.experimental import pallas as pl
from jax.experimental.pallas import tpu as pltpu
from jax.sharding import PartitionSpec as P

F32, BF16, I32 = jnp.float32, jnp.bfloat16, jnp.int32
HIGH = lax.Precision.HIGHEST
ROWS = 16
TAPS = 4
RELS = (-2, -1, 0, 1, 2, 3)
VMEM = pltpu.CompilerParams(vmem_limit_bytes=60 * 1024 * 1024)
NT = (((1,), (1,)), ((), ()))
TN = (((0,), (0,)), ((), ()))


def lanes(shape):
    return lax.broadcasted_iota(I32, shape, 1)


def pick(x, index):
    return jnp.take_along_axis(x, index, axis=1, mode="promise_in_bounds")


def split(x):
    high = x.astype(BF16)
    return high, (x - high.astype(F32)).astype(BF16)


def dot(a, b, dims=(((1,), (0,)), ((), ()))):
    return lax.dot_general(a, b, dims, preferred_element_type=F32)


def ahead(x):
    lane = lanes(x.shape) % 8
    below = pltpu.roll(x, x.shape[0] - 1, 0)
    return jnp.where(lane == 7, pltpu.roll(below, 7, 1), pltpu.roll(x, 127, 1))


def behind(x):
    lane = lanes(x.shape) % 8
    above = pltpu.roll(x, 1, 0)
    return jnp.where(lane == 0, pltpu.roll(above, 121, 1), pltpu.roll(x, 1, 1))


def geometry(shape, start, len_ref):
    lane = lanes(shape)
    window = lax.broadcasted_iota(I32, shape, 0) - 8
    even = start + 16 * window + 2 * (lane % 8)
    length = jnp.zeros(shape, I32)
    for r in range(ROWS):
        length = jnp.where(lane // 8 == r, len_ref[r], length)
    return even, length


def alive(pos, length):
    return (pos >= 0) & (pos < length)


def members(even, parity):
    offset = (even + parity) % 3
    left = (even // 2) % 2 == 0
    out = [[((parity,), None)], [((0, 1), None)], [], []]
    for o in range(3):
        out[2].append((tuple(parity - o + i for i in range(3)), offset == o))
    out[3] = [((0, 1, 2, 3), left), ((-2, -1, 0, 1), ~left)]
    return out


def to_chunks(xe, xo, g):
    lane = lanes(xe.shape)
    place = (lane // 8 + 12) % 16
    index = g * 64 + (lane % 8) * 8 + place // 2
    y = jnp.where(place % 2 == 0, pick(xe, index), pick(xo, index))
    return jnp.where(lane < 32, pltpu.roll(y, 1, 0), y)[8:]


def prep_kernel(e_ref, w_ref, b_ref, s_ref, t_ref):
    scaled = w_ref[...] * s_ref[...]
    wide = jnp.concatenate([scaled, jnp.zeros_like(scaled)], axis=0)
    t = lax.dot_general(wide, e_ref[...], NT, precision=HIGH, preferred_element_type=F32)
    b0 = jnp.sum(b_ref[...] * s_ref[...], axis=1, keepdims=True)
    row = lax.broadcasted_iota(I32, t.shape, 0)
    t_ref[...] = jnp.where(row == TAPS, b0, t)


def weigh(start, len_ref, ids_scr, t_ref):
    shape = (ids_scr.shape[0], 128)
    lane = lanes(shape)
    even, length = geometry(shape, start, len_ref)
    live = [alive(even, length), alive(even + 1, length)]
    ids, terms = [], []
    for e in range(2):
        index = ((lane // 8) % 8) * 16 + 2 * (lane % 8) + e
        found = jnp.where(
            lane < 64, pick(ids_scr[:, :128], index), pick(ids_scr[:, 128:], index)
        )
        taps = []
        for k in range(TAPS):
            value = jnp.zeros(shape, F32)
            for half in range(t_ref.shape[1] // 128):
                row = jnp.broadcast_to(t_ref[k : k + 1, half * 128 : half * 128 + 128], shape)
                here = (found >= half * 128) & (found < half * 128 + 128)
                value = jnp.where(here, pick(row, found & 127), value)
            taps.append(jnp.where(live[e], value, 0.0))
        terms.append(taps)
        ids.append(jnp.where(live[e], found, -1))
    b0 = t_ref[TAPS : TAPS + 1, :128]
    (ae, ao) = terms
    ce = jnp.where(live[0], b0 + behind(ae[0] + ao[1]) + ae[2] + ao[3], 0.0)
    co = jnp.where(live[1], b0 + behind(ao[0]) + ae[1] + ao[2] + ahead(ae[3]), 0.0)
    at = {-2: behind(ce), -1: behind(co), 0: ce, 1: co, 2: ahead(ce), 3: ahead(co)}
    weights = []
    for e in range(2):
        scores = []
        for b, cases in enumerate(members(even, e)):
            total = None
            for rels, where in cases:
                part = sum(at[r] for r in rels)
                total = part if total is None else jnp.where(where, part, total)
            scores.append(total * (1.0 / (b + 1)))
        top = functools.reduce(jnp.maximum, scores)
        parts = [jnp.exp(s - top) for s in scores]
        norm = sum(parts)
        weights.append([p / norm for p in parts])
    return ids, weights, even, length


def spread(values, even):
    out = {r: 0.0 for r in RELS}
    for e in range(2):
        for b, cases in enumerate(members(even, e)):
            share = values[e][b] * (1.0 / (b + 1))
            for rels, where in cases:
                part = share if where is None else jnp.where(where, share, 0.0)
                for r in rels:
                    out[r] = out[r] + part
    return out


def banded(bands_ref, g, w, count):
    shape = (160, 128)
    row = lax.broadcasted_iota(I32, shape, 0)
    lane = lanes(shape)
    rel = jnp.where(row % 8 == (lane % 64) // 8, row // 8 - 2 - 2 * (lane % 8), 99)
    out = jnp.zeros(shape, F32)
    for i, r in enumerate(RELS):
        line = bands_ref[pl.ds((g * len(RELS) + i) * count + w, 1), :]
        out = jnp.where(rel == r, line, out)
    high = out.astype(BF16).astype(F32)
    return jnp.where(lane < 64, high, out - high).astype(BF16)


def store_bands(bands, bands_ref, count):
    lane = lanes(bands[0].shape)
    for i, r in enumerate(RELS):
        turned = pltpu.roll(bands[r], 64, 1)
        for g in range(2):
            both = jnp.where((lane < 64) == (g == 0), bands[r], turned)
            at = (g * len(RELS) + i) * count
            bands_ref[at : at + count, :] = both[8 : 8 + count]


def one_hot_t(line, vocab):
    return jnp.where(
        lax.broadcasted_iota(I32, (vocab, 128), 0) == line, 1.0, 0.0
    ).astype(BF16)


def window_grads(ct_ref, hl, d_ref, d_base, g, w):
    wide = jnp.concatenate([hl, hl], axis=1)
    width = ct_ref.shape[2]
    base = pl.multiple_of(d_base + 128 * w + 48, 16)
    for n in range(0, width, 256):
        ct = ct_ref[pl.ds(g * 8, 8), pl.ds(pl.multiple_of(8 * w, 8), 8), n : n + 256]
        high, low = split(ct.reshape(64, 256))
        grads = dot(wide, jnp.concatenate([high, high, low, low], axis=0))
        d_ref[pl.ds(base, 32), n : n + 256] += grads[:32]
        d_ref[pl.ds(base + 32, 128), n : n + 256] = grads[32:]


def table_kernel(
    start_ref, len_ref, ids_ref, left_ref, right_ref, t_ref, w_ref, ct_ref,
    grad_ref, weights_ref, chunks_ref,
    ids_scr, bands_ref, d_ref, oh_ref, high_ref, low_ref,
):
    count = ids_ref.shape[0]
    chunks = count + 1
    vocab = t_ref.shape[1]
    start = start_ref[0]
    ids_scr[...] = jnp.zeros_like(ids_scr)
    ids_scr[7:8] = left_ref[...]
    ids_scr[8 : 8 + count] = ids_ref[...]
    ids_scr[8 + count : 9 + count] = right_ref[...]
    ids, weights, even, length = weigh(start, len_ref, ids_scr, t_ref)
    for e in range(2):
        for b in range(4):
            weights_ref[e * 4 + b] = weights[e][b]
    bands = spread(weights, even)
    for r in RELS:
        bands[r] = jnp.where(alive(even + r, length), 0.5 * bands[r], 0.0)
    store_bands(bands, bands_ref, count)
    per = chunks_ref.shape[0] // 2
    for g in range(2):
        chunks_ref[g * per : g * per + per, :] = to_chunks(ids[0], ids[1], g)
    rows = d_ref.shape[0] // 2
    for g in range(2):
        d_ref[g * rows : g * rows + 80, :] = jnp.zeros((80, d_ref.shape[1]), F32)
        d_ref[(g + 1) * rows - 64 : (g + 1) * rows, :] = jnp.zeros((64, d_ref.shape[1]), F32)

    def table_part(g, c, size):
        d_at = pl.multiple_of(g * rows + 128 * c + 24, 8)
        to = pl.multiple_of((g * chunks + c) * 128, 128)
        for i in range(0, size, 16):
            near = [d_ref[pl.ds(d_at + i + 8 * k, 16), :] for k in range(TAPS)]
            total = sum(w_ref[3 - k : 4 - k, :] * near[k] for k in range(TAPS))
            high, low = split(total)
            high_ref[pl.ds(to + i, 16), :] = high
            low_ref[pl.ds(to + i, 16), :] = low
        for i in range(size, 128, 16):
            zero = jnp.zeros((16, d_ref.shape[1]), BF16)
            high_ref[pl.ds(to + i, 16), :] = zero
            low_ref[pl.ds(to + i, 16), :] = zero
        oh_ref[:, pl.ds(to, 128)] = one_hot_t(chunks_ref[pl.ds(g * per + c, 1), :], vocab)

    for g in range(2):

        @pl.loop(0, count)
        def _(w):
            hl = banded(bands_ref, g, w, count)
            window_grads(ct_ref, hl, d_ref, g * rows, g, w)
            table_part(g, w, 128)

        table_part(g, count, 64)

    for n in range(0, grad_ref.shape[1], 256):
        grad_ref[:, n : n + 256] = dot(oh_ref[...], high_ref[:, n : n + 256]) + dot(
            oh_ref[...], low_ref[:, n : n + 256]
        )


def mix_kernel(
    start_ref, len_ref, weights_ref, chunks_ref, e_ref, w_ref, b_ref, ct_ref,
    latent_ref, small_ref,
    bands_ref, d_ref, oh_ref, x_ref, high_ref, low_ref, near_ref, q_ref,
):
    padded = weights_ref.shape[1]
    count = ct_ref.shape[1] // 8
    chunks = count + 1
    vocab, width = e_ref.shape
    start = start_ref[0]
    even, length = geometry((padded, 128), start, len_ref)
    weights = [[weights_ref[e * 4 + b] for b in range(4)] for e in range(2)]
    bands = spread(weights, even)
    for r in RELS:
        bands[r] = jnp.where(alive(even + r, length), 0.5 * bands[r], 0.0)
    store_bands(bands, bands_ref, count)
    per = chunks_ref.shape[0] // 2
    e_high, e_low = split(e_ref[...])
    d_ref[0:80, :] = jnp.zeros((80, width), F32)
    small_ref[...] = jnp.zeros_like(small_ref)
    near_ref[...] = jnp.zeros_like(near_ref)
    shape = (160, 128)
    row, lane = lax.broadcasted_iota(I32, shape, 0), lanes(shape)

    for g in range(2):
        d_ref[48:80, :] = jnp.zeros((32, width), F32)

        @pl.loop(0, chunks)
        def _(c):
            oh = one_hot_t(chunks_ref[pl.ds(g * per + c, 1), :], vocab)
            oh_ref[:, pl.ds(pl.multiple_of((g * chunks + c) * 128, 128), 128)] = oh
            to = pl.multiple_of(c * 128, 128)
            for n in range(0, width, 256):
                x_ref[pl.ds(to, 128), n : n + 256] = dot(oh, e_high[:, n : n + 256], TN) + dot(
                    oh, e_low[:, n : n + 256], TN
                )

        @pl.loop(0, count)
        def _(w):
            hl = banded(bands_ref, g, w, count)
            window_grads(ct_ref, hl, d_ref, 0, g, w)

        def conv_part(c, size):
            at = pl.multiple_of(c * 128, 128)
            sums = [jnp.zeros((8, width), F32) for _ in range(TAPS + 1)]
            for i in range(0, size, 16):
                d = d_ref[pl.ds(at + 48 + i, 16), :]
                total = b_ref[...]
                sums[TAPS] = sums[TAPS] + d[:8] + d[8:]
                for k in range(TAPS):
                    x = x_ref[pl.ds(at + i + 8 * k, 16), :]
                    total = total + w_ref[k : k + 1, :] * x
                    p = d * x
                    sums[k] = sums[k] + p[:8] + p[8:]
                high, low = split(total)
                high_ref[pl.ds(at + i, 16), :] = high
                low_ref[pl.ds(at + i, 16), :] = low
            for k in range(TAPS + 1):
                small_ref[k : k + 1, :] += jnp.sum(sums[k], axis=0, keepdims=True)

        @pl.loop(0, count)
        def _(c):
            conv_part(c, 128)

        conv_part(count, 32)

        @pl.loop(0, count)
        def _(w):
            hl = banded(bands_ref, g, w, count)
            band = hl.astype(F32).T.astype(BF16)
            at = pl.multiple_of(w * 128, 128)
            u_at = pl.multiple_of(8 * w, 8)
            for n in range(0, width, 256):
                both = dot(band, high_ref[pl.ds(at, 160), n : n + 256])
                rest = dot(band[:64], low_ref[pl.ds(at, 160), n : n + 256])
                out = both[:64] + both[64:] + rest
                latent_ref[pl.ds(g * 8, 8), pl.ds(u_at, 8), n : n + 256] = out.reshape(8, 8, 256)
            ct = ct_ref[pl.ds(g * 8, 8), pl.ds(u_at, 8), :].reshape(64, width)
            ct = jnp.concatenate(split(ct), axis=0)
            product = dot(high_ref[pl.ds(at, 160), :], ct, NT) + dot(
                low_ref[pl.ds(at, 160), :], ct, NT
            )
            rel = jnp.where(row % 8 == (lane % 64) // 8, row // 8 - 2 - 2 * (lane % 8), 99)
            for i, r in enumerate(RELS):
                line = jnp.sum(jnp.where(rel == r, product, 0.0), axis=0, keepdims=True)
                line = line + pltpu.roll(line, 64, 1)
                keep = (lanes((1, 128)) < 64) == (g == 0)
                near_ref[i, pl.ds(8 + w, 1), :] = jnp.where(
                    keep, line, near_ref[i, pl.ds(8 + w, 1), :]
                )

    near = {}
    for i, r in enumerate(RELS):
        near[r] = jnp.where(alive(even + r, length), 0.5 * near_ref[i], 0.0)
    d_scores = []
    for e in range(2):
        d_weights = []
        for b, cases in enumerate(members(even, e)):
            total = None
            for rels, where in cases:
                part = sum(near[r] for r in rels)
                total = part if total is None else jnp.where(where, part, total)
            d_weights.append(total * (1.0 / (b + 1)))
        mean = sum(weights[e][b] * d_weights[b] for b in range(4))
        d_scores.append([weights[e][b] * (d_weights[b] - mean) for b in range(4)])
    own = lax.broadcasted_iota(I32, (padded, 128), 0) - 8
    own = (own >= 0) & (own < count)
    q = spread(d_scores, even)
    for r in RELS:
        q[r] = jnp.where(own & alive(even + r, length), q[r], 0.0)
    qe = q[0] + behind(q[2]) + ahead(q[-2])
    qo = q[1] + behind(q[3]) + ahead(q[-1])
    q_sum = jnp.sum(jnp.sum(qe + qo, axis=0, keepdims=True), axis=1, keepdims=True)
    shifted = [
        (ahead(qe), ahead(qo)),
        (qo, ahead(qe)),
        (qe, qo),
        (behind(qo), qe),
    ]
    q_ref[...] = jnp.zeros_like(q_ref)
    for g in range(2):
        for k in range(TAPS):
            flat = to_chunks(*shifted[k], g)
            for c in range(chunks):
                at = (g * chunks + c) * 128
                q_ref[k : k + 1, at : at + 128] = flat[c : c + 1]
    q1, rest = q_ref[...].astype(BF16), q_ref[...]
    rest = rest - q1.astype(F32)
    q2 = rest.astype(BF16)
    q3 = (rest - q2.astype(F32)).astype(BF16)
    hist = dot(jnp.concatenate([q1, q2, q3], axis=0), oh_ref[...], NT)
    hist = hist[:8] + hist[8:16] + hist[16:]
    for k in range(TAPS):
        at = k * vocab
        small_ref[5 + at // width : 6 + at // width, at % width : at % width + vocab] = hist[k : k + 1]
    at = TAPS * vocab
    small_ref[5 + at // width : 6 + at // width, at % width : at % width + 128] = (
        jnp.broadcast_to(q_sum, (1, 128))
    )


def final_kernel(sum_ref, small_ref, e_ref, w_ref, b_ref, s_ref, ge_ref, gw_ref, gb_ref, gs_ref):
    vocab, width = e_ref.shape
    hist = []
    for k in range(TAPS):
        at = k * vocab
        hist.append(small_ref[5 + at // width : 6 + at // width, at % width : at % width + vocab])
    at = TAPS * vocab
    q_sum = small_ref[5 + at // width : 6 + at // width, at % width : at % width + 1]
    zero = jnp.zeros((8 - TAPS, vocab), F32)
    hist = jnp.concatenate(hist + [zero], axis=0)
    scaled = w_ref[...] * s_ref[...]
    scaled = jnp.concatenate([scaled, jnp.zeros((8 - TAPS, width), F32)], axis=0)
    ge_ref[...] = sum_ref[...] + lax.dot_general(
        hist, scaled, TN, precision=HIGH, preferred_element_type=F32
    )
    looked = jnp.dot(hist, e_ref[...], precision=HIGH, preferred_element_type=F32)[:TAPS]
    gw_ref[...] = small_ref[0:TAPS, :] + looked * s_ref[...]
    gb_ref[...] = small_ref[TAPS : TAPS + 1, :] + q_sum * s_ref[...]
    gs_ref[...] = q_sum * b_ref[...] + jnp.sum(looked * w_ref[...], axis=0, keepdims=True)


def partners(axis, mask):
    return [(i, i ^ mask) for i in range(lax.axis_size(axis))]


def part(v, index, size):
    return lax.dynamic_slice_in_dim(v, index * size, size, 0)


def scatter_sum(v, axis, low, bits):
    group = 1 << bits
    size = v.shape[0] // group
    me = (lax.axis_index(axis) >> low) & (group - 1)
    total = part(v, me, size)
    for m in range(1, group):
        total = total + lax.ppermute(part(v, me ^ m, size), axis, partners(axis, m << low))
    return total


def exchange_sum(v, axis, low, bits):
    return v + sum(
        lax.ppermute(v, axis, partners(axis, m << low)) for m in range(1, 1 << bits)
    )


def gather_back(v, small, axis, low, bits):
    group = 1 << bits
    size = v.shape[0]
    me = (lax.axis_index(axis) >> low) & (group - 1)
    both = jnp.concatenate([v, small], axis=0)
    out = jnp.zeros((group * size,) + v.shape[1:], v.dtype)
    out = lax.dynamic_update_slice_in_dim(out, v, me * size, 0)
    for m in range(1, group):
        got = lax.ppermute(both, axis, partners(axis, m << low))
        out = lax.dynamic_update_slice_in_dim(out, got[:size], (me ^ m) * size, 0)
        small = small + got[size:]
    return out, small


def per_device(byte_ids, lengths, embedding, conv_weight, conv_bias, score_weight, cotangent):
    rows, span = byte_ids.shape
    vocab, width = embedding.shape
    count = span // 16
    chunks = count + 1
    per = -(-chunks // 8) * 8
    padded = 8 + per
    half = span // 2
    seq = lax.axis_size("seq")
    start = (lax.axis_index("seq") * span).reshape(1)
    bias, scorer = conv_bias.reshape(1, width), score_weight.reshape(1, width)

    ids = byte_ids.reshape(rows, count, 16).transpose(1, 0, 2).reshape(count, rows * 16)
    up = [(i, i + 1) for i in range(seq - 1)]
    left = lax.ppermute(ids[-1:], "seq", up)
    right = lax.ppermute(ids[:1], "seq", [(j, i) for i, j in up])
    vm = pl.BlockSpec(memory_space=pltpu.VMEM)
    sm = pl.BlockSpec(memory_space=pltpu.SMEM)
    table_scores = pl.pallas_call(
        prep_kernel,
        out_shape=jax.ShapeDtypeStruct((8, vocab), F32),
        in_specs=[vm] * 4,
        out_specs=vm,
        name="prep",
    )(embedding, conv_weight, bias, scorer)

    d_rows = (span + 16) * 8
    grad_table, weights, id_chunks = pl.pallas_call(
        table_kernel,
        out_shape=(
            jax.ShapeDtypeStruct((vocab, width), F32),
            jax.ShapeDtypeStruct((8, padded, 128), F32),
            jax.ShapeDtypeStruct((2 * per, 128), I32),
        ),
        in_specs=[sm, sm] + [vm] * 6,
        out_specs=(vm, vm, vm),
        scratch_shapes=[
            pltpu.VMEM((padded, 256), I32),
            pltpu.VMEM((12 * count, 128), F32),
            pltpu.VMEM((2 * d_rows, width), F32),
            pltpu.VMEM((vocab, 2 * chunks * 128), BF16),
            pltpu.VMEM((2 * chunks * 128, width), BF16),
            pltpu.VMEM((2 * chunks * 128, width), BF16),
        ],
        compiler_params=VMEM,
        name="table_grad",
    )(start, lengths, ids, left, right, table_scores, conv_weight, cotangent)

    latent, small = pl.pallas_call(
        mix_kernel,
        out_shape=(
            jax.ShapeDtypeStruct((rows, half, width), F32),
            jax.ShapeDtypeStruct((8, width), F32),
        ),
        in_specs=[sm, sm] + [vm] * 6,
        out_specs=(vm, vm),
        scratch_shapes=[
            pltpu.VMEM((12 * count, 128), F32),
            pltpu.VMEM((d_rows, width), F32),
            pltpu.VMEM((vocab, 2 * chunks * 128), BF16),
            pltpu.VMEM((chunks * 128, width), F32),
            pltpu.VMEM((chunks * 128, width), BF16),
            pltpu.VMEM((chunks * 128, width), BF16),
            pltpu.VMEM((6, padded, 128), F32),
            pltpu.VMEM((8, 2 * chunks * 128), F32),
        ],
        compiler_params=VMEM,
        name="mix",
    )(start, lengths, weights, id_chunks, embedding, conv_weight, bias, cotangent)

    bits = seq.bit_length() - 1
    groups = [("seq", low, min(2, bits - low)) for low in range(0, bits, 2)]
    stages = [("dp", 0, lax.axis_size("dp").bit_length() - 1)] + groups[:-1]
    total = grad_table
    for stage in stages:
        total = scatter_sum(total, *stage)
    size = total.shape[0]
    both = exchange_sum(jnp.concatenate([total, small], axis=0), *groups[-1])
    total, small = both[:size], both[size:]
    for stage in reversed(stages):
        total, small = gather_back(total, small, *stage)

    grad_e, grad_w, grad_b, grad_s = pl.pallas_call(
        final_kernel,
        out_shape=(
            jax.ShapeDtypeStruct((vocab, width), F32),
            jax.ShapeDtypeStruct((TAPS, width), F32),
            jax.ShapeDtypeStruct((1, width), F32),
            jax.ShapeDtypeStruct((1, width), F32),
        ),
        in_specs=[vm] * 6,
        out_specs=(vm,) * 4,
        name="final",
    )(total, small, embedding, conv_weight, bias, scorer)
    return latent, grad_e, grad_w, grad_b.reshape(width), grad_s.reshape(width)


def solution(mesh):
    placed = (P("dp", "seq"), P("dp"), P(), P(), P(), P(), P("dp", "seq", None))
    return jax.shard_map(
        per_device,
        mesh=mesh,
        in_specs=placed,
        out_specs=(P("dp", "seq", None), P(), P(), P(), P()),
        check_vma=False,
    )
```

```python
import functools

import jax
import jax.numpy as jnp
from jax import lax
from jax.experimental import pallas as pl
from jax.experimental.pallas import tpu as pltpu
from jax.sharding import PartitionSpec as P

F32, BF16, I32 = jnp.float32, jnp.bfloat16, jnp.int32
HIGH = lax.Precision.HIGHEST
ROWS = 16
TAPS = 4
TABLE_BATCH, MIX_BATCH, LATENT_BATCH = 4, 2, 4
RING = 10
RELS = (-2, -1, 0, 1, 2, 3)
NT = (((1,), (1,)), ((), ()))
TN = (((0,), (0,)), ((), ()))


def lanes(shape):
    return lax.broadcasted_iota(I32, shape, 1)


def line(ref):
    return ref[...].reshape(1, ref.shape[0])


def pick(x, index):
    return jnp.take_along_axis(x, index, axis=1, mode="promise_in_bounds")


def split(x):
    high = x.astype(BF16)
    return high, (x - high.astype(F32)).astype(BF16)


def dot(a, b, dims=(((1,), (0,)), ((), ()))):
    return lax.dot_general(a, b, dims, preferred_element_type=F32)


def ahead(x):
    lane = lanes(x.shape) % 8
    below = pltpu.roll(x, x.shape[0] - 1, 0)
    return jnp.where(lane == 7, pltpu.roll(below, 7, 1), pltpu.roll(x, 127, 1))


def behind(x):
    lane = lanes(x.shape) % 8
    above = pltpu.roll(x, 1, 0)
    return jnp.where(lane == 0, pltpu.roll(above, 121, 1), pltpu.roll(x, 1, 1))


def geometry(shape, start, len_ref):
    lane = lanes(shape)
    window = lax.broadcasted_iota(I32, shape, 0) - 8
    even = start + 16 * window + 2 * (lane % 8)
    length = jnp.zeros(shape, I32)
    for r in range(ROWS):
        length = jnp.where(lane // 8 == r, len_ref[r], length)
    return even, length


def alive(pos, length):
    return (pos >= 0) & (pos < length)


def members(even, parity):
    offset = (even + parity) % 3
    left = (even // 2) % 2 == 0
    out = [[((parity,), None)], [((0, 1), None)], [], []]
    for o in range(3):
        out[2].append((tuple(parity - o + i for i in range(3)), offset == o))
    out[3] = [((0, 1, 2, 3), left), ((-2, -1, 0, 1), ~left)]
    return out


def to_chunks(xe, xo, g):
    lane = lanes(xe.shape)
    place = (lane // 8 + 12) % 16
    index = g * 64 + (lane % 8) * 8 + place // 2
    y = jnp.where(place % 2 == 0, pick(xe, index), pick(xo, index))
    return jnp.where(lane < 32, pltpu.roll(y, 1, 0), y)[8:]


def prep_kernel(e_ref, w_ref, b_ref, s_ref, ct_hbm, t_ref, high_ref, low_ref, ct_ref, sem):
    copy = pltpu.make_async_copy(ct_hbm, ct_ref, sem)
    copy.start()
    scaled = w_ref[...] * line(s_ref)
    wide = jnp.concatenate([scaled, jnp.zeros_like(scaled)], axis=0)
    t = lax.dot_general(wide, e_ref[...], NT, precision=HIGH, preferred_element_type=F32)
    b0 = jnp.sum(line(b_ref) * line(s_ref), axis=1, keepdims=True)
    row = lax.broadcasted_iota(I32, t.shape, 0)
    t_ref[...] = jnp.where(row == TAPS, b0, t)
    high_ref[...], low_ref[...] = split(e_ref[...])
    copy.wait()


def regroup(ids_ref, ids_scr, first, windows):
    for a in range(0, len(windows), 8):
        some = windows[a : a + 8]
        shape = (8, 128)
        lane = lanes(shape)
        window = lax.broadcasted_iota(I32, shape, 0) + some[0]
        column = 16 * some[0] // 128 * 128
        width = min(128, ids_ref.shape[1] - column)
        index = jnp.clip(16 * window + lane % 16 - column, 0, width - 1)
        for g in range(2):
            out = jnp.zeros(shape, I32)
            for r in range(8):
                row = ids_ref[g * 8 + r : g * 8 + r + 1, column : column + width]
                if width < 128:
                    row = jnp.concatenate([row, jnp.zeros((1, 128 - width), I32)], axis=1)
                found = pick(jnp.broadcast_to(row, shape), index)
                out = jnp.where(lane // 16 == r, found, out)
            at = first + a
            ids_scr[at : at + len(some), g * 128 : g * 128 + 128] = out[: len(some)]


def weigh(start, len_ref, ids_scr, t_ref):
    shape = (ids_scr.shape[0], 128)
    lane = lanes(shape)
    even, length = geometry(shape, start, len_ref)
    live = [alive(even, length), alive(even + 1, length)]
    ids, terms = [], []
    for e in range(2):
        index = ((lane // 8) % 8) * 16 + 2 * (lane % 8) + e
        found = jnp.where(
            lane < 64, pick(ids_scr[:, :128], index), pick(ids_scr[:, 128:], index)
        )
        taps = []
        for k in range(TAPS):
            value = jnp.zeros(shape, F32)
            for half in range(t_ref.shape[1] // 128):
                row = jnp.broadcast_to(t_ref[k : k + 1, half * 128 : half * 128 + 128], shape)
                here = (found >= half * 128) & (found < half * 128 + 128)
                value = jnp.where(here, pick(row, found & 127), value)
            taps.append(jnp.where(live[e], value, 0.0))
        terms.append(taps)
        ids.append(jnp.where(live[e], found, -1))
    b0 = t_ref[TAPS : TAPS + 1, :128]
    (ae, ao) = terms
    ce = jnp.where(live[0], b0 + behind(ae[0] + ao[1]) + ae[2] + ao[3], 0.0)
    co = jnp.where(live[1], b0 + behind(ao[0]) + ae[1] + ao[2] + ahead(ae[3]), 0.0)
    at = {-2: behind(ce), -1: behind(co), 0: ce, 1: co, 2: ahead(ce), 3: ahead(co)}
    weights = []
    for e in range(2):
        scores = []
        for b, cases in enumerate(members(even, e)):
            total = None
            for rels, where in cases:
                part = sum(at[r] for r in rels)
                total = part if total is None else jnp.where(where, part, total)
            scores.append(total * (1.0 / (b + 1)))
        top = functools.reduce(jnp.maximum, scores)
        parts = [jnp.exp(s - top) for s in scores]
        norm = sum(parts)
        weights.append([p / norm for p in parts])
    return ids, weights, even, length


def spread(values, even):
    out = {r: 0.0 for r in RELS}
    for e in range(2):
        for b, cases in enumerate(members(even, e)):
            share = values[e][b] * (1.0 / (b + 1))
            for rels, where in cases:
                part = share if where is None else jnp.where(where, share, 0.0)
                for r in rels:
                    out[r] = out[r] + part
    return out


def diagonals():
    shape = (8, 128)
    row, lane = lax.broadcasted_iota(I32, shape, 0), lanes(shape)
    same = row == (lane % 64) // 8
    return [same & (lane % 8 == u) for u in range(8)]


def banded(bands_ref, g, w, count, diagonal):
    lane = lanes((8, 128))
    tiles = [jnp.zeros((8, 128), F32) for _ in range(20)]
    for i, r in enumerate(RELS):
        line = bands_ref[pl.ds((g * len(RELS) + i) * count + w, 1), :]
        high = line.astype(BF16).astype(F32)
        line = jnp.where(lanes((1, 128)) < 64, high, line - high)
        line = jnp.broadcast_to(line, (8, 128))
        for u in range(8):
            at = 2 * u + 2 + r
            tiles[at] = jnp.where(diagonal[u], line, tiles[at])
    return jnp.concatenate(tiles, axis=0).astype(BF16)


def store_bands(bands, bands_ref, count):
    lane = lanes(bands[0].shape)
    for i, r in enumerate(RELS):
        turned = pltpu.roll(bands[r], 64, 1)
        for g in range(2):
            both = jnp.where((lane < 64) == (g == 0), bands[r], turned)
            at = (g * len(RELS) + i) * count
            bands_ref[at : at + count, :] = both[8 : 8 + count]


def one_hot_t(ids, vocab):
    return jnp.where(
        lax.broadcasted_iota(I32, (vocab, 128), 0) == ids, 1.0, 0.0
    ).astype(BF16)


def weave(*parts):
    order = [((i + 0.5) / len(p), k, step) for k, p in enumerate(parts) for i, step in enumerate(p)]
    for _, _, step in sorted(order, key=lambda item: item[:2]):
        step()


def run_stages(stages, lags):
    for slot in range(len(stages[0]) + max(lags)):
        now = [(items, slot - lag) for items, lag in zip(stages, lags)]
        weave(*[items[t] for items, t in now if 0 <= t < len(items)])


def batches(count, size):
    return [(g, list(range(b, b + size))) for g in range(2) for b in range(0, count, size)]


def window_grads(ct_ref, hl, d_ref, w, n):
    wide = jnp.concatenate([hl, hl], axis=1)
    at = 128 * w + 48
    high, low = split(ct_ref[:, 8 * w : 8 * w + 8, n : n + 256].reshape(64, 256))
    grads = dot(wide, jnp.concatenate([high, high, low, low], axis=0))
    d_ref[at : at + 32, n : n + 256] += grads[:32]
    d_ref[at + 32 : at + 160, n : n + 256] = grads[32:]


def table_kernel(
    start_ref, len_ref, ids_ref, left_ref, right_ref, t_ref, w_ref, ct_ref,
    grad_ref, weights_ref, chunks_ref, hl0, hl1,
    ids_scr, bands_ref, *scratch,
):
    d_refs, oh_refs, high_refs, low_refs = (scratch[2 * i : 2 * i + 2] for i in range(4))
    hl_refs = (hl0, hl1)
    count = ids_ref.shape[1] // 16
    chunks = count + 1
    vocab = t_ref.shape[1]
    start = start_ref[0]
    ids_scr[...] = jnp.zeros_like(ids_scr)
    regroup(left_ref, ids_scr, 7, [count - 1])
    regroup(ids_ref, ids_scr, 8, list(range(count)))
    regroup(right_ref, ids_scr, 8 + count, [0])
    ids, weights, even, length = weigh(start, len_ref, ids_scr, t_ref)
    for e in range(2):
        for b in range(4):
            weights_ref[e * 4 + b] = weights[e][b]
    bands = spread(weights, even)
    for r in RELS:
        bands[r] = jnp.where(alive(even + r, length), 0.5 * bands[r], 0.0)
    store_bands(bands, bands_ref, count)
    per = chunks_ref.shape[0] // 2
    for g in range(2):
        chunks_ref[g * per : g * per + per, :] = to_chunks(ids[0], ids[1], g)
    width = w_ref.shape[1]
    for d_ref in d_refs:
        d_ref[:80, :] = jnp.zeros((80, width), F32)
        d_ref[-64:, :] = jnp.zeros((64, width), F32)

    diagonal = diagonals()

    def grad_steps(g, w):
        made = []

        def step(n):
            if not made:
                made.append(banded(bands_ref, g, w, count, diagonal))
                hl_refs[g][w * 160 : w * 160 + 160, :] = made[0]
            window_grads(ct_ref.at[g * 8 : g * 8 + 8], made[0], d_refs[g], w, n)

        return [functools.partial(step, n) for n in range(0, width, 256)]

    def part_steps(g, c):
        d_ref, oh_ref, high_ref, low_ref = (x[g] for x in (d_refs, oh_refs, high_refs, low_refs))
        to = c * 128
        size = 128 if c < count else 64

        def mark():
            ids = chunks_ref[g * per + c : g * per + c + 1, :]
            oh_ref[:, to : to + 128] = one_hot_t(ids, vocab)
            if size < 128:
                zero = jnp.zeros((128 - size, width), BF16)
                high_ref[to + size : to + 128, :] = zero
                low_ref[to + size : to + 128, :] = zero

        def step(n):
            cols = slice(n, n + 128)
            taps = [jnp.broadcast_to(w_ref[k : k + 1, cols], (64, 128)) for k in range(TAPS)]
            for i in range(0, size, 64):
                near = d_ref[to + 24 + i : to + 112 + i, cols]
                total = sum(taps[3 - k] * near[8 * k : 8 * k + 64] for k in range(TAPS))
                high, low = split(total)
                high_ref[to + i : to + i + 64, cols] = high
                low_ref[to + i : to + i + 64, cols] = low

        return [mark] + [functools.partial(step, n) for n in range(0, width, 128)]

    def sum_steps(g, cs):
        at = slice(cs[0] * 128, cs[-1] * 128 + 128)

        def step(n):
            cols = slice(n, n + 256)
            oh = oh_refs[g][:, at]
            total = dot(oh, high_refs[g][at, cols]) + dot(oh, low_refs[g][at, cols])
            if g == 0 and cs[0] == 0:
                grad_ref[:, cols] = total
            else:
                grad_ref[:, cols] += total

        return [functools.partial(step, n) for n in range(0, width, 256)]

    stages = [[], [], []]
    for g, ws in batches(count, min(TABLE_BATCH, count)):
        cs = ws + [count] * (ws[-1] == count - 1)
        stages[0].append(sum((grad_steps(g, w) for w in ws), []))
        stages[1].append(sum((part_steps(g, c) for c in cs), []))
        stages[2].append(sum_steps(g, cs))
    run_stages(stages, (0, 1, 2))


def near_kernel(
    start_ref, len_ref, weights_ref, chunks_ref, e_high, e_low, w_ref, b_ref, s_ref, hl0, hl1, ct_hbm,
    small_ref, high0, low0, high1, low1,
    near_ref, q_ref, sums_ref, oh0, oh1, d0, d1, x_ref, ct_ref, sem,
):
    copy = pltpu.make_async_copy(ct_hbm, ct_ref, sem)
    copy.start()
    oh_refs, d_refs, hl_refs = (oh0, oh1), (d0, d1), (hl0, hl1)
    high_refs, low_refs = (high0, high1), (low0, low1)
    padded = weights_ref.shape[1]
    count = ct_ref.shape[1] // 8
    chunks = count + 1
    vocab, width = e_high.shape
    start = start_ref[0]
    per = chunks_ref.shape[0] // 2
    small_ref[...] = jnp.zeros_like(small_ref)
    near_ref[...] = jnp.zeros_like(near_ref)
    sums_ref[...] = jnp.zeros_like(sums_ref)
    diagonal = diagonals()
    for d_ref in d_refs:
        d_ref[48:80, :] = jnp.zeros((32, width), F32)
    bias = line(b_ref)
    turned = chunks_ref[...].astype(F32).T

    def slot(g, c):
        return (g * chunks + c) % RING * 128

    def bytes_at(g, c, first, size, cols):
        here = min(128 - first, size)
        at = slot(g, c) + first
        x = x_ref[at : at + here, cols]
        if here == size:
            return x
        at = slot(g, c + 1)
        return jnp.concatenate([x, x_ref[at : at + size - here, cols]], axis=0)

    def look_up_steps(g, cs):
        at = slice(cs[0] * 128, cs[-1] * 128 + 128)

        def mark(c):
            column = jnp.broadcast_to(turned[:, g * per + c : g * per + c + 1], (128, vocab))
            found = jnp.where(column == lanes((128, vocab)).astype(F32), 1.0, 0.0)
            oh_refs[g][c * 128 : c * 128 + 128, :] = found.astype(BF16)

        def step(n):
            cols = slice(n, n + 256)
            oh = oh_refs[g][at, :]
            x = dot(oh, e_high[:, cols]) + dot(oh, e_low[:, cols])
            for i, c in enumerate(cs):
                to = slot(g, c)
                x_ref[to : to + 128, cols] = x[i * 128 : i * 128 + 128]

        return [functools.partial(mark, c) for c in cs] + [
            functools.partial(step, n) for n in range(0, width, 256)
        ]

    def grad_steps(g, w):
        def step(n):
            hl = hl_refs[g][w * 160 : w * 160 + 160, :]
            window_grads(ct_ref.at[g * 8 : g * 8 + 8], hl, d_refs[g], w, n)

        return [functools.partial(step, n) for n in range(0, width, 256)]

    def conv_steps(g, c):
        at = c * 128
        size = 128 if c < count else 32
        step_size = min(size, 64)

        def step(n):
            cols = slice(n, n + 128)
            taps = [jnp.broadcast_to(w_ref[k : k + 1, cols], (step_size, 128)) for k in range(TAPS)]
            first = jnp.broadcast_to(bias[:, cols], (step_size, 128))
            sums = [sums_ref[8 * k : 8 * k + 8, cols] for k in range(TAPS + 1)]
            for i in range(at, at + size, step_size):
                d = d_refs[g][i + 48 : i + 48 + step_size, cols]
                x = bytes_at(g, c, i - at, step_size + 24, cols)
                total = first
                products = [d]
                for k in range(TAPS):
                    near = x[8 * k : 8 * k + step_size]
                    total = total + taps[k] * near
                    products.append(d * near)
                for k, p in enumerate(products):
                    sums[k] = sums[k] + p.reshape(step_size // 8, 8, 128).sum(0)
                high, low = split(total)
                high_refs[g][i : i + step_size, cols] = high
                low_refs[g][i : i + step_size, cols] = low
            for k in range(TAPS + 1):
                sums_ref[8 * k : 8 * k + 8, cols] = sums[k]

        return [functools.partial(step, n) for n in range(0, width, 128)]

    def meet_steps(g, w):
        at = slice(w * 128, w * 128 + 160)

        def meet():
            ct = ct_ref[g * 8 : g * 8 + 8, 8 * w : 8 * w + 8, :].reshape(64, width)
            ct = jnp.concatenate(split(ct), axis=0)
            product = dot(high_refs[g][at, :], ct, NT) + dot(low_refs[g][at, :], ct, NT)
            for i, r in enumerate(RELS):
                total = jnp.zeros((8, 128), F32)
                for u in range(8):
                    row = 8 * (2 * u + 2 + r)
                    total = total + jnp.where(diagonal[u], product[row : row + 8], 0.0)
                found = jnp.sum(total, axis=0, keepdims=True)
                found = found + pltpu.roll(found, 64, 1)
                near_ref[i, 8 + w : 9 + w, g * 64 : g * 64 + 64] = found[:, g * 64 : g * 64 + 64]

        return [meet]

    stages = [[], [], [], []]
    for g, ws in batches(count, MIX_BATCH):
        cs = ws + [count] * (ws[-1] == count - 1)
        stages[0].append(look_up_steps(g, cs))
        stages[1].append(sum((grad_steps(g, w) for w in ws), []))
        stages[2].append(sum((conv_steps(g, c) for c in cs), []))
        stages[3].append(sum((meet_steps(g, w) for w in ws), []))
    stages[1][0].insert(0, copy.wait)
    run_stages(stages, (0, 1, 2, 4))

    for k in range(TAPS + 1):
        total = jnp.sum(sums_ref[8 * k : 8 * k + 8, :], axis=0, keepdims=True)
        to = (k + TAPS) % (TAPS + 1)
        small_ref[to : to + 1, :] = total
    even, length = geometry((padded, 128), start, len_ref)
    weights = [[weights_ref[e * 4 + b] for b in range(4)] for e in range(2)]
    near = {}
    for i, r in enumerate(RELS):
        near[r] = jnp.where(alive(even + r, length), 0.5 * near_ref[i], 0.0)
    d_scores = []
    for e in range(2):
        d_weights = []
        for b, cases in enumerate(members(even, e)):
            total = None
            for rels, where in cases:
                part = sum(near[r] for r in rels)
                total = part if total is None else jnp.where(where, part, total)
            d_weights.append(total * (1.0 / (b + 1)))
        mean = sum(weights[e][b] * d_weights[b] for b in range(4))
        d_scores.append([weights[e][b] * (d_weights[b] - mean) for b in range(4)])
    own = lax.broadcasted_iota(I32, (padded, 128), 0) - 8
    own = (own >= 0) & (own < count)
    q = spread(d_scores, even)
    for r in RELS:
        q[r] = jnp.where(own & alive(even + r, length), q[r], 0.0)
    qe = q[0] + behind(q[2]) + ahead(q[-2])
    qo = q[1] + behind(q[3]) + ahead(q[-1])
    q_sum = jnp.sum(jnp.sum(qe + qo, axis=0, keepdims=True), axis=1, keepdims=True)
    shifted = [
        (ahead(qe), ahead(qo)),
        (qo, ahead(qe)),
        (qe, qo),
        (behind(qo), qe),
    ]
    q_ref[...] = jnp.zeros_like(q_ref)
    for g in range(2):
        for k in range(TAPS):
            flat = to_chunks(*shifted[k], g)
            for c in range(chunks):
                at = (g * chunks + c) * 128
                q_ref[k : k + 1, at : at + 128] = flat[c : c + 1]
    q1, rest = q_ref[...].astype(BF16), q_ref[...]
    rest = rest - q1.astype(F32)
    q2 = rest.astype(BF16)
    q3 = (rest - q2.astype(F32)).astype(BF16)
    q = jnp.concatenate([q1, q2, q3], axis=0)
    xs = chunks * 128
    hist = dot(q[:, :xs], oh_refs[0][...]) + dot(q[:, xs:], oh_refs[1][...])
    hist = hist[:8] + hist[8:16] + hist[16:]
    h_high, h_low = split(hist)
    looked = dot(jnp.concatenate([h_high, h_low], axis=0), e_high[...])
    looked = looked[:8] + looked[8:] + dot(h_high, e_low[...])
    for k in range(TAPS):
        small_ref[k : k + 1, :] += looked[k : k + 1] * line(s_ref)
        at = k * vocab
        small_ref[6 + at // width : 7 + at // width, at % width : at % width + vocab] = hist[k : k + 1]
    small_ref[TAPS : TAPS + 1, :] += q_sum * line(s_ref)
    small_ref[5:6, :] = q_sum * bias + jnp.sum(
        looked[:TAPS] * w_ref[...], axis=0, keepdims=True
    )


def latent_kernel(high0, low0, high1, low1, hl0, hl1, out_ref, latent_ref, sems):
    half, width = latent_ref.shape[1:]
    size = min(LATENT_BATCH, half // 8)
    copies = []
    for g, (high_ref, low_ref, hl_ref) in enumerate(((high0, low0, hl0), (high1, low1, hl1))):
        for w in range(half // 8):
            band = hl_ref[w * 160 : w * 160 + 160, :].astype(F32).T.astype(BF16)
            at = slice(w * 128, w * 128 + 160)
            for n in range(0, width, 256):
                both = dot(band, high_ref[at, n : n + 256])
                rest = dot(band[:64], low_ref[at, n : n + 256])
                out = both[:64] + both[64:] + rest
                latent_ref[g * 8 : g * 8 + 8, 8 * w : 8 * w + 8, n : n + 256] = out.reshape(8, 8, 256)
            if (w + 1) % size == 0:
                done = (pl.ds(g * 8, 8), pl.ds(8 * (w + 1 - size), 8 * size))
                copy = pltpu.make_async_copy(
                    latent_ref.at[done], out_ref.at[done], sems.at[len(copies)]
                )
                copy.start()
                copies.append(copy)
    for copy in copies:
        copy.wait()


def final_kernel(sum_ref, small_ref, w_ref, s_ref, ge_ref, gw_ref, gb_ref, gs_ref):
    vocab, width = sum_ref.shape
    hist = []
    for k in range(TAPS):
        at = k * vocab
        hist.append(small_ref[6 + at // width : 7 + at // width, at % width : at % width + vocab])
    hist = jnp.concatenate(hist + [jnp.zeros((8 - TAPS, vocab), F32)], axis=0).T
    scaled = w_ref[...] * line(s_ref)
    columns = [jnp.broadcast_to(hist[:, k : k + 1], (vocab, 128)) for k in range(TAPS)]
    for n in range(0, width, 128):
        cols = slice(n, n + 128)
        ge_ref[:, cols] = sum_ref[:, cols] + sum(
            columns[k] * scaled[k : k + 1, cols] for k in range(TAPS)
        )
    gw_ref[...] = small_ref[0:TAPS, :]
    gb_ref[...] = small_ref[TAPS : TAPS + 1, :].reshape(width)
    gs_ref[...] = small_ref[TAPS + 1 : TAPS + 2, :].reshape(width)


def in_vmem(*arrays):
    return [pltpu.with_memory_space_constraint(a, pltpu.VMEM) for a in arrays]


def in_hbm(*arrays):
    return [pltpu.with_memory_space_constraint(a, pltpu.HBM) for a in arrays]


def limit(megabytes):
    return pltpu.CompilerParams(vmem_limit_bytes=megabytes * 1024 * 1024)


def cost(flops, moved):
    return pl.CostEstimate(flops=flops, bytes_accessed=moved, transcendentals=0)


def vm(n):
    return [pl.BlockSpec(memory_space=pltpu.VMEM)] * n


def sm(n):
    return [pl.BlockSpec(memory_space=pltpu.SMEM)] * n


def sizes(span):
    count = span // 16
    chunks = count + 1
    per = -(-chunks // 8) * 8
    return count, chunks, per, (span + 16) * 8


def prep_call(*params):
    vocab, width = params[0].shape
    return pl.pallas_call(
        prep_kernel,
        out_shape=(
            pltpu.VMEM((8, vocab), F32),
            pltpu.VMEM((vocab, width), BF16),
            pltpu.VMEM((vocab, width), BF16),
            pltpu.VMEM(params[-1].shape, F32),
        ),
        in_specs=vm(4) + [pl.BlockSpec(memory_space=pl.ANY)],
        out_specs=vm(4),
        scratch_shapes=[pltpu.SemaphoreType.DMA(())],
        compiler_params=limit(4),
        cost_estimate=cost(10**8, 10**6),
        name="prep",
    )(*in_hbm(*params))


def table_call(start, lengths, ids, left, right, table_scores, conv_weight, cotangent):
    rows, half, width = cotangent.shape
    count, chunks, per, d_rows = sizes(2 * half)
    vocab = table_scores.shape[1]
    return pl.pallas_call(
        table_kernel,
        out_shape=(
            pltpu.VMEM((vocab, width), F32),
            pltpu.VMEM((8, 8 + per, 128), F32),
            pltpu.VMEM((2 * per, 128), I32),
            pltpu.VMEM((160 * count, 128), BF16),
            pltpu.VMEM((160 * count, 128), BF16),
        ),
        in_specs=sm(2) + vm(6),
        out_specs=vm(5),
        scratch_shapes=[
            pltpu.VMEM((8 + per, 256), I32),
            pltpu.VMEM((12 * count, 128), F32),
        ]
        + [pltpu.VMEM((d_rows, width), F32)] * 2
        + [pltpu.VMEM((vocab, chunks * 128), BF16)] * 2
        + [pltpu.VMEM((chunks * 128, width), BF16)] * 4,
        compiler_params=limit(34),
        cost_estimate=cost(8 * 10**9, 2 * 10**7),
        name="table_grad",
    )(
        start, lengths, *in_hbm(ids), *in_vmem(left, right, table_scores),
        *in_hbm(conv_weight), *in_vmem(cotangent),
    )


def near_call(start, lengths, weights, id_chunks, e_high, e_low, conv_weight, bias, scorer, hl0, hl1, ct):
    rows, half, width = ct.shape
    count, chunks, per, d_rows = sizes(2 * half)
    vocab = e_high.shape[0]
    return pl.pallas_call(
        near_kernel,
        out_shape=[pltpu.VMEM((8, width), F32)] + [pltpu.VMEM((chunks * 128, width), BF16)] * 4,
        in_specs=sm(2) + vm(9) + [pl.BlockSpec(memory_space=pl.ANY)],
        out_specs=vm(5),
        scratch_shapes=[
            pltpu.VMEM((6, 8 + per, 128), F32),
            pltpu.VMEM((8, 2 * chunks * 128), F32),
            pltpu.VMEM((8 * (TAPS + 1), width), F32),
        ]
        + [pltpu.VMEM((chunks * 128, vocab), BF16)] * 2
        + [pltpu.VMEM((d_rows, width), F32)] * 2
        + [
            pltpu.VMEM((RING * 128, width), F32),
            pltpu.VMEM(ct.shape, F32),
            pltpu.SemaphoreType.DMA(()),
        ],
        compiler_params=limit(30),
        cost_estimate=cost(16 * 10**9, 4 * 10**7),
        name="near",
    )(
        start, lengths, *in_vmem(weights, id_chunks, e_high, e_low),
        *in_hbm(conv_weight, bias, scorer), *in_vmem(hl0, hl1), *in_hbm(ct),
    )


def latent_call(kept, shape):
    rows, half, width = shape
    count = half // 8
    return pl.pallas_call(
        latent_kernel,
        out_shape=jax.ShapeDtypeStruct(shape, F32),
        in_specs=vm(6),
        out_specs=pl.BlockSpec(memory_space=pl.ANY),
        scratch_shapes=[
            pltpu.VMEM(shape, F32),
            pltpu.SemaphoreType.DMA((2 * (count // min(LATENT_BATCH, count)),)),
        ],
        compiler_params=limit(8),
        cost_estimate=cost(4 * 10**9, 10**7),
        name="latent",
    )(*in_vmem(*kept))


def partners(axis, mask):
    return [(i, i ^ mask) for i in range(lax.axis_size(axis))]


def part(v, index, size):
    return lax.dynamic_slice_in_dim(v, index * size, size, 0)


def scatter_sum(v, axis, low, bits):
    group = 1 << bits
    size = v.shape[0] // group
    me = (lax.axis_index(axis) >> low) & (group - 1)
    total = part(v, me, size)
    for m in range(1, group):
        total = total + lax.ppermute(part(v, me ^ m, size), axis, partners(axis, m << low))
    return total


def exchange_sum(v, axis, low, bits):
    return v + sum(
        lax.ppermute(v, axis, partners(axis, m << low)) for m in range(1, 1 << bits)
    )


def gather_back(v, small, axis, low, bits):
    group = 1 << bits
    size = v.shape[0]
    me = (lax.axis_index(axis) >> low) & (group - 1)
    both = jnp.concatenate([v, small], axis=0)
    out = jnp.zeros((group * size,) + v.shape[1:], v.dtype)
    out = lax.dynamic_update_slice_in_dim(out, v, me * size, 0)
    for m in range(1, group):
        got = lax.ppermute(both, axis, partners(axis, m << low))
        out = lax.dynamic_update_slice_in_dim(out, got[:size], (me ^ m) * size, 0)
        small = small + got[size:]
    return out, small


def per_device(byte_ids, lengths, embedding, conv_weight, conv_bias, score_weight, cotangent):
    rows, span = byte_ids.shape
    vocab, width = embedding.shape
    count = span // 16
    seq = lax.axis_size("seq")
    start = (lax.axis_index("seq") * span).reshape(1)

    up = [(i, i + 1) for i in range(seq - 1)]
    left = lax.ppermute(byte_ids, "seq", up)
    right = lax.ppermute(byte_ids, "seq", [(j, i) for i, j in up])
    table_scores, e_high, e_low, ct = prep_call(
        embedding, conv_weight, conv_bias, score_weight, cotangent
    )
    grad_table, weights, id_chunks, hl0, hl1 = table_call(
        start, lengths, byte_ids, left, right, table_scores, conv_weight, ct
    )
    small, *kept = near_call(
        start, lengths, weights, id_chunks, e_high, e_low, conv_weight, conv_bias, score_weight,
        hl0, hl1, cotangent,
    )
    latent = latent_call(kept + [hl0, hl1], cotangent.shape)

    bits = seq.bit_length() - 1
    groups = [("seq", low, min(2, bits - low)) for low in range(0, bits, 2)]
    stages = [("dp", 0, lax.axis_size("dp").bit_length() - 1)] + groups[:-1]
    total = grad_table
    for stage in stages:
        total = scatter_sum(total, *stage)
    size = total.shape[0]
    both = exchange_sum(jnp.concatenate([total, small], axis=0), *groups[-1])
    both, latent = lax.optimization_barrier((both, latent))
    total, small = both[:size], both[size:]
    for stage in reversed(stages):
        total, small = gather_back(total, small, *stage)

    grad_e, grad_w, grad_b, grad_s = pl.pallas_call(
        final_kernel,
        out_shape=(
            jax.ShapeDtypeStruct((vocab, width), F32),
            jax.ShapeDtypeStruct((TAPS, width), F32),
            jax.ShapeDtypeStruct((width,), F32),
            jax.ShapeDtypeStruct((width,), F32),
        ),
        in_specs=vm(4),
        out_specs=vm(4),
        compiler_params=limit(4),
        name="final",
    )(*in_vmem(total, small), *in_hbm(conv_weight, score_weight))
    return latent, grad_e, grad_w, grad_b, grad_s


def solution(mesh):
    placed = (P("dp", "seq"), P("dp"), P(), P(), P(), P(), P("dp", "seq", None))
    return jax.shard_map(
        per_device,
        mesh=mesh,
        in_specs=placed,
        out_specs=(P("dp", "seq", None), P(), P(), P(), P()),
        check_vma=False,
    )
```

```python
import functools

import jax
import jax.numpy as jnp
from jax import lax
from jax.experimental import pallas as pl
from jax.experimental.pallas import tpu as pltpu
from jax.sharding import PartitionSpec as P

F32, BF16, I32 = jnp.float32, jnp.bfloat16, jnp.int32
HIGH = lax.Precision.HIGHEST
ROWS = 16
TAPS = 4
TABLE_BATCH, MIX_BATCH, LATENT_BATCH = 4, 4, 4
RING = 18
RELS = (-2, -1, 0, 1, 2, 3)
NT = (((1,), (1,)), ((), ()))
TN = (((0,), (0,)), ((), ()))


def lanes(shape):
    return lax.broadcasted_iota(I32, shape, 1)


def line(ref):
    return ref[...].reshape(1, ref.shape[0])


def pick(x, index):
    return jnp.take_along_axis(x, index, axis=1, mode="promise_in_bounds")


def split(x):
    high = x.astype(BF16)
    return high, (x - high.astype(F32)).astype(BF16)


def dot(a, b, dims=(((1,), (0,)), ((), ()))):
    return lax.dot_general(a, b, dims, preferred_element_type=F32)


def ahead(x):
    lane = lanes(x.shape) % 8
    below = pltpu.roll(x, x.shape[0] - 1, 0)
    return jnp.where(lane == 7, pltpu.roll(below, 7, 1), pltpu.roll(x, 127, 1))


def behind(x):
    lane = lanes(x.shape) % 8
    above = pltpu.roll(x, 1, 0)
    return jnp.where(lane == 0, pltpu.roll(above, 121, 1), pltpu.roll(x, 1, 1))


def geometry(shape, start, len_ref):
    lane = lanes(shape)
    window = lax.broadcasted_iota(I32, shape, 0) - 8
    even = start + 16 * window + 2 * (lane % 8)
    length = jnp.zeros(shape, I32)
    for r in range(ROWS):
        length = jnp.where(lane // 8 == r, len_ref[r], length)
    return even, length


def alive(pos, length):
    return (pos >= 0) & (pos < length)


def members(even, parity):
    offset = (even + parity) % 3
    left = (even // 2) % 2 == 0
    out = [[((parity,), None)], [((0, 1), None)], [], []]
    for o in range(3):
        out[2].append((tuple(parity - o + i for i in range(3)), offset == o))
    out[3] = [((0, 1, 2, 3), left), ((-2, -1, 0, 1), ~left)]
    return out


def to_chunks(xe, xo, g):
    lane = lanes(xe.shape)
    place = (lane // 8 + 12) % 16
    index = g * 64 + (lane % 8) * 8 + place // 2
    y = jnp.where(place % 2 == 0, pick(xe, index), pick(xo, index))
    return jnp.where(lane < 32, pltpu.roll(y, 1, 0), y)[8:]


def prep_kernel(e_ref, w_ref, b_ref, s_ref, ct_hbm, t_ref, high_ref, low_ref, ct_ref, sem):
    copy = pltpu.make_async_copy(ct_hbm, ct_ref, sem)
    copy.start()
    scaled = w_ref[...] * line(s_ref)
    wide = jnp.concatenate([scaled, jnp.zeros_like(scaled)], axis=0)
    t = lax.dot_general(wide, e_ref[...], NT, precision=HIGH, preferred_element_type=F32)
    b0 = jnp.sum(line(b_ref) * line(s_ref), axis=1, keepdims=True)
    row = lax.broadcasted_iota(I32, t.shape, 0)
    t_ref[...] = jnp.where(row == TAPS, b0, t)
    high_ref[...], low_ref[...] = split(e_ref[...])
    copy.wait()


def regroup(ids_ref, ids_scr, first, windows):
    for a in range(0, len(windows), 8):
        some = windows[a : a + 8]
        shape = (8, 128)
        lane = lanes(shape)
        window = lax.broadcasted_iota(I32, shape, 0) + some[0]
        column = 16 * some[0] // 128 * 128
        width = min(128, ids_ref.shape[1] - column)
        index = jnp.clip(16 * window + lane % 16 - column, 0, width - 1)
        for g in range(2):
            out = jnp.zeros(shape, I32)
            for r in range(8):
                row = ids_ref[g * 8 + r : g * 8 + r + 1, column : column + width]
                if width < 128:
                    row = jnp.concatenate([row, jnp.zeros((1, 128 - width), I32)], axis=1)
                found = pick(jnp.broadcast_to(row, shape), index)
                out = jnp.where(lane // 16 == r, found, out)
            at = first + a
            ids_scr[at : at + len(some), g * 128 : g * 128 + 128] = out[: len(some)]


def weigh(start, len_ref, ids_scr, t_ref):
    shape = (ids_scr.shape[0], 128)
    lane = lanes(shape)
    even, length = geometry(shape, start, len_ref)
    live = [alive(even, length), alive(even + 1, length)]
    ids, terms = [], []
    for e in range(2):
        index = ((lane // 8) % 8) * 16 + 2 * (lane % 8) + e
        found = jnp.where(
            lane < 64, pick(ids_scr[:, :128], index), pick(ids_scr[:, 128:], index)
        )
        taps = []
        for k in range(TAPS):
            value = jnp.zeros(shape, F32)
            for half in range(t_ref.shape[1] // 128):
                row = jnp.broadcast_to(t_ref[k : k + 1, half * 128 : half * 128 + 128], shape)
                here = (found >= half * 128) & (found < half * 128 + 128)
                value = jnp.where(here, pick(row, found & 127), value)
            taps.append(jnp.where(live[e], value, 0.0))
        terms.append(taps)
        ids.append(jnp.where(live[e], found, -1))
    b0 = t_ref[TAPS : TAPS + 1, :128]
    (ae, ao) = terms
    ce = jnp.where(live[0], b0 + behind(ae[0] + ao[1]) + ae[2] + ao[3], 0.0)
    co = jnp.where(live[1], b0 + behind(ao[0]) + ae[1] + ao[2] + ahead(ae[3]), 0.0)
    at = {-2: behind(ce), -1: behind(co), 0: ce, 1: co, 2: ahead(ce), 3: ahead(co)}
    weights = []
    for e in range(2):
        scores = []
        for b, cases in enumerate(members(even, e)):
            total = None
            for rels, where in cases:
                part = sum(at[r] for r in rels)
                total = part if total is None else jnp.where(where, part, total)
            scores.append(total * (1.0 / (b + 1)))
        top = functools.reduce(jnp.maximum, scores)
        parts = [jnp.exp(s - top) for s in scores]
        norm = sum(parts)
        weights.append([p / norm for p in parts])
    return ids, weights, even, length


def spread(values, even):
    out = {r: 0.0 for r in RELS}
    for e in range(2):
        for b, cases in enumerate(members(even, e)):
            share = values[e][b] * (1.0 / (b + 1))
            for rels, where in cases:
                part = share if where is None else jnp.where(where, share, 0.0)
                for r in rels:
                    out[r] = out[r] + part
    return out


def diagonals():
    shape = (8, 128)
    row, lane = lax.broadcasted_iota(I32, shape, 0), lanes(shape)
    same = row == (lane % 64) // 8
    return [same & (lane % 8 == u) for u in range(8)]


def banded(bands_ref, g, w, count, diagonal):
    lane = lanes((8, 128))
    tiles = [jnp.zeros((8, 128), F32) for _ in range(20)]
    for i, r in enumerate(RELS):
        line = bands_ref[pl.ds((g * len(RELS) + i) * count + w, 1), :]
        high = line.astype(BF16).astype(F32)
        line = jnp.where(lanes((1, 128)) < 64, high, line - high)
        line = jnp.broadcast_to(line, (8, 128))
        for u in range(8):
            at = 2 * u + 2 + r
            tiles[at] = jnp.where(diagonal[u], line, tiles[at])
    return jnp.concatenate(tiles, axis=0).astype(BF16)


def store_bands(bands, bands_ref, count):
    lane = lanes(bands[0].shape)
    for i, r in enumerate(RELS):
        turned = pltpu.roll(bands[r], 64, 1)
        for g in range(2):
            both = jnp.where((lane < 64) == (g == 0), bands[r], turned)
            at = (g * len(RELS) + i) * count
            bands_ref[at : at + count, :] = both[8 : 8 + count]


def one_hot_t(ids, vocab):
    return jnp.where(
        lax.broadcasted_iota(I32, (vocab, 128), 0) == ids, 1.0, 0.0
    ).astype(BF16)


def weave(*parts):
    order = [((i + 0.5) / len(p), k, step) for k, p in enumerate(parts) for i, step in enumerate(p)]
    for _, _, step in sorted(order, key=lambda item: item[:2]):
        step()


def run_stages(stages, lags):
    for slot in range(len(stages[0]) + max(lags)):
        now = [(items, slot - lag) for items, lag in zip(stages, lags)]
        weave(*[items[t] for items, t in now if 0 <= t < len(items)])


def batches(count, size):
    return [(g, list(range(b, b + size))) for g in range(2) for b in range(0, count, size)]


class Halves:
    def __init__(self, first, second):
        self.refs, self.size = (first, second), first.shape[0]

    def parts(self, lo, hi):
        for ref, base in zip(self.refs, (0, self.size)):
            a, b = max(lo, base), min(hi, base + self.size)
            if a < b:
                yield ref, a - base, b - base, a - lo, b - lo

    def load(self, lo, hi, cols):
        found = [ref[a:b, cols] for ref, a, b, _, _ in self.parts(lo, hi)]
        return found[0] if len(found) == 1 else jnp.concatenate(found, axis=0)

    def store(self, lo, value, cols):
        for ref, a, b, i, j in self.parts(lo, lo + value.shape[0]):
            ref[a:b, cols] = value[i:j]


def window_grads(ct_ref, both_ref, hl, d, w, n):
    wide = jnp.concatenate([hl, hl], axis=1)
    at = 128 * w + 48
    cols = slice(n, n + 256)
    high, low = split(ct_ref[:, 8 * w : 8 * w + 8, cols].reshape(64, 256))
    both_ref[128 * w : 128 * w + 64, cols] = high
    both_ref[128 * w + 64 : 128 * w + 128, cols] = low
    grads = dot(wide, jnp.concatenate([high, high, low, low], axis=0))
    d.store(at, d.load(at, at + 32, cols) + grads[:32], cols)
    d.store(at + 32, grads[32:], cols)


def table_kernel(
    start_ref, len_ref, ids_ref, left_ref, right_ref, t_ref, w_ref, ct_ref,
    grad_ref, weights_ref, chunks_ref, hl0, hl1, both0, both1, d00, d01, d10, d11,
    ids_scr, bands_ref, *scratch,
):
    oh0, oh1, high_ref, low_ref = scratch
    oh_refs = (oh0, oh1)
    hl_refs, both_refs = (hl0, hl1), (both0, both1)
    ds = (Halves(d00, d01), Halves(d10, d11))
    count = ids_ref.shape[1] // 16
    chunks = count + 1
    vocab = t_ref.shape[1]
    start = start_ref[0]
    ids_scr[...] = jnp.zeros_like(ids_scr)
    regroup(left_ref, ids_scr, 7, [count - 1])
    regroup(ids_ref, ids_scr, 8, list(range(count)))
    regroup(right_ref, ids_scr, 8 + count, [0])
    ids, weights, even, length = weigh(start, len_ref, ids_scr, t_ref)
    for e in range(2):
        for b in range(4):
            weights_ref[e * 4 + b] = weights[e][b]
    bands = spread(weights, even)
    for r in RELS:
        bands[r] = jnp.where(alive(even + r, length), 0.5 * bands[r], 0.0)
    store_bands(bands, bands_ref, count)
    per = chunks_ref.shape[0] // 2
    for g in range(2):
        chunks_ref[g * per : g * per + per, :] = to_chunks(ids[0], ids[1], g)
    width = w_ref.shape[1]
    for d in ds:
        d.store(0, jnp.zeros((80, width), F32), slice(None))
        d.store(2 * d.size - 64, jnp.zeros((64, width), F32), slice(None))

    diagonal = diagonals()

    def grad_steps(g, w):
        made = []

        def step(n):
            if not made:
                made.append(banded(bands_ref, g, w, count, diagonal))
                hl_refs[g][w * 160 : w * 160 + 160, :] = made[0]
            window_grads(ct_ref.at[g * 8 : g * 8 + 8], both_refs[g], made[0], ds[g], w, n)

        return [functools.partial(step, n) for n in range(0, width, 256)]

    def part_steps(g, c, put):
        d, oh_ref = ds[g], oh_refs[g]
        to = c * 128
        size = 128 if c < count else 64

        def mark():
            ids = chunks_ref[g * per + c : g * per + c + 1, :]
            oh_ref[:, to : to + 128] = one_hot_t(ids, vocab)
            if size < 128:
                zero = jnp.zeros((128 - size, width), BF16)
                high_ref[put + size : put + 128, :] = zero
                low_ref[put + size : put + 128, :] = zero

        def step(n):
            cols = slice(n, n + 128)
            taps = [jnp.broadcast_to(w_ref[k : k + 1, cols], (64, 128)) for k in range(TAPS)]
            for i in range(0, size, 64):
                near = d.load(to + 24 + i, to + 112 + i, cols)
                total = sum(taps[3 - k] * near[8 * k : 8 * k + 64] for k in range(TAPS))
                high, low = split(total)
                high_ref[put + i : put + i + 64, cols] = high
                low_ref[put + i : put + i + 64, cols] = low

        return [mark] + [functools.partial(step, n) for n in range(0, width, 128)]

    def sum_steps(g, cs, put):
        held = slice(put, put + 128 * len(cs))
        at = slice(cs[0] * 128, cs[-1] * 128 + 128)

        def step(n):
            cols = slice(n, n + 256)
            oh = oh_refs[g][:, at]
            both = jnp.concatenate([high_ref[held, cols], low_ref[held, cols]], axis=0)
            total = dot(jnp.concatenate([oh, oh], axis=1), both)
            if g == 0 and cs[0] == 0:
                grad_ref[:, cols] = total
            else:
                grad_ref[:, cols] += total

        return [functools.partial(step, n) for n in range(0, width, 256)]

    stages = [[], [], []]
    for t, (g, ws) in enumerate(batches(count, min(TABLE_BATCH, count))):
        cs = ws + [count] * (ws[-1] == count - 1)
        put = t % 3 * (TABLE_BATCH + 1) * 128
        stages[0].append(sum((grad_steps(g, w) for w in ws), []))
        stages[1].append(sum((part_steps(g, c, put + 128 * i) for i, c in enumerate(cs)), []))
        stages[2].append(sum_steps(g, cs, put))
    run_stages(stages, (0, 1, 2))


def near_kernel(
    start_ref, len_ref, weights_ref, chunks_ref, e_high, e_low, w_ref, b_ref, s_ref, both0, both1, d00, d01, d10, d11,
    small_ref, high0, low0, high1, low1,
    near_ref, q_ref, sums_ref, oh0, oh1, x_ref,
):
    oh_refs, both_refs = (oh0, oh1), (both0, both1)
    ds = (Halves(d00, d01), Halves(d10, d11))
    high_refs, low_refs = (high0, high1), (low0, low1)
    padded = weights_ref.shape[1]
    count = both0.shape[0] // 128
    chunks = count + 1
    vocab, width = e_high.shape
    start = start_ref[0]
    per = chunks_ref.shape[0] // 2
    small_ref[...] = jnp.zeros_like(small_ref)
    near_ref[...] = jnp.zeros_like(near_ref)
    sums_ref[...] = jnp.zeros_like(sums_ref)
    diagonal = diagonals()
    bias = line(b_ref)
    turned = chunks_ref[...].astype(F32).T

    def slot(g, c):
        return (g * chunks + c) % RING * 128

    def bytes_at(g, c, first, size, cols):
        here = min(128 - first, size)
        at = slot(g, c) + first
        x = x_ref[at : at + here, cols]
        if here == size:
            return x
        at = slot(g, c + 1)
        return jnp.concatenate([x, x_ref[at : at + size - here, cols]], axis=0)

    def look_up_steps(g, cs):
        at = slice(cs[0] * 128, cs[-1] * 128 + 128)

        def mark(c):
            column = jnp.broadcast_to(turned[:, g * per + c : g * per + c + 1], (128, vocab))
            found = jnp.where(column == lanes((128, vocab)).astype(F32), 1.0, 0.0)
            oh_refs[g][c * 128 : c * 128 + 128, :] = found.astype(BF16)

        def step(n):
            cols = slice(n, n + 256)
            oh = oh_refs[g][at, :]
            table = jnp.concatenate([e_high[:, cols], e_low[:, cols]], axis=0)
            x = dot(jnp.concatenate([oh, oh], axis=1), table)
            for i, c in enumerate(cs):
                to = slot(g, c)
                x_ref[to : to + 128, cols] = x[i * 128 : i * 128 + 128]

        return [functools.partial(mark, c) for c in cs] + [
            functools.partial(step, n) for n in range(0, width, 256)
        ]

    def conv_steps(g, c):
        at = c * 128
        size = 128 if c < count else 32
        step_size = min(size, 64)

        def step(n):
            cols = slice(n, n + 128)
            taps = [jnp.broadcast_to(w_ref[k : k + 1, cols], (step_size, 128)) for k in range(TAPS)]
            first = jnp.broadcast_to(bias[:, cols], (step_size, 128))
            sums = [sums_ref[8 * k : 8 * k + 8, cols] for k in range(TAPS + 1)]
            for i in range(at, at + size, step_size):
                d = ds[g].load(i + 48, i + 48 + step_size, cols)
                x = bytes_at(g, c, i - at, step_size + 24, cols)
                total = first
                products = [d]
                for k in range(TAPS):
                    near = x[8 * k : 8 * k + step_size]
                    total = total + taps[k] * near
                    products.append(d * near)
                for k, p in enumerate(products):
                    sums[k] = sums[k] + p.reshape(step_size // 8, 8, 128).sum(0)
                high, low = split(total)
                high_refs[g][i : i + step_size, cols] = high
                low_refs[g][i : i + step_size, cols] = low
            for k in range(TAPS + 1):
                sums_ref[8 * k : 8 * k + 8, cols] = sums[k]

        return [functools.partial(step, n) for n in range(0, width, 128)]

    def meet_steps(g, w):
        at = slice(w * 128, w * 128 + 160)

        made = []

        def product(n):
            cols = slice(n, n + 256)
            ct = both_refs[g][128 * w : 128 * w + 128, cols]
            wide = jnp.concatenate([high_refs[g][at, cols], low_refs[g][at, cols]], axis=1)
            both = dot(wide, jnp.concatenate([ct, ct], axis=1), NT)
            made.append(both if n == 0 else made.pop() + both)

        def meet():
            product = made.pop()
            for i, r in enumerate(RELS):
                total = jnp.zeros((8, 128), F32)
                for u in range(8):
                    row = 8 * (2 * u + 2 + r)
                    total = total + jnp.where(diagonal[u], product[row : row + 8], 0.0)
                found = jnp.sum(total, axis=0, keepdims=True)
                found = found + pltpu.roll(found, 64, 1)
                near_ref[i, 8 + w : 9 + w, g * 64 : g * 64 + 64] = found[:, g * 64 : g * 64 + 64]

        return [functools.partial(product, n) for n in range(0, width, 256)] + [meet]

    stages = [[], [], []]
    for g, ws in batches(count, MIX_BATCH):
        cs = ws + [count] * (ws[-1] == count - 1)
        stages[0].append(look_up_steps(g, cs))
        stages[1].append(sum((conv_steps(g, c) for c in cs), []))
        stages[2].append(sum((meet_steps(g, w) for w in ws), []))
    run_stages(stages, (0, 2, 4))

    for k in range(TAPS + 1):
        total = jnp.sum(sums_ref[8 * k : 8 * k + 8, :], axis=0, keepdims=True)
        to = (k + TAPS) % (TAPS + 1)
        small_ref[to : to + 1, :] = total
    even, length = geometry((padded, 128), start, len_ref)
    weights = [[weights_ref[e * 4 + b] for b in range(4)] for e in range(2)]
    near = {}
    for i, r in enumerate(RELS):
        near[r] = jnp.where(alive(even + r, length), 0.5 * near_ref[i], 0.0)
    d_scores = []
    for e in range(2):
        d_weights = []
        for b, cases in enumerate(members(even, e)):
            total = None
            for rels, where in cases:
                part = sum(near[r] for r in rels)
                total = part if total is None else jnp.where(where, part, total)
            d_weights.append(total * (1.0 / (b + 1)))
        mean = sum(weights[e][b] * d_weights[b] for b in range(4))
        d_scores.append([weights[e][b] * (d_weights[b] - mean) for b in range(4)])
    own = lax.broadcasted_iota(I32, (padded, 128), 0) - 8
    own = (own >= 0) & (own < count)
    q = spread(d_scores, even)
    for r in RELS:
        q[r] = jnp.where(own & alive(even + r, length), q[r], 0.0)
    qe = q[0] + behind(q[2]) + ahead(q[-2])
    qo = q[1] + behind(q[3]) + ahead(q[-1])
    q_sum = jnp.sum(jnp.sum(qe + qo, axis=0, keepdims=True), axis=1, keepdims=True)
    shifted = [
        (ahead(qe), ahead(qo)),
        (qo, ahead(qe)),
        (qe, qo),
        (behind(qo), qe),
    ]
    q_ref[...] = jnp.zeros_like(q_ref)
    for g in range(2):
        for k in range(TAPS):
            flat = to_chunks(*shifted[k], g)
            for c in range(chunks):
                at = (g * chunks + c) * 128
                q_ref[k : k + 1, at : at + 128] = flat[c : c + 1]
    q1, rest = q_ref[...].astype(BF16), q_ref[...]
    rest = rest - q1.astype(F32)
    q2 = rest.astype(BF16)
    q3 = (rest - q2.astype(F32)).astype(BF16)
    q = jnp.concatenate([q1, q2, q3], axis=0)
    xs = chunks * 128
    hist = dot(q[:, :xs], oh_refs[0][...]) + dot(q[:, xs:], oh_refs[1][...])
    hist = hist[:8] + hist[8:16] + hist[16:]
    h_high, h_low = split(hist)
    looked = dot(jnp.concatenate([h_high, h_low], axis=0), e_high[...])
    looked = looked[:8] + looked[8:] + dot(h_high, e_low[...])
    for k in range(TAPS):
        small_ref[k : k + 1, :] += looked[k : k + 1] * line(s_ref)
        at = k * vocab
        small_ref[6 + at // width : 7 + at // width, at % width : at % width + vocab] = hist[k : k + 1]
    small_ref[TAPS : TAPS + 1, :] += q_sum * line(s_ref)
    small_ref[5:6, :] = q_sum * bias + jnp.sum(
        looked[:TAPS] * w_ref[...], axis=0, keepdims=True
    )


def latent_kernel(high0, low0, high1, low1, hl0, hl1, out_ref, latent_ref, sems):
    half, width = latent_ref.shape[1:]
    size = min(LATENT_BATCH, half // 8)
    copies = []
    for g, (high_ref, low_ref, hl_ref) in enumerate(((high0, low0, hl0), (high1, low1, hl1))):
        for w in range(half // 8):
            band = hl_ref[w * 160 : w * 160 + 160, :].astype(F32).T.astype(BF16)
            at = slice(w * 128, w * 128 + 160)
            for n in range(0, width, 256):
                both = dot(band, high_ref[at, n : n + 256])
                rest = dot(band[:64], low_ref[at, n : n + 256])
                out = both[:64] + both[64:] + rest
                latent_ref[g * 8 : g * 8 + 8, 8 * w : 8 * w + 8, n : n + 256] = out.reshape(8, 8, 256)
            if (w + 1) % size == 0:
                done = (pl.ds(g * 8, 8), pl.ds(8 * (w + 1 - size), 8 * size))
                copy = pltpu.make_async_copy(
                    latent_ref.at[done], out_ref.at[done], sems.at[len(copies)]
                )
                copy.start()
                copies.append(copy)
    for copy in copies:
        copy.wait()


def final_kernel(stages, place_ref, mine_ref, theirs_ref, w_ref, s_ref, ge_ref, gw_ref, gb_ref, gs_ref):
    vocab, width = ge_ref.shape
    places = [(0, None)]
    size = vocab
    for i in reversed(range(len(stages))):
        places = [(low | m << 2 * i, None) for m in range(1 << stages[i][2]) for low, _ in places]
    for stage in stages:
        size >>= stage[2]
    half = len(places) // 2
    pieces = [(mine_ref, p * (size + 8)) for p in range(half)]
    pieces += [(theirs_ref, p * (size + 8)) for p in range(half)]
    small = sum(ref[at + size : at + size + 8, :] for ref, at in pieces)
    hist = []
    for k in range(TAPS):
        at = k * vocab
        hist.append(small[6 + at // width : 7 + at // width, at % width : at % width + vocab])
    hist = jnp.concatenate(hist + [jnp.zeros((8 - TAPS, vocab), F32)], axis=0).T
    scaled = w_ref[...] * line(s_ref)
    for k in range(TAPS):
        turned = jnp.broadcast_to(hist[:, k : k + 1], (vocab, 128))
        for n in range(0, width, 128):
            add = turned * scaled[k : k + 1, n : n + 128]
            ge_ref[:, n : n + 128] = add if k == 0 else ge_ref[:, n : n + 128] + add
    for (mask, _), (ref, at) in zip(places, pieces):
        row, rest = 0, vocab
        for i, stage in enumerate(stages):
            rest >>= stage[2]
            row = row + (place_ref[i] ^ ((mask >> 2 * i) & 3)) * rest
        row = pl.multiple_of(row, 8)
        ge_ref[pl.ds(row, size), :] += ref[at : at + size, :]
    gw_ref[...] = small[:TAPS]
    gb_ref[...] = small[TAPS : TAPS + 1].reshape(width)
    gs_ref[...] = small[TAPS + 1 : TAPS + 2].reshape(width)


def in_vmem(*arrays):
    return [pltpu.with_memory_space_constraint(a, pltpu.VMEM) for a in arrays]


def in_hbm(*arrays):
    return [pltpu.with_memory_space_constraint(a, pltpu.HBM) for a in arrays]


def limit(megabytes):
    return pltpu.CompilerParams(vmem_limit_bytes=megabytes * 1024 * 1024)


def cost(flops, moved):
    return pl.CostEstimate(flops=flops, bytes_accessed=moved, transcendentals=0)


def vm(n):
    return [pl.BlockSpec(memory_space=pltpu.VMEM)] * n


def sm(n):
    return [pl.BlockSpec(memory_space=pltpu.SMEM)] * n


def sizes(span):
    count = span // 16
    chunks = count + 1
    per = -(-chunks // 8) * 8
    return count, chunks, per, (span + 16) * 8


def prep_call(*params):
    vocab, width = params[0].shape
    return pl.pallas_call(
        prep_kernel,
        out_shape=(
            pltpu.VMEM((8, vocab), F32),
            pltpu.VMEM((vocab, width), BF16),
            pltpu.VMEM((vocab, width), BF16),
            pltpu.VMEM(params[-1].shape, F32),
        ),
        in_specs=vm(4) + [pl.BlockSpec(memory_space=pl.ANY)],
        out_specs=vm(4),
        scratch_shapes=[pltpu.SemaphoreType.DMA(())],
        compiler_params=limit(4),
        cost_estimate=cost(10**8, 10**6),
        name="prep",
    )(*in_hbm(*params))


def table_call(start, lengths, ids, left, right, table_scores, conv_weight, cotangent):
    rows, half, width = cotangent.shape
    count, chunks, per, d_rows = sizes(2 * half)
    vocab = table_scores.shape[1]
    return pl.pallas_call(
        table_kernel,
        out_shape=(
            pltpu.VMEM((vocab, width), F32),
            pltpu.VMEM((8, 8 + per, 128), F32),
            pltpu.VMEM((2 * per, 128), I32),
            pltpu.VMEM((160 * count, 128), BF16),
            pltpu.VMEM((160 * count, 128), BF16),
            pltpu.VMEM((128 * count, width), BF16),
            pltpu.VMEM((128 * count, width), BF16),
        )
        + (pltpu.VMEM((d_rows // 2, width), F32),) * 4,
        in_specs=sm(2) + vm(6),
        out_specs=vm(11),
        scratch_shapes=[
            pltpu.VMEM((8 + per, 256), I32),
            pltpu.VMEM((12 * count, 128), F32),
        ]
        + [pltpu.VMEM((vocab, chunks * 128), BF16)] * 2
        + [pltpu.VMEM((3 * (TABLE_BATCH + 1) * 128, width), BF16)] * 2,
        compiler_params=limit(12),
        cost_estimate=cost(8 * 10**9, 2 * 10**7),
        name="table_grad",
    )(
        start, lengths, *in_hbm(ids), *in_vmem(left, right, table_scores),
        *in_hbm(conv_weight), *in_vmem(cotangent),
    )


def near_call(start, lengths, weights, id_chunks, e_high, e_low, conv_weight, bias, scorer, *grads):
    count, chunks, per, d_rows = sizes(grads[0].shape[0] // 8)
    vocab, width = e_high.shape
    return pl.pallas_call(
        near_kernel,
        out_shape=[pltpu.VMEM((8, width), F32)] + [pltpu.VMEM((chunks * 128, width), BF16)] * 4,
        in_specs=sm(2) + vm(13),
        out_specs=vm(5),
        scratch_shapes=[
            pltpu.VMEM((6, 8 + per, 128), F32),
            pltpu.VMEM((8, 2 * chunks * 128), F32),
            pltpu.VMEM((8 * (TAPS + 1), width), F32),
        ]
        + [pltpu.VMEM((chunks * 128, vocab), BF16)] * 2
        + [pltpu.VMEM((RING * 128, width), F32)],
        compiler_params=limit(12),
        cost_estimate=cost(16 * 10**9, 4 * 10**7),
        name="near",
    )(
        start, lengths, *in_vmem(weights, id_chunks, e_high, e_low),
        *in_hbm(conv_weight, bias, scorer), *in_vmem(*grads),
    )


def latent_call(kept, shape):
    rows, half, width = shape
    count = half // 8
    return pl.pallas_call(
        latent_kernel,
        out_shape=jax.ShapeDtypeStruct(shape, F32),
        in_specs=vm(6),
        out_specs=pl.BlockSpec(memory_space=pl.ANY),
        scratch_shapes=[
            pltpu.VMEM(shape, F32),
            pltpu.SemaphoreType.DMA((2 * (count // min(LATENT_BATCH, count)),)),
        ],
        compiler_params=limit(8),
        cost_estimate=cost(4 * 10**9, 10**7),
        name="latent",
    )(*in_vmem(*kept))


def partners(axis, mask):
    return [(i, i ^ mask) for i in range(lax.axis_size(axis))]


U32 = jnp.uint32


def offsets(axis, low, bits, size):
    me = (lax.axis_index(axis).astype(U32) >> low) & ((1 << bits) - 1)
    return [(me ^ m) * U32(size) for m in range(1 << bits)]


def part(v, at, size):
    return lax.dynamic_slice(v, (at, U32(0)), (size, v.shape[1]))


def scatter_sum(v, places, size, axis, low):
    total = part(v, places[0], size)
    for m in range(1, len(places)):
        total = total + lax.ppermute(part(v, places[m], size), axis, partners(axis, m << low))
    return total


def exchange_sum(v, axis, low, bits):
    return v + sum(
        lax.ppermute(v, axis, partners(axis, m << low)) for m in range(1, 1 << bits)
    )


def own_place(axis, low, bits):
    return (lax.axis_index(axis) >> low) & ((1 << bits) - 1)


def per_device(byte_ids, lengths, embedding, conv_weight, conv_bias, score_weight, cotangent):
    rows, span = byte_ids.shape
    vocab, width = embedding.shape
    count = span // 16
    seq = lax.axis_size("seq")
    start = (lax.axis_index("seq") * span).reshape(1)

    bits = seq.bit_length() - 1
    groups = [("seq", low, min(2, bits - low)) for low in range(0, bits, 2)]
    stages = [("dp", 0, lax.axis_size("dp").bit_length() - 1)] + groups[:-1]
    parts, places = [], []
    for axis, low, wide in stages:
        parts.append((parts[-1] if parts else vocab) >> wide)
        places.append(offsets(axis, low, wide, parts[-1]))
    here = jnp.stack([own_place(*stage) for stage in stages])
    byte_ids, start, here, places = lax.optimization_barrier((byte_ids, start, here, places))
    up = [(i, i + 1) for i in range(seq - 1)]
    left = lax.ppermute(byte_ids, "seq", up)
    right = lax.ppermute(byte_ids, "seq", [(j, i) for i, j in up])
    table_scores, e_high, e_low, ct = prep_call(
        embedding, conv_weight, conv_bias, score_weight, cotangent
    )
    grad_table, weights, id_chunks, hl0, hl1, *grads = table_call(
        start, lengths, byte_ids, left, right, table_scores, conv_weight, ct
    )
    small, *kept = near_call(
        start, lengths, weights, id_chunks, e_high, e_low, conv_weight, conv_bias, score_weight,
        *grads,
    )
    latent = latent_call(kept + [hl0, hl1], cotangent.shape)

    total = grad_table
    for (axis, low, bits), size, at in zip(stages, parts, places):
        total = scatter_sum(total, at, size, axis, low)
    both = exchange_sum(jnp.concatenate([total, small], axis=0), *groups[-1])
    both, latent = lax.optimization_barrier((both, latent))
    for axis, low, wide in reversed(stages[1:]):
        got = [lax.ppermute(both, axis, partners(axis, m << low)) for m in range(1, 1 << wide)]
        both = jnp.concatenate([both] + got, axis=0)
    theirs = lax.ppermute(both, "dp", partners("dp", 1))

    grad_e, grad_w, grad_b, grad_s = pl.pallas_call(
        functools.partial(final_kernel, stages),
        out_shape=(
            jax.ShapeDtypeStruct((vocab, width), F32),
            jax.ShapeDtypeStruct((TAPS, width), F32),
            jax.ShapeDtypeStruct((width,), F32),
            jax.ShapeDtypeStruct((width,), F32),
        ),
        in_specs=sm(1) + vm(4),
        out_specs=vm(4),
        compiler_params=limit(4),
        name="final",
    )(here, *in_vmem(both, theirs), *in_hbm(conv_weight, score_weight))
    return latent, grad_e, grad_w, grad_b, grad_s


def solution(mesh):
    placed = (P("dp", "seq"), P("dp"), P(), P(), P(), P(), P("dp", "seq", None))
    return jax.shard_map(
        per_device,
        mesh=mesh,
        in_specs=placed,
        out_specs=(P("dp", "seq", None), P(), P(), P(), P()),
        check_vma=False,
    )
```

```python
import functools

import jax
import jax.numpy as jnp
from jax import lax
from jax.experimental import pallas as pl
from jax.experimental.pallas import tpu as pltpu
from jax.sharding import PartitionSpec as P

F32, BF16, I32 = jnp.float32, jnp.bfloat16, jnp.int32
HIGH = lax.Precision.HIGHEST
ROWS = 16
TAPS = 4
TABLE_BATCH, MIX_BATCH, LATENT_BATCH = 4, 4, 4
RING = 18
RELS = (-2, -1, 0, 1, 2, 3)
NT = (((1,), (1,)), ((), ()))
TN = (((0,), (0,)), ((), ()))


def lanes(shape):
    return lax.broadcasted_iota(I32, shape, 1)


def line(ref):
    return ref[...].reshape(1, ref.shape[0])


def pick(x, index):
    return jnp.take_along_axis(x, index, axis=1, mode="promise_in_bounds")


def split(x):
    high = x.astype(BF16)
    return high, (x - high.astype(F32)).astype(BF16)


def dot(a, b, dims=(((1,), (0,)), ((), ()))):
    return lax.dot_general(a, b, dims, preferred_element_type=F32)


def ahead(x):
    lane = lanes(x.shape) % 8
    below = pltpu.roll(x, x.shape[0] - 1, 0)
    return jnp.where(lane == 7, pltpu.roll(below, 7, 1), pltpu.roll(x, 127, 1))


def behind(x):
    lane = lanes(x.shape) % 8
    above = pltpu.roll(x, 1, 0)
    return jnp.where(lane == 0, pltpu.roll(above, 121, 1), pltpu.roll(x, 1, 1))


def geometry(shape, start, len_ref):
    lane = lanes(shape)
    window = lax.broadcasted_iota(I32, shape, 0) - 8
    even = start + 16 * window + 2 * (lane % 8)
    length = jnp.zeros(shape, I32)
    for r in range(ROWS):
        length = jnp.where(lane // 8 == r, len_ref[r], length)
    return even, length


def alive(pos, length):
    return (pos >= 0) & (pos < length)


def members(even, parity):
    offset = (even + parity) % 3
    left = (even // 2) % 2 == 0
    out = [[((parity,), None)], [((0, 1), None)], [], []]
    for o in range(3):
        out[2].append((tuple(parity - o + i for i in range(3)), offset == o))
    out[3] = [((0, 1, 2, 3), left), ((-2, -1, 0, 1), ~left)]
    return out


def to_chunks(xe, xo, g):
    lane = lanes(xe.shape)
    place = (lane // 8 + 12) % 16
    index = g * 64 + (lane % 8) * 8 + place // 2
    y = jnp.where(place % 2 == 0, pick(xe, index), pick(xo, index))
    return jnp.where(lane < 32, pltpu.roll(y, 1, 0), y)[8:]


def prep_kernel(
    start_hbm, len_hbm, ids_hbm, e_hbm, w_hbm, b_hbm, s_hbm, ct_hbm,
    t_ref, high_ref, low_ref, even_ref, length_ref, ids_ref, w_ref, b_ref, s_ref, ct_ref,
    start_ref, len_ref, e_ref, sems,
):
    pairs = [
        (w_hbm, w_ref), (b_hbm, b_ref), (s_hbm, s_ref), (e_hbm, e_ref),
        (start_hbm, start_ref), (len_hbm, len_ref), (ids_hbm, ids_ref),
    ]
    copies = [pltpu.make_async_copy(a, b, sems.at[i]) for i, (a, b) in enumerate(pairs)]
    for r in range(0, ROWS, 2):
        rows = pl.ds(r, 2)
        copies.append(pltpu.make_async_copy(ct_hbm.at[rows], ct_ref.at[rows], sems.at[len(copies)]))
    for copy in copies:
        copy.start()
    for copy in copies[:4]:
        copy.wait()
    scaled = w_ref[...] * line(s_ref)
    wide = jnp.concatenate([scaled, jnp.zeros_like(scaled)], axis=0)
    t = lax.dot_general(wide, e_ref[...], NT, precision=HIGH, preferred_element_type=F32)
    b0 = jnp.sum(line(b_ref) * line(s_ref), axis=1, keepdims=True)
    row = lax.broadcasted_iota(I32, t.shape, 0)
    t_ref[...] = jnp.where(row == TAPS, b0, t)
    high_ref[...], low_ref[...] = split(e_ref[...])
    for copy in copies[4:]:
        copy.wait()
    even_ref[...], length_ref[...] = geometry(even_ref.shape, start_ref[0], len_ref)


def regroup(ids_ref, ids_scr, first, windows):
    for a in range(0, len(windows), 8):
        some = windows[a : a + 8]
        shape = (8, 128)
        lane = lanes(shape)
        window = lax.broadcasted_iota(I32, shape, 0) + some[0]
        column = 16 * some[0] // 128 * 128
        width = min(128, ids_ref.shape[1] - column)
        index = jnp.clip(16 * window + lane % 16 - column, 0, width - 1)
        for g in range(2):
            out = jnp.zeros(shape, I32)
            for r in range(8):
                row = ids_ref[g * 8 + r : g * 8 + r + 1, column : column + width]
                if width < 128:
                    row = jnp.concatenate([row, jnp.zeros((1, 128 - width), I32)], axis=1)
                found = pick(jnp.broadcast_to(row, shape), index)
                out = jnp.where(lane // 16 == r, found, out)
            at = first + a
            ids_scr[at : at + len(some), g * 128 : g * 128 + 128] = out[: len(some)]


def weigh(even, length, ids_scr, t_ref):
    shape = (ids_scr.shape[0], 128)
    lane = lanes(shape)
    live = [alive(even, length), alive(even + 1, length)]
    ids, terms = [], []
    for e in range(2):
        index = ((lane // 8) % 8) * 16 + 2 * (lane % 8) + e
        found = jnp.where(
            lane < 64, pick(ids_scr[:, :128], index), pick(ids_scr[:, 128:], index)
        )
        taps = []
        for k in range(TAPS):
            value = jnp.zeros(shape, F32)
            for half in range(t_ref.shape[1] // 128):
                row = jnp.broadcast_to(t_ref[k : k + 1, half * 128 : half * 128 + 128], shape)
                here = (found >= half * 128) & (found < half * 128 + 128)
                value = jnp.where(here, pick(row, found & 127), value)
            taps.append(jnp.where(live[e], value, 0.0))
        terms.append(taps)
        ids.append(jnp.where(live[e], found, -1))
    b0 = t_ref[TAPS : TAPS + 1, :128]
    (ae, ao) = terms
    ce = jnp.where(live[0], b0 + behind(ae[0] + ao[1]) + ae[2] + ao[3], 0.0)
    co = jnp.where(live[1], b0 + behind(ao[0]) + ae[1] + ao[2] + ahead(ae[3]), 0.0)
    at = {-2: behind(ce), -1: behind(co), 0: ce, 1: co, 2: ahead(ce), 3: ahead(co)}
    weights = []
    for e in range(2):
        scores = []
        for b, cases in enumerate(members(even, e)):
            total = None
            for rels, where in cases:
                part = sum(at[r] for r in rels)
                total = part if total is None else jnp.where(where, part, total)
            scores.append(total * (1.0 / (b + 1)))
        top = functools.reduce(jnp.maximum, scores)
        parts = [jnp.exp(s - top) for s in scores]
        norm = sum(parts)
        weights.append([p / norm for p in parts])
    return ids, weights


def spread(values, even):
    out = {r: 0.0 for r in RELS}
    for e in range(2):
        for b, cases in enumerate(members(even, e)):
            share = values[e][b] * (1.0 / (b + 1))
            for rels, where in cases:
                part = share if where is None else jnp.where(where, share, 0.0)
                for r in rels:
                    out[r] = out[r] + part
    return out


def diagonals():
    shape = (8, 128)
    row, lane = lax.broadcasted_iota(I32, shape, 0), lanes(shape)
    same = row == (lane % 64) // 8
    return [same & (lane % 8 == u) for u in range(8)]


def banded(bands_ref, g, w, count, diagonal):
    lane = lanes((8, 128))
    tiles = [jnp.zeros((8, 128), F32) for _ in range(20)]
    for i, r in enumerate(RELS):
        line = bands_ref[pl.ds((g * len(RELS) + i) * count + w, 1), :]
        high = line.astype(BF16).astype(F32)
        line = jnp.where(lanes((1, 128)) < 64, high, line - high)
        line = jnp.broadcast_to(line, (8, 128))
        for u in range(8):
            at = 2 * u + 2 + r
            tiles[at] = jnp.where(diagonal[u], line, tiles[at])
    return jnp.concatenate(tiles, axis=0).astype(BF16)


def store_bands(bands, bands_ref, count):
    lane = lanes(bands[0].shape)
    for i, r in enumerate(RELS):
        turned = pltpu.roll(bands[r], 64, 1)
        for g in range(2):
            both = jnp.where((lane < 64) == (g == 0), bands[r], turned)
            at = (g * len(RELS) + i) * count
            bands_ref[at : at + count, :] = both[8 : 8 + count]


def one_hot_t(ids, vocab):
    return jnp.where(
        lax.broadcasted_iota(I32, (vocab, 128), 0) == ids, 1.0, 0.0
    ).astype(BF16)


def weave(*parts):
    order = [((i + 0.5) / len(p), k, step) for k, p in enumerate(parts) for i, step in enumerate(p)]
    for _, _, step in sorted(order, key=lambda item: item[:2]):
        step()


def run_stages(stages, lags):
    for slot in range(len(stages[0]) + max(lags)):
        now = [(items, slot - lag) for items, lag in zip(stages, lags)]
        weave(*[items[t] for items, t in now if 0 <= t < len(items)])


def batches(count, size):
    return [(g, list(range(b, b + size))) for g in range(2) for b in range(0, count, size)]


class Halves:
    def __init__(self, first, second):
        self.refs, self.size = (first, second), first.shape[0]

    def parts(self, lo, hi):
        for ref, base in zip(self.refs, (0, self.size)):
            a, b = max(lo, base), min(hi, base + self.size)
            if a < b:
                yield ref, a - base, b - base, a - lo, b - lo

    def load(self, lo, hi, cols):
        found = [ref[a:b, cols] for ref, a, b, _, _ in self.parts(lo, hi)]
        return found[0] if len(found) == 1 else jnp.concatenate(found, axis=0)

    def store(self, lo, value, cols):
        for ref, a, b, i, j in self.parts(lo, lo + value.shape[0]):
            ref[a:b, cols] = value[i:j]


def window_grads(ct_ref, both_ref, hl, d, w, n):
    wide = jnp.concatenate([hl, hl], axis=1)
    at = 128 * w + 48
    cols = slice(n, n + 256)
    high, low = split(ct_ref[:, 8 * w : 8 * w + 8, cols].reshape(64, 256))
    both_ref[128 * w : 128 * w + 64, cols] = high
    both_ref[128 * w + 64 : 128 * w + 128, cols] = low
    grads = dot(wide, jnp.concatenate([high, high, low, low], axis=0))
    d.store(at, d.load(at, at + 32, cols) + grads[:32], cols)
    d.store(at + 32, grads[32:], cols)


def table_kernel(
    even_ref, length_ref, ids_ref, left_ref, right_ref, t_ref, w_ref, ct_ref,
    grad_ref, weights_ref, chunks_ref, hl0, hl1, both0, both1, d00, d01, d10, d11,
    ids_scr, bands_ref, *scratch,
):
    oh0, oh1, high_ref, low_ref = scratch
    oh_refs = (oh0, oh1)
    hl_refs, both_refs = (hl0, hl1), (both0, both1)
    ds = (Halves(d00, d01), Halves(d10, d11))
    count = ids_ref.shape[1] // 16
    chunks = count + 1
    vocab = t_ref.shape[1]
    even, length = even_ref[...], length_ref[...]
    ids_scr[...] = jnp.zeros_like(ids_scr)
    regroup(left_ref, ids_scr, 7, [count - 1])
    regroup(ids_ref, ids_scr, 8, list(range(count)))
    regroup(right_ref, ids_scr, 8 + count, [0])
    ids, weights = weigh(even, length, ids_scr, t_ref)
    for e in range(2):
        for b in range(4):
            weights_ref[e * 4 + b] = weights[e][b]
    bands = spread(weights, even)
    for r in RELS:
        bands[r] = jnp.where(alive(even + r, length), 0.5 * bands[r], 0.0)
    store_bands(bands, bands_ref, count)
    per = chunks_ref.shape[0] // 2
    for g in range(2):
        chunks_ref[g * per : g * per + per, :] = to_chunks(ids[0], ids[1], g)
    width = w_ref.shape[1]
    for d in ds:
        d.store(0, jnp.zeros((80, width), F32), slice(None))
        d.store(2 * d.size - 64, jnp.zeros((64, width), F32), slice(None))

    diagonal = diagonals()

    def grad_steps(g, w):
        made = []

        def step(n):
            if not made:
                made.append(banded(bands_ref, g, w, count, diagonal))
                hl_refs[g][w * 160 : w * 160 + 160, :] = made[0]
            window_grads(ct_ref.at[g * 8 : g * 8 + 8], both_refs[g], made[0], ds[g], w, n)

        return [functools.partial(step, n) for n in range(0, width, 256)]

    def part_steps(g, c, put):
        d, oh_ref = ds[g], oh_refs[g]
        to = c * 128
        size = 128 if c < count else 64

        def mark():
            ids = chunks_ref[g * per + c : g * per + c + 1, :]
            oh_ref[:, to : to + 128] = one_hot_t(ids, vocab)
            if size < 128:
                zero = jnp.zeros((128 - size, width), BF16)
                high_ref[put + size : put + 128, :] = zero
                low_ref[put + size : put + 128, :] = zero

        def step(n):
            cols = slice(n, n + 128)
            taps = [jnp.broadcast_to(w_ref[k : k + 1, cols], (64, 128)) for k in range(TAPS)]
            for i in range(0, size, 64):
                near = d.load(to + 24 + i, to + 112 + i, cols)
                total = sum(taps[3 - k] * near[8 * k : 8 * k + 64] for k in range(TAPS))
                high, low = split(total)
                high_ref[put + i : put + i + 64, cols] = high
                low_ref[put + i : put + i + 64, cols] = low

        return [mark] + [functools.partial(step, n) for n in range(0, width, 128)]

    def sum_steps(g, cs, put):
        held = slice(put, put + 128 * len(cs))
        at = slice(cs[0] * 128, cs[-1] * 128 + 128)

        def step(n):
            cols = slice(n, n + 256)
            oh = oh_refs[g][:, at]
            both = jnp.concatenate([high_ref[held, cols], low_ref[held, cols]], axis=0)
            total = dot(jnp.concatenate([oh, oh], axis=1), both)
            if g == 0 and cs[0] == 0:
                grad_ref[:, cols] = total
            else:
                grad_ref[:, cols] += total

        return [functools.partial(step, n) for n in range(0, width, 256)]

    stages = [[], [], []]
    for t, (g, ws) in enumerate(batches(count, min(TABLE_BATCH, count))):
        cs = ws + [count] * (ws[-1] == count - 1)
        put = t % 3 * (TABLE_BATCH + 1) * 128
        stages[0].append(sum((grad_steps(g, w) for w in ws), []))
        stages[1].append(sum((part_steps(g, c, put + 128 * i) for i, c in enumerate(cs)), []))
        stages[2].append(sum_steps(g, cs, put))
    run_stages(stages, (0, 1, 2))


def near_kernel(
    even_ref, length_ref, weights_ref, chunks_ref, e_high, e_low, w_ref, b_ref, s_ref, both0, both1, d00, d01, d10, d11,
    small_ref, high0, low0, high1, low1,
    near_ref, q_ref, sums_ref, oh0, oh1, x_ref,
):
    oh_refs, both_refs = (oh0, oh1), (both0, both1)
    ds = (Halves(d00, d01), Halves(d10, d11))
    high_refs, low_refs = (high0, high1), (low0, low1)
    padded = weights_ref.shape[1]
    count = both0.shape[0] // 128
    chunks = count + 1
    vocab, width = e_high.shape
    per = chunks_ref.shape[0] // 2
    small_ref[...] = jnp.zeros_like(small_ref)
    near_ref[...] = jnp.zeros_like(near_ref)
    sums_ref[...] = jnp.zeros_like(sums_ref)
    diagonal = diagonals()
    bias = line(b_ref)
    turned = chunks_ref[...].astype(F32).T

    def slot(g, c):
        return (g * chunks + c) % RING * 128

    def bytes_at(g, c, first, size, cols):
        here = min(128 - first, size)
        at = slot(g, c) + first
        x = x_ref[at : at + here, cols]
        if here == size:
            return x
        at = slot(g, c + 1)
        return jnp.concatenate([x, x_ref[at : at + size - here, cols]], axis=0)

    def look_up_steps(g, cs):
        at = slice(cs[0] * 128, cs[-1] * 128 + 128)

        def mark(c):
            column = jnp.broadcast_to(turned[:, g * per + c : g * per + c + 1], (128, vocab))
            found = jnp.where(column == lanes((128, vocab)).astype(F32), 1.0, 0.0)
            oh_refs[g][c * 128 : c * 128 + 128, :] = found.astype(BF16)

        def step(n):
            cols = slice(n, n + 256)
            oh = oh_refs[g][at, :]
            table = jnp.concatenate([e_high[:, cols], e_low[:, cols]], axis=0)
            x = dot(jnp.concatenate([oh, oh], axis=1), table)
            for i, c in enumerate(cs):
                to = slot(g, c)
                x_ref[to : to + 128, cols] = x[i * 128 : i * 128 + 128]

        return [functools.partial(mark, c) for c in cs] + [
            functools.partial(step, n) for n in range(0, width, 256)
        ]

    def conv_steps(g, c):
        at = c * 128
        size = 128 if c < count else 32
        step_size = min(size, 64)

        def step(n):
            cols = slice(n, n + 128)
            taps = [jnp.broadcast_to(w_ref[k : k + 1, cols], (step_size, 128)) for k in range(TAPS)]
            first = jnp.broadcast_to(bias[:, cols], (step_size, 128))
            sums = [sums_ref[8 * k : 8 * k + 8, cols] for k in range(TAPS + 1)]
            for i in range(at, at + size, step_size):
                d = ds[g].load(i + 48, i + 48 + step_size, cols)
                x = bytes_at(g, c, i - at, step_size + 24, cols)
                total = first
                products = [d]
                for k in range(TAPS):
                    near = x[8 * k : 8 * k + step_size]
                    total = total + taps[k] * near
                    products.append(d * near)
                for k, p in enumerate(products):
                    sums[k] = sums[k] + p.reshape(step_size // 8, 8, 128).sum(0)
                high, low = split(total)
                high_refs[g][i : i + step_size, cols] = high
                low_refs[g][i : i + step_size, cols] = low
            for k in range(TAPS + 1):
                sums_ref[8 * k : 8 * k + 8, cols] = sums[k]

        return [functools.partial(step, n) for n in range(0, width, 128)]

    def meet_steps(g, w):
        at = slice(w * 128, w * 128 + 160)

        made = []

        def product(n):
            cols = slice(n, n + 256)
            ct = both_refs[g][128 * w : 128 * w + 128, cols]
            wide = jnp.concatenate([high_refs[g][at, cols], low_refs[g][at, cols]], axis=1)
            both = dot(wide, jnp.concatenate([ct, ct], axis=1), NT)
            made.append(both if n == 0 else made.pop() + both)

        def meet():
            product = made.pop()
            for i, r in enumerate(RELS):
                total = jnp.zeros((8, 128), F32)
                for u in range(8):
                    row = 8 * (2 * u + 2 + r)
                    total = total + jnp.where(diagonal[u], product[row : row + 8], 0.0)
                found = jnp.sum(total, axis=0, keepdims=True)
                found = found + pltpu.roll(found, 64, 1)
                near_ref[i, 8 + w : 9 + w, g * 64 : g * 64 + 64] = found[:, g * 64 : g * 64 + 64]

        return [functools.partial(product, n) for n in range(0, width, 256)] + [meet]

    stages = [[], [], []]
    for g, ws in batches(count, MIX_BATCH):
        cs = ws + [count] * (ws[-1] == count - 1)
        stages[0].append(look_up_steps(g, cs))
        stages[1].append(sum((conv_steps(g, c) for c in cs), []))
        stages[2].append(sum((meet_steps(g, w) for w in ws), []))
    run_stages(stages, (0, 2, 4))

    for k in range(TAPS + 1):
        total = jnp.sum(sums_ref[8 * k : 8 * k + 8, :], axis=0, keepdims=True)
        to = (k + TAPS) % (TAPS + 1)
        small_ref[to : to + 1, :] = total
    even, length = even_ref[...], length_ref[...]
    weights = [[weights_ref[e * 4 + b] for b in range(4)] for e in range(2)]
    near = {}
    for i, r in enumerate(RELS):
        near[r] = jnp.where(alive(even + r, length), 0.5 * near_ref[i], 0.0)
    d_scores = []
    for e in range(2):
        d_weights = []
        for b, cases in enumerate(members(even, e)):
            total = None
            for rels, where in cases:
                part = sum(near[r] for r in rels)
                total = part if total is None else jnp.where(where, part, total)
            d_weights.append(total * (1.0 / (b + 1)))
        mean = sum(weights[e][b] * d_weights[b] for b in range(4))
        d_scores.append([weights[e][b] * (d_weights[b] - mean) for b in range(4)])
    own = lax.broadcasted_iota(I32, (padded, 128), 0) - 8
    own = (own >= 0) & (own < count)
    q = spread(d_scores, even)
    for r in RELS:
        q[r] = jnp.where(own & alive(even + r, length), q[r], 0.0)
    qe = q[0] + behind(q[2]) + ahead(q[-2])
    qo = q[1] + behind(q[3]) + ahead(q[-1])
    q_sum = jnp.sum(jnp.sum(qe + qo, axis=0, keepdims=True), axis=1, keepdims=True)
    shifted = [
        (ahead(qe), ahead(qo)),
        (qo, ahead(qe)),
        (qe, qo),
        (behind(qo), qe),
    ]
    q_ref[...] = jnp.zeros_like(q_ref)
    for g in range(2):
        for k in range(TAPS):
            flat = to_chunks(*shifted[k], g)
            for c in range(chunks):
                at = (g * chunks + c) * 128
                q_ref[k : k + 1, at : at + 128] = flat[c : c + 1]
    q1, rest = q_ref[...].astype(BF16), q_ref[...]
    rest = rest - q1.astype(F32)
    q2 = rest.astype(BF16)
    q3 = (rest - q2.astype(F32)).astype(BF16)
    q = jnp.concatenate([q1, q2, q3], axis=0)
    xs = chunks * 128
    hist = dot(q[:, :xs], oh_refs[0][...]) + dot(q[:, xs:], oh_refs[1][...])
    hist = hist[:8] + hist[8:16] + hist[16:]
    h_high, h_low = split(hist)
    looked = dot(jnp.concatenate([h_high, h_low], axis=0), e_high[...])
    looked = looked[:8] + looked[8:] + dot(h_high, e_low[...])
    for k in range(TAPS):
        small_ref[k : k + 1, :] += looked[k : k + 1] * line(s_ref)
        at = k * vocab
        small_ref[6 + at // width : 7 + at // width, at % width : at % width + vocab] = hist[k : k + 1]
    small_ref[TAPS : TAPS + 1, :] += q_sum * line(s_ref)
    small_ref[5:6, :] = q_sum * bias + jnp.sum(
        looked[:TAPS] * w_ref[...], axis=0, keepdims=True
    )


def latent_kernel(high0, low0, high1, low1, hl0, hl1, out_ref, latent_ref, sems):
    half, width = latent_ref.shape[1:]
    size = min(LATENT_BATCH, half // 8)
    copies = []
    for g, (high_ref, low_ref, hl_ref) in enumerate(((high0, low0, hl0), (high1, low1, hl1))):
        for w in range(half // 8):
            band = hl_ref[w * 160 : w * 160 + 160, :].astype(F32).T.astype(BF16)
            at = slice(w * 128, w * 128 + 160)
            for n in range(0, width, 256):
                both = dot(band, high_ref[at, n : n + 256])
                rest = dot(band[:64], low_ref[at, n : n + 256])
                out = both[:64] + both[64:] + rest
                latent_ref[g * 8 : g * 8 + 8, 8 * w : 8 * w + 8, n : n + 256] = out.reshape(8, 8, 256)
            if (w + 1) % size == 0:
                done = (pl.ds(g * 8, 8), pl.ds(8 * (w + 1 - size), 8 * size))
                copy = pltpu.make_async_copy(
                    latent_ref.at[done], out_ref.at[done], sems.at[len(copies)]
                )
                copy.start()
                copies.append(copy)
    for copy in copies:
        copy.wait()


def final_kernel(stages, place_ref, mine_ref, theirs_ref, w_ref, s_ref, ge_ref, gw_ref, gb_ref, gs_ref):
    vocab, width = ge_ref.shape
    places = [(0, None)]
    size = vocab
    for i in reversed(range(len(stages))):
        places = [(low | m << 2 * i, None) for m in range(1 << stages[i][2]) for low, _ in places]
    for stage in stages:
        size >>= stage[2]
    half = len(places) // 2
    pieces = [(mine_ref, p * (size + 8)) for p in range(half)]
    pieces += [(theirs_ref, p * (size + 8)) for p in range(half)]
    small = sum(ref[at + size : at + size + 8, :] for ref, at in pieces)
    hist = []
    for k in range(TAPS):
        at = k * vocab
        hist.append(small[6 + at // width : 7 + at // width, at % width : at % width + vocab])
    hist = jnp.concatenate(hist + [jnp.zeros((8 - TAPS, vocab), F32)], axis=0).T
    scaled = w_ref[...] * line(s_ref)
    for k in range(TAPS):
        turned = jnp.broadcast_to(hist[:, k : k + 1], (vocab, 128))
        for n in range(0, width, 128):
            add = turned * scaled[k : k + 1, n : n + 128]
            ge_ref[:, n : n + 128] = add if k == 0 else ge_ref[:, n : n + 128] + add
    for (mask, _), (ref, at) in zip(places, pieces):
        row, rest = 0, vocab
        for i, stage in enumerate(stages):
            rest >>= stage[2]
            row = row + (place_ref[i] ^ ((mask >> 2 * i) & 3)) * rest
        row = pl.multiple_of(row, 8)
        ge_ref[pl.ds(row, size), :] += ref[at : at + size, :]
    gw_ref[...] = small[:TAPS]
    gb_ref[...] = small[TAPS : TAPS + 1].reshape(width)
    gs_ref[...] = small[TAPS + 1 : TAPS + 2].reshape(width)


def in_vmem(*arrays):
    return [pltpu.with_memory_space_constraint(a, pltpu.VMEM) for a in arrays]


def in_hbm(*arrays):
    return [pltpu.with_memory_space_constraint(a, pltpu.HBM) for a in arrays]


def limit(megabytes):
    return pltpu.CompilerParams(vmem_limit_bytes=megabytes * 1024 * 1024)


def cost(flops, moved):
    return pl.CostEstimate(flops=flops, bytes_accessed=moved, transcendentals=0)


def vm(n):
    return [pl.BlockSpec(memory_space=pltpu.VMEM)] * n


def sm(n):
    return [pl.BlockSpec(memory_space=pltpu.SMEM)] * n


def sizes(span):
    count = span // 16
    chunks = count + 1
    per = -(-chunks // 8) * 8
    return count, chunks, per, (span + 16) * 8


def prep_call(start, lengths, ids, embedding, conv_weight, bias, scorer, cotangent):
    vocab, width = embedding.shape
    count, chunks, per, d_rows = sizes(ids.shape[1])
    return pl.pallas_call(
        prep_kernel,
        out_shape=(
            pltpu.VMEM((8, vocab), F32),
            pltpu.VMEM((vocab, width), BF16),
            pltpu.VMEM((vocab, width), BF16),
            pltpu.VMEM((8 + per, 128), I32),
            pltpu.VMEM((8 + per, 128), I32),
            pltpu.VMEM(ids.shape, I32),
            pltpu.VMEM(conv_weight.shape, F32),
            pltpu.VMEM(bias.shape, F32),
            pltpu.VMEM(scorer.shape, F32),
            pltpu.VMEM(cotangent.shape, F32),
        ),
        in_specs=[pl.BlockSpec(memory_space=pl.ANY)] * 8,
        out_specs=vm(10),
        scratch_shapes=[
            pltpu.SMEM((1,), I32),
            pltpu.SMEM(lengths.shape, I32),
            pltpu.VMEM((vocab, width), F32),
            pltpu.SemaphoreType.DMA((7 + ROWS // 2,)),
        ],
        compiler_params=limit(4),
        cost_estimate=cost(10**8, 10**6),
        name="prep",
    )(*in_hbm(start, lengths, ids, embedding, conv_weight, bias, scorer, cotangent))


def table_call(even, length, ids, left, right, table_scores, conv_weight, cotangent):
    rows, half, width = cotangent.shape
    count, chunks, per, d_rows = sizes(2 * half)
    vocab = table_scores.shape[1]
    return pl.pallas_call(
        table_kernel,
        out_shape=(
            pltpu.VMEM((vocab, width), F32),
            pltpu.VMEM((8, 8 + per, 128), F32),
            pltpu.VMEM((2 * per, 128), I32),
            pltpu.VMEM((160 * count, 128), BF16),
            pltpu.VMEM((160 * count, 128), BF16),
            pltpu.VMEM((128 * count, width), BF16),
            pltpu.VMEM((128 * count, width), BF16),
        )
        + (pltpu.VMEM((d_rows // 2, width), F32),) * 4,
        in_specs=vm(8),
        out_specs=vm(11),
        scratch_shapes=[
            pltpu.VMEM((8 + per, 256), I32),
            pltpu.VMEM((12 * count, 128), F32),
        ]
        + [pltpu.VMEM((vocab, chunks * 128), BF16)] * 2
        + [pltpu.VMEM((3 * (TABLE_BATCH + 1) * 128, width), BF16)] * 2,
        compiler_params=limit(12),
        cost_estimate=cost(8 * 10**9, 2 * 10**7),
        name="table_grad",
    )(*in_vmem(even, length, ids, left, right, table_scores, conv_weight, cotangent))


def near_call(even, length, weights, id_chunks, e_high, e_low, conv_weight, bias, scorer, *grads):
    count, chunks, per, d_rows = sizes(grads[0].shape[0] // 8)
    vocab, width = e_high.shape
    return pl.pallas_call(
        near_kernel,
        out_shape=[pltpu.VMEM((8, width), F32)] + [pltpu.VMEM((chunks * 128, width), BF16)] * 4,
        in_specs=vm(15),
        out_specs=vm(5),
        scratch_shapes=[
            pltpu.VMEM((6, 8 + per, 128), F32),
            pltpu.VMEM((8, 2 * chunks * 128), F32),
            pltpu.VMEM((8 * (TAPS + 1), width), F32),
        ]
        + [pltpu.VMEM((chunks * 128, vocab), BF16)] * 2
        + [pltpu.VMEM((RING * 128, width), F32)],
        compiler_params=limit(12),
        cost_estimate=cost(16 * 10**9, 4 * 10**7),
        name="near",
    )(*in_vmem(even, length, weights, id_chunks, e_high, e_low, conv_weight, bias, scorer, *grads))


def latent_call(kept, shape):
    rows, half, width = shape
    count = half // 8
    return pl.pallas_call(
        latent_kernel,
        out_shape=jax.ShapeDtypeStruct(shape, F32),
        in_specs=vm(6),
        out_specs=pl.BlockSpec(memory_space=pl.ANY),
        scratch_shapes=[
            pltpu.VMEM(shape, F32),
            pltpu.SemaphoreType.DMA((2 * (count // min(LATENT_BATCH, count)),)),
        ],
        compiler_params=limit(8),
        cost_estimate=cost(4 * 10**9, 10**7),
        name="latent",
    )(*in_vmem(*kept))


def partners(axis, mask):
    return [(i, i ^ mask) for i in range(lax.axis_size(axis))]


U32 = jnp.uint32


def offsets(axis, low, bits, size):
    me = (lax.axis_index(axis).astype(U32) >> low) & ((1 << bits) - 1)
    return [(me ^ m) * U32(size) for m in range(1 << bits)]


def part(v, at, size):
    return lax.dynamic_slice(v, (at, U32(0)), (size, v.shape[1]))


def scatter_sum(v, places, size, axis, low):
    total = part(v, places[0], size)
    for m in range(1, len(places)):
        total = total + lax.ppermute(part(v, places[m], size), axis, partners(axis, m << low))
    return total


def exchange_sum(v, axis, low, bits):
    return v + sum(
        lax.ppermute(v, axis, partners(axis, m << low)) for m in range(1, 1 << bits)
    )


def own_place(axis, low, bits):
    return (lax.axis_index(axis) >> low) & ((1 << bits) - 1)


def per_device(byte_ids, lengths, embedding, conv_weight, conv_bias, score_weight, cotangent):
    rows, span = byte_ids.shape
    vocab, width = embedding.shape
    count = span // 16
    seq = lax.axis_size("seq")
    start = (lax.axis_index("seq") * span).reshape(1)

    bits = seq.bit_length() - 1
    groups = [("seq", low, min(2, bits - low)) for low in range(0, bits, 2)]
    stages = [("dp", 0, lax.axis_size("dp").bit_length() - 1)] + groups[:-1]
    parts, places = [], []
    for axis, low, wide in stages:
        parts.append((parts[-1] if parts else vocab) >> wide)
        places.append(offsets(axis, low, wide, parts[-1]))
    here = jnp.stack([own_place(*stage) for stage in stages])
    byte_ids, start, here, places = lax.optimization_barrier((byte_ids, start, here, places))
    up = [(i, i + 1) for i in range(seq - 1)]
    left = lax.ppermute(byte_ids, "seq", up)
    right = lax.ppermute(byte_ids, "seq", [(j, i) for i, j in up])
    table_scores, e_high, e_low, even, length, ids, taps, bias, scorer, ct = prep_call(
        start, lengths, byte_ids, embedding, conv_weight, conv_bias, score_weight, cotangent
    )
    grad_table, weights, id_chunks, hl0, hl1, *grads = table_call(
        even, length, ids, left, right, table_scores, taps, ct
    )
    small, *kept = near_call(
        even, length, weights, id_chunks, e_high, e_low, taps, bias, scorer, *grads
    )
    latent = latent_call(kept + [hl0, hl1], cotangent.shape)

    total = grad_table
    for (axis, low, bits), size, at in zip(stages, parts, places):
        total = scatter_sum(total, at, size, axis, low)
    both = exchange_sum(jnp.concatenate([total, small], axis=0), *groups[-1])
    both, latent = lax.optimization_barrier((both, latent))
    for axis, low, wide in reversed(stages[1:]):
        got = [lax.ppermute(both, axis, partners(axis, m << low)) for m in range(1, 1 << wide)]
        both = jnp.concatenate([both] + got, axis=0)
    theirs = lax.ppermute(both, "dp", partners("dp", 1))

    grad_e, grad_w, grad_b, grad_s = pl.pallas_call(
        functools.partial(final_kernel, stages),
        out_shape=(
            jax.ShapeDtypeStruct((vocab, width), F32),
            jax.ShapeDtypeStruct((TAPS, width), F32),
            jax.ShapeDtypeStruct((width,), F32),
            jax.ShapeDtypeStruct((width,), F32),
        ),
        in_specs=sm(1) + vm(4),
        out_specs=vm(4),
        compiler_params=limit(4),
        name="final",
    )(here, *in_vmem(both, theirs, taps, scorer))
    return latent, grad_e, grad_w, grad_b, grad_s


def solution(mesh):
    placed = (P("dp", "seq"), P("dp"), P(), P(), P(), P(), P("dp", "seq", None))
    return jax.shard_map(
        per_device,
        mesh=mesh,
        in_specs=placed,
        out_specs=(P("dp", "seq", None), P(), P(), P(), P()),
        check_vma=False,
    )
```

```python
import functools

import jax
import jax.numpy as jnp
from jax import lax
from jax.experimental import pallas as pl
from jax.experimental.pallas import tpu as pltpu
from jax.sharding import PartitionSpec as P

F32, BF16, I32 = jnp.float32, jnp.bfloat16, jnp.int32
HIGH = lax.Precision.HIGHEST
ROWS = 16
TAPS = 4
TABLE_BATCH, MIX_BATCH, LATENT_BATCH = 4, 4, 4
RING = 18
RELS = (-2, -1, 0, 1, 2, 3)
NT = (((1,), (1,)), ((), ()))
TN = (((0,), (0,)), ((), ()))


def lanes(shape):
    return lax.broadcasted_iota(I32, shape, 1)


def line(ref):
    return ref[...].reshape(1, ref.shape[0])


def pick(x, index):
    return jnp.take_along_axis(x, index, axis=1, mode="promise_in_bounds")


def split(x):
    high = x.astype(BF16)
    return high, (x - high.astype(F32)).astype(BF16)


def dot(a, b, dims=(((1,), (0,)), ((), ()))):
    return lax.dot_general(a, b, dims, preferred_element_type=F32)


def ahead(x):
    lane = lanes(x.shape) % 8
    below = pltpu.roll(x, x.shape[0] - 1, 0)
    return jnp.where(lane == 7, pltpu.roll(below, 7, 1), pltpu.roll(x, 127, 1))


def behind(x):
    lane = lanes(x.shape) % 8
    above = pltpu.roll(x, 1, 0)
    return jnp.where(lane == 0, pltpu.roll(above, 121, 1), pltpu.roll(x, 1, 1))


def geometry(shape, start, len_ref):
    lane = lanes(shape)
    window = lax.broadcasted_iota(I32, shape, 0) - 8
    even = start + 16 * window + 2 * (lane % 8)
    length = jnp.zeros(shape, I32)
    for r in range(ROWS):
        length = jnp.where(lane // 8 == r, len_ref[r], length)
    return even, length


def alive(pos, length):
    return (pos >= 0) & (pos < length)


def members(even, parity):
    offset = (even + parity) % 3
    left = (even // 2) % 2 == 0
    out = [[((parity,), None)], [((0, 1), None)], [], []]
    for o in range(3):
        out[2].append((tuple(parity - o + i for i in range(3)), offset == o))
    out[3] = [((0, 1, 2, 3), left), ((-2, -1, 0, 1), ~left)]
    return out


def to_chunks(xe, xo, g):
    lane = lanes(xe.shape)
    place = (lane // 8 + 12) % 16
    index = g * 64 + (lane % 8) * 8 + place // 2
    y = jnp.where(place % 2 == 0, pick(xe, index), pick(xo, index))
    return jnp.where(lane < 32, pltpu.roll(y, 1, 0), y)[8:]


def prep_kernel(
    start_hbm, len_hbm, ids_hbm, e_hbm, w_hbm, b_hbm, s_hbm, ct_hbm,
    t_ref, high_ref, low_ref, even_ref, length_ref, ids_ref, w_ref, b_ref, s_ref, ct_ref,
    start_ref, len_ref, e_ref, sems,
):
    pairs = [
        (w_hbm, w_ref), (b_hbm, b_ref), (s_hbm, s_ref), (e_hbm, e_ref),
        (start_hbm, start_ref), (len_hbm, len_ref), (ids_hbm, ids_ref),
    ]
    copies = [pltpu.make_async_copy(a, b, sems.at[i]) for i, (a, b) in enumerate(pairs)]
    for r in range(0, ROWS, 2):
        rows = pl.ds(r, 2)
        copies.append(pltpu.make_async_copy(ct_hbm.at[rows], ct_ref.at[rows], sems.at[len(copies)]))
    for copy in copies:
        copy.start()
    for copy in copies[:4]:
        copy.wait()
    scaled = w_ref[...] * line(s_ref)
    wide = jnp.concatenate([scaled, jnp.zeros_like(scaled)], axis=0)
    t = lax.dot_general(wide, e_ref[...], NT, precision=HIGH, preferred_element_type=F32)
    b0 = jnp.sum(line(b_ref) * line(s_ref), axis=1, keepdims=True)
    row = lax.broadcasted_iota(I32, t.shape, 0)
    t_ref[...] = jnp.where(row == TAPS, b0, t)
    high_ref[...], low_ref[...] = split(e_ref[...])
    for copy in copies[4:]:
        copy.wait()
    even_ref[...], length_ref[...] = geometry(even_ref.shape, start_ref[0], len_ref)


def regroup(ids_ref, ids_scr, first, windows):
    for a in range(0, len(windows), 8):
        some = windows[a : a + 8]
        shape = (8, 128)
        lane = lanes(shape)
        window = lax.broadcasted_iota(I32, shape, 0) + some[0]
        column = 16 * some[0] // 128 * 128
        width = min(128, ids_ref.shape[1] - column)
        index = jnp.clip(16 * window + lane % 16 - column, 0, width - 1)
        for g in range(2):
            out = jnp.zeros(shape, I32)
            for r in range(8):
                row = ids_ref[g * 8 + r : g * 8 + r + 1, column : column + width]
                if width < 128:
                    row = jnp.concatenate([row, jnp.zeros((1, 128 - width), I32)], axis=1)
                found = pick(jnp.broadcast_to(row, shape), index)
                out = jnp.where(lane // 16 == r, found, out)
            at = first + a
            ids_scr[at : at + len(some), g * 128 : g * 128 + 128] = out[: len(some)]


def weigh(even, length, ids_scr, t_ref):
    shape = (ids_scr.shape[0], 128)
    lane = lanes(shape)
    live = [alive(even, length), alive(even + 1, length)]
    ids, terms = [], []
    for e in range(2):
        index = ((lane // 8) % 8) * 16 + 2 * (lane % 8) + e
        found = jnp.where(
            lane < 64, pick(ids_scr[:, :128], index), pick(ids_scr[:, 128:], index)
        )
        taps = []
        for k in range(TAPS):
            value = jnp.zeros(shape, F32)
            for half in range(t_ref.shape[1] // 128):
                row = jnp.broadcast_to(t_ref[k : k + 1, half * 128 : half * 128 + 128], shape)
                here = (found >= half * 128) & (found < half * 128 + 128)
                value = jnp.where(here, pick(row, found & 127), value)
            taps.append(jnp.where(live[e], value, 0.0))
        terms.append(taps)
        ids.append(jnp.where(live[e], found, -1))
    b0 = t_ref[TAPS : TAPS + 1, :128]
    (ae, ao) = terms
    ce = jnp.where(live[0], b0 + behind(ae[0] + ao[1]) + ae[2] + ao[3], 0.0)
    co = jnp.where(live[1], b0 + behind(ao[0]) + ae[1] + ao[2] + ahead(ae[3]), 0.0)
    at = {-2: behind(ce), -1: behind(co), 0: ce, 1: co, 2: ahead(ce), 3: ahead(co)}
    weights = []
    for e in range(2):
        scores = []
        for b, cases in enumerate(members(even, e)):
            total = None
            for rels, where in cases:
                part = sum(at[r] for r in rels)
                total = part if total is None else jnp.where(where, part, total)
            scores.append(total * (1.0 / (b + 1)))
        top = functools.reduce(jnp.maximum, scores)
        parts = [jnp.exp(s - top) for s in scores]
        norm = sum(parts)
        weights.append([p / norm for p in parts])
    return ids, weights


def spread(values, even):
    out = {r: 0.0 for r in RELS}
    for e in range(2):
        for b, cases in enumerate(members(even, e)):
            share = values[e][b] * (1.0 / (b + 1))
            for rels, where in cases:
                part = share if where is None else jnp.where(where, share, 0.0)
                for r in rels:
                    out[r] = out[r] + part
    return out


def diagonals():
    shape = (8, 128)
    row, lane = lax.broadcasted_iota(I32, shape, 0), lanes(shape)
    same = row == (lane % 64) // 8
    return [same & (lane % 8 == u) for u in range(8)]


def banded(bands_ref, g, w, count, diagonal):
    lane = lanes((8, 128))
    tiles = [jnp.zeros((8, 128), F32) for _ in range(20)]
    for i, r in enumerate(RELS):
        line = bands_ref[pl.ds((g * len(RELS) + i) * count + w, 1), :]
        high = line.astype(BF16).astype(F32)
        line = jnp.where(lanes((1, 128)) < 64, high, line - high)
        line = jnp.broadcast_to(line, (8, 128))
        for u in range(8):
            at = 2 * u + 2 + r
            tiles[at] = jnp.where(diagonal[u], line, tiles[at])
    return jnp.concatenate(tiles, axis=0).astype(BF16)


def store_bands(bands, bands_ref, count):
    lane = lanes(bands[0].shape)
    for i, r in enumerate(RELS):
        turned = pltpu.roll(bands[r], 64, 1)
        for g in range(2):
            both = jnp.where((lane < 64) == (g == 0), bands[r], turned)
            at = (g * len(RELS) + i) * count
            bands_ref[at : at + count, :] = both[8 : 8 + count]


def one_hot_t(ids, vocab):
    value = lax.broadcasted_iota(I32, (vocab, 128), 0).astype(F32).astype(BF16)
    match = value == jnp.broadcast_to(ids.astype(F32), (16, 128)).astype(BF16)[:1]
    return jnp.where(match, jnp.ones((), BF16), jnp.zeros((), BF16))


def weave(*parts):
    late = [0.9 if k == len(parts) - 2 else 0.0 for k in range(len(parts))]
    order = [((i + late[k]) / len(p), k, s) for k, p in enumerate(parts) for i, s in enumerate(p)]
    for _, _, step in sorted(order, key=lambda item: item[:2]):
        step()


def run_stages(stages, lags):
    for slot in range(len(stages[0]) + max(lags)):
        now = [(items, slot - lag) for items, lag in zip(stages, lags)]
        weave(*[items[t] for items, t in now if 0 <= t < len(items)])


def batches(count, size):
    return [(g, list(range(b, b + size))) for g in range(2) for b in range(0, count, size)]


class Halves:
    def __init__(self, first, second):
        self.refs, self.size = (first, second), first.shape[0]

    def parts(self, lo, hi):
        for ref, base in zip(self.refs, (0, self.size)):
            a, b = max(lo, base), min(hi, base + self.size)
            if a < b:
                yield ref, a - base, b - base, a - lo, b - lo

    def load(self, lo, hi, cols):
        found = [ref[a:b, cols] for ref, a, b, _, _ in self.parts(lo, hi)]
        return found[0] if len(found) == 1 else jnp.concatenate(found, axis=0)

    def store(self, lo, value, cols):
        for ref, a, b, i, j in self.parts(lo, lo + value.shape[0]):
            ref[a:b, cols] = value[i:j]


def window_grads(ct_ref, both_ref, hl, d, w, n):
    wide = jnp.concatenate([hl, hl], axis=1)
    at = 128 * w + 48
    cols = slice(n, n + 256)
    high, low = split(ct_ref[:, 8 * w : 8 * w + 8, cols].reshape(64, 256))
    both_ref[128 * w : 128 * w + 64, cols] = high
    both_ref[128 * w + 64 : 128 * w + 128, cols] = low
    grads = dot(wide, jnp.concatenate([high, high, low, low], axis=0))
    d.store(at, d.load(at, at + 32, cols) + grads[:32], cols)
    d.store(at + 32, grads[32:], cols)


def table_kernel(
    even_ref, length_ref, ids_ref, left_ref, right_ref, t_ref, w_ref, ct_ref,
    grad_ref, weights_ref, chunks_ref, hl0, hl1, both0, both1, d00, d01, d10, d11,
    ids_scr, bands_ref, *scratch,
):
    oh0, oh1, high_ref, low_ref = scratch
    oh_refs = (oh0, oh1)
    hl_refs, both_refs = (hl0, hl1), (both0, both1)
    ds = (Halves(d00, d01), Halves(d10, d11))
    count = ids_ref.shape[1] // 16
    chunks = count + 1
    vocab = t_ref.shape[1]
    even, length = even_ref[...], length_ref[...]
    ids_scr[...] = jnp.zeros_like(ids_scr)
    regroup(left_ref, ids_scr, 7, [count - 1])
    regroup(ids_ref, ids_scr, 8, list(range(count)))
    regroup(right_ref, ids_scr, 8 + count, [0])
    ids, weights = weigh(even, length, ids_scr, t_ref)
    for e in range(2):
        for b in range(4):
            weights_ref[e * 4 + b] = weights[e][b]
    bands = spread(weights, even)
    for r in RELS:
        bands[r] = jnp.where(alive(even + r, length), 0.5 * bands[r], 0.0)
    store_bands(bands, bands_ref, count)
    per = chunks_ref.shape[0] // 2
    for g in range(2):
        chunks_ref[g * per : g * per + per, :] = to_chunks(ids[0], ids[1], g)
    width = w_ref.shape[1]
    for d in ds:
        d.store(0, jnp.zeros((80, width), F32), slice(None))
        d.store(2 * d.size - 64, jnp.zeros((64, width), F32), slice(None))

    diagonal = diagonals()

    def grad_steps(g, w):
        made = []

        def step(n):
            if not made:
                made.append(banded(bands_ref, g, w, count, diagonal))
                hl_refs[g][w * 160 : w * 160 + 160, :] = made[0]
            window_grads(ct_ref.at[g * 8 : g * 8 + 8], both_refs[g], made[0], ds[g], w, n)

        return [functools.partial(step, n) for n in range(0, width, 256)]

    def part_steps(g, c, put):
        d, oh_ref = ds[g], oh_refs[g]
        to = c * 128
        size = 128 if c < count else 64

        def mark():
            ids = chunks_ref[g * per + c : g * per + c + 1, :]
            oh_ref[:, to : to + 128] = one_hot_t(ids, vocab)
            if size < 128:
                zero = jnp.zeros((128 - size, width), BF16)
                high_ref[put + size : put + 128, :] = zero
                low_ref[put + size : put + 128, :] = zero

        def step(n):
            cols = slice(n, n + 128)
            taps = [jnp.broadcast_to(w_ref[k : k + 1, cols], (64, 128)) for k in range(TAPS)]
            for i in range(0, size, 64):
                near = d.load(to + 24 + i, to + 112 + i, cols)
                total = sum(taps[3 - k] * near[8 * k : 8 * k + 64] for k in range(TAPS))
                high, low = split(total)
                high_ref[put + i : put + i + 64, cols] = high
                low_ref[put + i : put + i + 64, cols] = low

        return [mark] + [functools.partial(step, n) for n in range(0, width, 128)]

    def sum_steps(g, cs, put):
        held = slice(put, put + 128 * len(cs))
        at = slice(cs[0] * 128, cs[-1] * 128 + 128)

        def step(n):
            cols = slice(n, n + 256)
            oh = oh_refs[g][:, at]
            both = jnp.concatenate([high_ref[held, cols], low_ref[held, cols]], axis=0)
            total = dot(jnp.concatenate([oh, oh], axis=1), both)
            if g == 0 and cs[0] == 0:
                grad_ref[:, cols] = total
            else:
                grad_ref[:, cols] += total

        return [functools.partial(step, n) for n in range(0, width, 256)]

    stages = [[], [], []]
    for t, (g, ws) in enumerate(batches(count, min(TABLE_BATCH, count))):
        cs = ws + [count] * (ws[-1] == count - 1)
        put = t % 3 * (TABLE_BATCH + 1) * 128
        stages[0].append(sum((grad_steps(g, w) for w in ws), []))
        stages[1].append(sum((part_steps(g, c, put + 128 * i) for i, c in enumerate(cs)), []))
        stages[2].append(sum_steps(g, cs, put))
    run_stages(stages, (0, 1, 2))


def near_kernel(
    even_ref, length_ref, weights_ref, chunks_ref, e_high, e_low, w_ref, b_ref, s_ref, both0, both1, d00, d01, d10, d11,
    small_ref, high0, low0, high1, low1,
    near_ref, q_ref, sums_ref, oh0, oh1, x_ref,
):
    oh_refs, both_refs = (oh0, oh1), (both0, both1)
    ds = (Halves(d00, d01), Halves(d10, d11))
    high_refs, low_refs = (high0, high1), (low0, low1)
    padded = weights_ref.shape[1]
    count = both0.shape[0] // 128
    chunks = count + 1
    vocab, width = e_high.shape
    per = chunks_ref.shape[0] // 2
    small_ref[...] = jnp.zeros_like(small_ref)
    near_ref[...] = jnp.zeros_like(near_ref)
    sums_ref[...] = jnp.zeros_like(sums_ref)
    diagonal = diagonals()
    bias = line(b_ref)
    turned = chunks_ref[...].astype(F32).T

    def slot(g, c):
        return (g * chunks + c) % RING * 128

    def bytes_at(g, c, first, size, cols):
        here = min(128 - first, size)
        at = slot(g, c) + first
        x = x_ref[at : at + here, cols]
        if here == size:
            return x
        at = slot(g, c + 1)
        return jnp.concatenate([x, x_ref[at : at + size - here, cols]], axis=0)

    def look_up_steps(g, cs):
        at = slice(cs[0] * 128, cs[-1] * 128 + 128)

        def mark(c):
            column = turned[:, g * per + c : g * per + c + 1]
            column = jnp.broadcast_to(column, (128, 128)).astype(BF16)
            for v in range(0, vocab, 128):
                match = column == (lanes((128, 128)) + v).astype(F32).astype(BF16)
                found = jnp.where(match, jnp.ones((), BF16), jnp.zeros((), BF16))
                oh_refs[g][c * 128 : c * 128 + 128, v : v + 128] = found

        def step(n):
            cols = slice(n, n + 256)
            oh = oh_refs[g][at, :]
            table = jnp.concatenate([e_high[:, cols], e_low[:, cols]], axis=0)
            x = dot(jnp.concatenate([oh, oh], axis=1), table)
            for i, c in enumerate(cs):
                to = slot(g, c)
                x_ref[to : to + 128, cols] = x[i * 128 : i * 128 + 128]

        return [functools.partial(mark, c) for c in cs] + [
            functools.partial(step, n) for n in range(0, width, 256)
        ]

    def conv_steps(g, c):
        at = c * 128
        size = 128 if c < count else 32
        step_size = min(size, 64)

        def step(n):
            cols = slice(n, n + 128)
            taps = [jnp.broadcast_to(w_ref[k : k + 1, cols], (step_size, 128)) for k in range(TAPS)]
            first = jnp.broadcast_to(bias[:, cols], (step_size, 128))
            sums = [sums_ref[8 * k : 8 * k + 8, cols] for k in range(TAPS + 1)]
            for i in range(at, at + size, step_size):
                d = ds[g].load(i + 48, i + 48 + step_size, cols)
                x = bytes_at(g, c, i - at, step_size + 24, cols)
                total = first
                products = [d]
                for k in range(TAPS):
                    near = x[8 * k : 8 * k + step_size]
                    total = total + taps[k] * near
                    products.append(d * near)
                for k, p in enumerate(products):
                    sums[k] = sums[k] + p.reshape(step_size // 8, 8, 128).sum(0)
                high, low = split(total)
                high_refs[g][i : i + step_size, cols] = high
                low_refs[g][i : i + step_size, cols] = low
            for k in range(TAPS + 1):
                sums_ref[8 * k : 8 * k + 8, cols] = sums[k]

        return [functools.partial(step, n) for n in range(0, width, 128)]

    def meet_steps(g, w):
        at = slice(w * 128, w * 128 + 160)

        made = []

        def product(n):
            cols = slice(n, n + 256)
            ct = both_refs[g][128 * w : 128 * w + 128, cols]
            wide = jnp.concatenate([high_refs[g][at, cols], low_refs[g][at, cols]], axis=1)
            both = dot(wide, jnp.concatenate([ct, ct], axis=1), NT)
            made.append(both if n == 0 else made.pop() + both)

        def meet():
            product = made.pop()
            for i, r in enumerate(RELS):
                total = jnp.zeros((8, 128), F32)
                for u in range(8):
                    row = 8 * (2 * u + 2 + r)
                    total = total + jnp.where(diagonal[u], product[row : row + 8], 0.0)
                found = jnp.sum(total, axis=0, keepdims=True)
                found = found + pltpu.roll(found, 64, 1)
                near_ref[i, 8 + w : 9 + w, g * 64 : g * 64 + 64] = found[:, g * 64 : g * 64 + 64]

        return [functools.partial(product, n) for n in range(0, width, 256)] + [meet]

    stages = [[], [], []]
    for g, ws in batches(count, MIX_BATCH):
        cs = ws + [count] * (ws[-1] == count - 1)
        stages[0].append(look_up_steps(g, cs))
        stages[1].append(sum((conv_steps(g, c) for c in cs), []))
        stages[2].append(sum((meet_steps(g, w) for w in ws), []))
    run_stages(stages, (0, 2, 4))

    for k in range(TAPS + 1):
        total = jnp.sum(sums_ref[8 * k : 8 * k + 8, :], axis=0, keepdims=True)
        to = (k + TAPS) % (TAPS + 1)
        small_ref[to : to + 1, :] = total
    even, length = even_ref[...], length_ref[...]
    weights = [[weights_ref[e * 4 + b] for b in range(4)] for e in range(2)]
    near = {}
    for i, r in enumerate(RELS):
        near[r] = jnp.where(alive(even + r, length), 0.5 * near_ref[i], 0.0)
    d_scores = []
    for e in range(2):
        d_weights = []
        for b, cases in enumerate(members(even, e)):
            total = None
            for rels, where in cases:
                part = sum(near[r] for r in rels)
                total = part if total is None else jnp.where(where, part, total)
            d_weights.append(total * (1.0 / (b + 1)))
        mean = sum(weights[e][b] * d_weights[b] for b in range(4))
        d_scores.append([weights[e][b] * (d_weights[b] - mean) for b in range(4)])
    own = lax.broadcasted_iota(I32, (padded, 128), 0) - 8
    own = (own >= 0) & (own < count)
    q = spread(d_scores, even)
    for r in RELS:
        q[r] = jnp.where(own & alive(even + r, length), q[r], 0.0)
    qe = q[0] + behind(q[2]) + ahead(q[-2])
    qo = q[1] + behind(q[3]) + ahead(q[-1])
    q_sum = jnp.sum(jnp.sum(qe + qo, axis=0, keepdims=True), axis=1, keepdims=True)
    shifted = [
        (ahead(qe), ahead(qo)),
        (qo, ahead(qe)),
        (qe, qo),
        (behind(qo), qe),
    ]
    q_ref[...] = jnp.zeros_like(q_ref)
    for g in range(2):
        for k in range(TAPS):
            flat = to_chunks(*shifted[k], g)
            for c in range(chunks):
                at = (g * chunks + c) * 128
                q_ref[k : k + 1, at : at + 128] = flat[c : c + 1]
    q1, rest = q_ref[...].astype(BF16), q_ref[...]
    rest = rest - q1.astype(F32)
    q2 = rest.astype(BF16)
    q3 = (rest - q2.astype(F32)).astype(BF16)
    q = jnp.concatenate([q1, q2, q3], axis=0)
    xs = chunks * 128
    hist = dot(q[:, :xs], oh_refs[0][...]) + dot(q[:, xs:], oh_refs[1][...])
    hist = hist[:8] + hist[8:16] + hist[16:]
    h_high, h_low = split(hist)
    looked = dot(jnp.concatenate([h_high, h_low], axis=0), e_high[...])
    looked = looked[:8] + looked[8:] + dot(h_high, e_low[...])
    for k in range(TAPS):
        small_ref[k : k + 1, :] += looked[k : k + 1] * line(s_ref)
        at = k * vocab
        small_ref[6 + at // width : 7 + at // width, at % width : at % width + vocab] = hist[k : k + 1]
    small_ref[TAPS : TAPS + 1, :] += q_sum * line(s_ref)
    small_ref[5:6, :] = q_sum * bias + jnp.sum(
        looked[:TAPS] * w_ref[...], axis=0, keepdims=True
    )


def latent_kernel(high0, low0, high1, low1, hl0, hl1, out_ref, latent_ref, sems):
    half, width = latent_ref.shape[1:]
    size = min(LATENT_BATCH, half // 8)
    copies = []
    for g, (high_ref, low_ref, hl_ref) in enumerate(((high0, low0, hl0), (high1, low1, hl1))):
        for w in range(half // 8):
            band = hl_ref[w * 160 : w * 160 + 160, :].astype(F32).T.astype(BF16)
            at = slice(w * 128, w * 128 + 160)
            for n in range(0, width, 256):
                both = dot(band, high_ref[at, n : n + 256])
                rest = dot(band[:64], low_ref[at, n : n + 256])
                out = both[:64] + both[64:] + rest
                latent_ref[g * 8 : g * 8 + 8, 8 * w : 8 * w + 8, n : n + 256] = out.reshape(8, 8, 256)
            if (w + 1) % size == 0:
                done = (pl.ds(g * 8, 8), pl.ds(8 * (w + 1 - size), 8 * size))
                copy = pltpu.make_async_copy(
                    latent_ref.at[done], out_ref.at[done], sems.at[len(copies)]
                )
                copy.start()
                copies.append(copy)
    for copy in copies:
        copy.wait()


def final_kernel(stages, place_ref, mine_ref, theirs_ref, w_ref, s_ref, ge_ref, gw_ref, gb_ref, gs_ref):
    vocab, width = ge_ref.shape
    places = [(0, None)]
    size = vocab
    for i in reversed(range(len(stages))):
        places = [(low | m << 2 * i, None) for m in range(1 << stages[i][2]) for low, _ in places]
    for stage in stages:
        size >>= stage[2]
    half = len(places) // 2
    pieces = [(mine_ref, p * (size + 8)) for p in range(half)]
    pieces += [(theirs_ref, p * (size + 8)) for p in range(half)]
    small = sum(ref[at + size : at + size + 8, :] for ref, at in pieces)
    hist = []
    for k in range(TAPS):
        at = k * vocab
        hist.append(small[6 + at // width : 7 + at // width, at % width : at % width + vocab])
    hist = jnp.concatenate(hist + [jnp.zeros((8 - TAPS, vocab), F32)], axis=0).T
    scaled = w_ref[...] * line(s_ref)
    for k in range(TAPS):
        turned = jnp.broadcast_to(hist[:, k : k + 1], (vocab, 128))
        for n in range(0, width, 128):
            add = turned * scaled[k : k + 1, n : n + 128]
            ge_ref[:, n : n + 128] = add if k == 0 else ge_ref[:, n : n + 128] + add
    for (mask, _), (ref, at) in zip(places, pieces):
        row, rest = 0, vocab
        for i, stage in enumerate(stages):
            rest >>= stage[2]
            row = row + (place_ref[i] ^ ((mask >> 2 * i) & 3)) * rest
        row = pl.multiple_of(row, 8)
        ge_ref[pl.ds(row, size), :] += ref[at : at + size, :]
    gw_ref[...] = small[:TAPS]
    gb_ref[...] = small[TAPS : TAPS + 1].reshape(width)
    gs_ref[...] = small[TAPS + 1 : TAPS + 2].reshape(width)


def in_vmem(*arrays):
    return [pltpu.with_memory_space_constraint(a, pltpu.VMEM) for a in arrays]


def in_hbm(*arrays):
    return [pltpu.with_memory_space_constraint(a, pltpu.HBM) for a in arrays]


def limit(megabytes):
    return pltpu.CompilerParams(vmem_limit_bytes=megabytes * 1024 * 1024)


def cost(flops, moved):
    return pl.CostEstimate(flops=flops, bytes_accessed=moved, transcendentals=0)


def vm(n):
    return [pl.BlockSpec(memory_space=pltpu.VMEM)] * n


def sm(n):
    return [pl.BlockSpec(memory_space=pltpu.SMEM)] * n


def sizes(span):
    count = span // 16
    chunks = count + 1
    per = -(-chunks // 8) * 8
    return count, chunks, per, (span + 16) * 8


def prep_call(start, lengths, ids, embedding, conv_weight, bias, scorer, cotangent):
    vocab, width = embedding.shape
    count, chunks, per, d_rows = sizes(ids.shape[1])
    return pl.pallas_call(
        prep_kernel,
        out_shape=(
            pltpu.VMEM((8, vocab), F32),
            pltpu.VMEM((vocab, width), BF16),
            pltpu.VMEM((vocab, width), BF16),
            pltpu.VMEM((8 + per, 128), I32),
            pltpu.VMEM((8 + per, 128), I32),
            pltpu.VMEM(ids.shape, I32),
            pltpu.VMEM(conv_weight.shape, F32),
            pltpu.VMEM(bias.shape, F32),
            pltpu.VMEM(scorer.shape, F32),
            pltpu.VMEM(cotangent.shape, F32),
        ),
        in_specs=[pl.BlockSpec(memory_space=pl.ANY)] * 8,
        out_specs=vm(10),
        scratch_shapes=[
            pltpu.SMEM((1,), I32),
            pltpu.SMEM(lengths.shape, I32),
            pltpu.VMEM((vocab, width), F32),
            pltpu.SemaphoreType.DMA((7 + ROWS // 2,)),
        ],
        compiler_params=limit(4),
        cost_estimate=cost(10**8, 10**6),
        name="prep",
    )(*in_hbm(start, lengths, ids, embedding, conv_weight, bias, scorer, cotangent))


def table_call(even, length, ids, left, right, table_scores, conv_weight, cotangent):
    rows, half, width = cotangent.shape
    count, chunks, per, d_rows = sizes(2 * half)
    vocab = table_scores.shape[1]
    return pl.pallas_call(
        table_kernel,
        out_shape=(
            pltpu.VMEM((vocab, width), F32),
            pltpu.VMEM((8, 8 + per, 128), F32),
            pltpu.VMEM((2 * per, 128), I32),
            pltpu.VMEM((160 * count, 128), BF16),
            pltpu.VMEM((160 * count, 128), BF16),
            pltpu.VMEM((128 * count, width), BF16),
            pltpu.VMEM((128 * count, width), BF16),
        )
        + (pltpu.VMEM((d_rows // 2, width), F32),) * 4,
        in_specs=vm(8),
        out_specs=vm(11),
        scratch_shapes=[
            pltpu.VMEM((8 + per, 256), I32),
            pltpu.VMEM((12 * count, 128), F32),
        ]
        + [pltpu.VMEM((vocab, chunks * 128), BF16)] * 2
        + [pltpu.VMEM((3 * (TABLE_BATCH + 1) * 128, width), BF16)] * 2,
        compiler_params=limit(12),
        cost_estimate=cost(8 * 10**9, 2 * 10**7),
        name="table_grad",
    )(*in_vmem(even, length, ids, left, right, table_scores, conv_weight, cotangent))


def near_call(even, length, weights, id_chunks, e_high, e_low, conv_weight, bias, scorer, *grads):
    count, chunks, per, d_rows = sizes(grads[0].shape[0] // 8)
    vocab, width = e_high.shape
    return pl.pallas_call(
        near_kernel,
        out_shape=[pltpu.VMEM((8, width), F32)] + [pltpu.VMEM((chunks * 128, width), BF16)] * 4,
        in_specs=vm(15),
        out_specs=vm(5),
        scratch_shapes=[
            pltpu.VMEM((6, 8 + per, 128), F32),
            pltpu.VMEM((8, 2 * chunks * 128), F32),
            pltpu.VMEM((8 * (TAPS + 1), width), F32),
        ]
        + [pltpu.VMEM((chunks * 128, vocab), BF16)] * 2
        + [pltpu.VMEM((RING * 128, width), F32)],
        compiler_params=limit(12),
        cost_estimate=cost(16 * 10**9, 4 * 10**7),
        name="near",
    )(*in_vmem(even, length, weights, id_chunks, e_high, e_low, conv_weight, bias, scorer, *grads))


def latent_call(kept, shape):
    rows, half, width = shape
    count = half // 8
    return pl.pallas_call(
        latent_kernel,
        out_shape=jax.ShapeDtypeStruct(shape, F32),
        in_specs=vm(6),
        out_specs=pl.BlockSpec(memory_space=pl.ANY),
        scratch_shapes=[
            pltpu.VMEM(shape, F32),
            pltpu.SemaphoreType.DMA((2 * (count // min(LATENT_BATCH, count)),)),
        ],
        compiler_params=limit(8),
        cost_estimate=cost(4 * 10**9, 10**7),
        name="latent",
    )(*in_vmem(*kept))


def partners(axis, mask):
    return [(i, i ^ mask) for i in range(lax.axis_size(axis))]


U32 = jnp.uint32


def offsets(axis, low, bits, size):
    me = (lax.axis_index(axis).astype(U32) >> low) & ((1 << bits) - 1)
    return [(me ^ m) * U32(size) for m in range(1 << bits)]


def part(v, at, size):
    return lax.dynamic_slice(v, (at, U32(0)), (size, v.shape[1]))


def scatter_sum(v, places, size, axis, low):
    total = part(v, places[0], size)
    for m in range(1, len(places)):
        total = total + lax.ppermute(part(v, places[m], size), axis, partners(axis, m << low))
    return total


def exchange_sum(v, axis, low, bits):
    return v + sum(
        lax.ppermute(v, axis, partners(axis, m << low)) for m in range(1, 1 << bits)
    )


def own_place(axis, low, bits):
    return (lax.axis_index(axis) >> low) & ((1 << bits) - 1)


def per_device(byte_ids, lengths, embedding, conv_weight, conv_bias, score_weight, cotangent):
    rows, span = byte_ids.shape
    vocab, width = embedding.shape
    count = span // 16
    seq = lax.axis_size("seq")
    start = (lax.axis_index("seq") * span).reshape(1)

    bits = seq.bit_length() - 1
    groups = [("seq", low, min(2, bits - low)) for low in range(0, bits, 2)]
    stages = [("dp", 0, lax.axis_size("dp").bit_length() - 1)] + groups[:-1]
    parts, places = [], []
    for axis, low, wide in stages:
        parts.append((parts[-1] if parts else vocab) >> wide)
        places.append(offsets(axis, low, wide, parts[-1]))
    here = jnp.stack([own_place(*stage) for stage in stages])
    byte_ids, start, here, places = lax.optimization_barrier((byte_ids, start, here, places))
    up = [(i, i + 1) for i in range(seq - 1)]
    left = lax.ppermute(byte_ids, "seq", up)
    right = lax.ppermute(byte_ids, "seq", [(j, i) for i, j in up])
    table_scores, e_high, e_low, even, length, ids, taps, bias, scorer, ct = prep_call(
        start, lengths, byte_ids, embedding, conv_weight, conv_bias, score_weight, cotangent
    )
    grad_table, weights, id_chunks, hl0, hl1, *grads = table_call(
        even, length, ids, left, right, table_scores, taps, ct
    )
    small, *kept = near_call(
        even, length, weights, id_chunks, e_high, e_low, taps, bias, scorer, *grads
    )
    latent = latent_call(kept + [hl0, hl1], cotangent.shape)

    total = grad_table
    for (axis, low, bits), size, at in zip(stages, parts, places):
        total = scatter_sum(total, at, size, axis, low)
    both = exchange_sum(jnp.concatenate([total, small], axis=0), *groups[-1])
    both, latent = lax.optimization_barrier((both, latent))
    for axis, low, wide in reversed(stages[1:]):
        got = [lax.ppermute(both, axis, partners(axis, m << low)) for m in range(1, 1 << wide)]
        both = jnp.concatenate([both] + got, axis=0)
    theirs = lax.ppermute(both, "dp", partners("dp", 1))

    grad_e, grad_w, grad_b, grad_s = pl.pallas_call(
        functools.partial(final_kernel, stages),
        out_shape=(
            jax.ShapeDtypeStruct((vocab, width), F32),
            jax.ShapeDtypeStruct((TAPS, width), F32),
            jax.ShapeDtypeStruct((width,), F32),
            jax.ShapeDtypeStruct((width,), F32),
        ),
        in_specs=sm(1) + vm(4),
        out_specs=vm(4),
        compiler_params=limit(4),
        name="final",
    )(here, *in_vmem(both, theirs, taps, scorer))
    return latent, grad_e, grad_w, grad_b, grad_s


def solution(mesh):
    placed = (P("dp", "seq"), P("dp"), P(), P(), P(), P(), P("dp", "seq", None))
    return jax.shard_map(
        per_device,
        mesh=mesh,
        in_specs=placed,
        out_specs=(P("dp", "seq", None), P(), P(), P(), P()),
        check_vma=False,
    )
```

```python
import functools

import jax
import jax.numpy as jnp
from jax import lax
from jax.experimental import pallas as pl
from jax.experimental.pallas import tpu as pltpu
from jax.sharding import PartitionSpec as P

F32, BF16, I32 = jnp.float32, jnp.bfloat16, jnp.int32
HIGH = lax.Precision.HIGHEST
ROWS = 16
TAPS = 4
TABLE_BATCH, MIX_BATCH, LATENT_BATCH = 2, 4, 4
RING = 18
RELS = (-2, -1, 0, 1, 2, 3)
NT = (((1,), (1,)), ((), ()))
TN = (((0,), (0,)), ((), ()))


def lanes(shape):
    return lax.broadcasted_iota(I32, shape, 1)


def line(ref):
    return ref[...].reshape(1, ref.shape[0])


def pick(x, index):
    return jnp.take_along_axis(x, index, axis=1, mode="promise_in_bounds")


def split(x):
    high = x.astype(BF16)
    return high, (x - high.astype(F32)).astype(BF16)


def dot(a, b, dims=(((1,), (0,)), ((), ()))):
    return lax.dot_general(a, b, dims, preferred_element_type=F32)


def ahead(x):
    lane = lanes(x.shape) % 8
    below = pltpu.roll(x, x.shape[0] - 1, 0)
    return jnp.where(lane == 7, pltpu.roll(below, 7, 1), pltpu.roll(x, 127, 1))


def behind(x):
    lane = lanes(x.shape) % 8
    above = pltpu.roll(x, 1, 0)
    return jnp.where(lane == 0, pltpu.roll(above, 121, 1), pltpu.roll(x, 1, 1))


def geometry(shape, start, len_ref):
    lane = lanes(shape)
    window = lax.broadcasted_iota(I32, shape, 0) - 8
    even = start + 16 * window + 2 * (lane % 8)
    length = jnp.zeros(shape, I32)
    for r in range(ROWS):
        length = jnp.where(lane // 8 == r, len_ref[r], length)
    return even, length


def alive(pos, length):
    return (pos >= 0) & (pos < length)


def members(even, parity):
    offset = (even + parity) % 3
    left = (even // 2) % 2 == 0
    out = [[((parity,), None)], [((0, 1), None)], [], []]
    for o in range(3):
        out[2].append((tuple(parity - o + i for i in range(3)), offset == o))
    out[3] = [((0, 1, 2, 3), left), ((-2, -1, 0, 1), ~left)]
    return out


def to_chunks(xe, xo, g):
    lane = lanes(xe.shape)
    place = (lane // 8 + 12) % 16
    index = g * 64 + (lane % 8) * 8 + place // 2
    y = jnp.where(place % 2 == 0, pick(xe, index), pick(xo, index))
    return jnp.where(lane < 32, pltpu.roll(y, 1, 0), y)[8:]


def prep_kernel(
    start_hbm, len_hbm, ids_hbm, e_hbm, w_hbm, b_hbm, s_hbm, ct_hbm,
    t_ref, high_ref, low_ref, even_ref, length_ref, ids_ref, w_ref, b_ref, s_ref, ct_ref,
    start_ref, len_ref, e_ref, sems,
):
    pairs = [
        (w_hbm, w_ref), (b_hbm, b_ref), (s_hbm, s_ref), (e_hbm, e_ref),
        (start_hbm, start_ref), (len_hbm, len_ref), (ids_hbm, ids_ref),
    ]
    copies = [pltpu.make_async_copy(a, b, sems.at[i]) for i, (a, b) in enumerate(pairs)]
    for r in range(0, ROWS, 2):
        rows = pl.ds(r, 2)
        copies.append(pltpu.make_async_copy(ct_hbm.at[rows], ct_ref.at[rows], sems.at[len(copies)]))
    for copy in copies:
        copy.start()
    for copy in copies[:4]:
        copy.wait()
    scaled = w_ref[...] * line(s_ref)
    wide = jnp.concatenate([scaled, jnp.zeros_like(scaled)], axis=0)
    t = lax.dot_general(wide, e_ref[...], NT, precision=HIGH, preferred_element_type=F32)
    b0 = jnp.sum(line(b_ref) * line(s_ref), axis=1, keepdims=True)
    row = lax.broadcasted_iota(I32, t.shape, 0)
    t_ref[...] = jnp.where(row == TAPS, b0, t)
    high_ref[...], low_ref[...] = split(e_ref[...])
    for copy in copies[4:]:
        copy.wait()
    even_ref[...], length_ref[...] = geometry(even_ref.shape, start_ref[0], len_ref)


def regroup(ids_ref, ids_scr, first, windows):
    for a in range(0, len(windows), 8):
        some = windows[a : a + 8]
        shape = (8, 128)
        lane = lanes(shape)
        window = lax.broadcasted_iota(I32, shape, 0) + some[0]
        column = 16 * some[0] // 128 * 128
        width = min(128, ids_ref.shape[1] - column)
        index = jnp.clip(16 * window + lane % 16 - column, 0, width - 1)
        for g in range(2):
            out = jnp.zeros(shape, I32)
            for r in range(8):
                row = ids_ref[g * 8 + r : g * 8 + r + 1, column : column + width]
                if width < 128:
                    row = jnp.concatenate([row, jnp.zeros((1, 128 - width), I32)], axis=1)
                found = pick(jnp.broadcast_to(row, shape), index)
                out = jnp.where(lane // 16 == r, found, out)
            at = first + a
            ids_scr[at : at + len(some), g * 128 : g * 128 + 128] = out[: len(some)]


def weigh(even, length, ids_scr, t_ref):
    shape = (ids_scr.shape[0], 128)
    lane = lanes(shape)
    live = [alive(even, length), alive(even + 1, length)]
    ids, terms = [], []
    for e in range(2):
        index = ((lane // 8) % 8) * 16 + 2 * (lane % 8) + e
        found = jnp.where(
            lane < 64, pick(ids_scr[:, :128], index), pick(ids_scr[:, 128:], index)
        )
        taps = []
        for k in range(TAPS):
            value = jnp.zeros(shape, F32)
            for half in range(t_ref.shape[1] // 128):
                row = jnp.broadcast_to(t_ref[k : k + 1, half * 128 : half * 128 + 128], shape)
                here = (found >= half * 128) & (found < half * 128 + 128)
                value = jnp.where(here, pick(row, found & 127), value)
            taps.append(jnp.where(live[e], value, 0.0))
        terms.append(taps)
        ids.append(jnp.where(live[e], found, -1))
    b0 = t_ref[TAPS : TAPS + 1, :128]
    (ae, ao) = terms
    ce = jnp.where(live[0], b0 + behind(ae[0] + ao[1]) + ae[2] + ao[3], 0.0)
    co = jnp.where(live[1], b0 + behind(ao[0]) + ae[1] + ao[2] + ahead(ae[3]), 0.0)
    at = {-2: behind(ce), -1: behind(co), 0: ce, 1: co, 2: ahead(ce), 3: ahead(co)}
    weights = []
    for e in range(2):
        scores = []
        for b, cases in enumerate(members(even, e)):
            total = None
            for rels, where in cases:
                part = sum(at[r] for r in rels)
                total = part if total is None else jnp.where(where, part, total)
            scores.append(total * (1.0 / (b + 1)))
        top = functools.reduce(jnp.maximum, scores)
        parts = [jnp.exp(s - top) for s in scores]
        norm = sum(parts)
        weights.append([p / norm for p in parts])
    return ids, weights


def spread(values, even):
    out = {r: 0.0 for r in RELS}
    for e in range(2):
        for b, cases in enumerate(members(even, e)):
            share = values[e][b] * (1.0 / (b + 1))
            for rels, where in cases:
                part = share if where is None else jnp.where(where, share, 0.0)
                for r in rels:
                    out[r] = out[r] + part
    return out


def diagonals():
    shape = (8, 128)
    row, lane = lax.broadcasted_iota(I32, shape, 0), lanes(shape)
    same = row == (lane % 64) // 8
    return [same & (lane % 8 == u) for u in range(8)]


def banded(bands_ref, g, w, count, diagonal):
    lane = lanes((8, 128))
    tiles = [jnp.zeros((8, 128), F32) for _ in range(20)]
    for i, r in enumerate(RELS):
        line = bands_ref[pl.ds((g * len(RELS) + i) * count + w, 1), :]
        high = line.astype(BF16).astype(F32)
        line = jnp.where(lanes((1, 128)) < 64, high, line - high)
        line = jnp.broadcast_to(line, (8, 128))
        for u in range(8):
            at = 2 * u + 2 + r
            tiles[at] = jnp.where(diagonal[u], line, tiles[at])
    return jnp.concatenate(tiles, axis=0).astype(BF16)


def store_bands(bands, bands_ref, count):
    lane = lanes(bands[0].shape)
    for i, r in enumerate(RELS):
        turned = pltpu.roll(bands[r], 64, 1)
        for g in range(2):
            both = jnp.where((lane < 64) == (g == 0), bands[r], turned)
            at = (g * len(RELS) + i) * count
            bands_ref[at : at + count, :] = both[8 : 8 + count]


def one_hot_t(ids, vocab):
    value = lax.broadcasted_iota(I32, (vocab, 128), 0).astype(F32).astype(BF16)
    match = value == jnp.broadcast_to(ids.astype(F32), (16, 128)).astype(BF16)[:1]
    return jnp.where(match, jnp.ones((), BF16), jnp.zeros((), BF16))


def weave(*parts):
    late = [0.9 if k == len(parts) - 2 else 0.0 for k in range(len(parts))]
    order = [((i + late[k]) / len(p), k, s) for k, p in enumerate(parts) for i, s in enumerate(p)]
    for _, _, step in sorted(order, key=lambda item: item[:2]):
        step()


def run_stages(stages, lags):
    for slot in range(len(stages[0]) + max(lags)):
        now = [(items, slot - lag) for items, lag in zip(stages, lags)]
        weave(*[items[t] for items, t in now if 0 <= t < len(items)])


def batches(count, size):
    return [(g, list(range(b, b + size))) for g in range(2) for b in range(0, count, size)]


class Halves:
    def __init__(self, first, second):
        self.refs, self.size = (first, second), first.shape[0]

    def parts(self, lo, hi):
        for ref, base in zip(self.refs, (0, self.size)):
            a, b = max(lo, base), min(hi, base + self.size)
            if a < b:
                yield ref, a - base, b - base, a - lo, b - lo

    def load(self, lo, hi, cols):
        found = [ref[a:b, cols] for ref, a, b, _, _ in self.parts(lo, hi)]
        return found[0] if len(found) == 1 else jnp.concatenate(found, axis=0)

    def store(self, lo, value, cols):
        for ref, a, b, i, j in self.parts(lo, lo + value.shape[0]):
            ref[a:b, cols] = value[i:j]


def window_grads(ct_ref, both_ref, hl, d, w, n):
    wide = jnp.concatenate([hl, hl], axis=1)
    at = 128 * w + 48
    cols = slice(n, n + 256)
    high, low = split(ct_ref[:, 8 * w : 8 * w + 8, cols].reshape(64, 256))
    both_ref[128 * w : 128 * w + 64, cols] = high
    both_ref[128 * w + 64 : 128 * w + 128, cols] = low
    grads = dot(wide, jnp.concatenate([high, high, low, low], axis=0))
    d.store(at, d.load(at, at + 32, cols) + grads[:32], cols)
    d.store(at + 32, grads[32:], cols)


def table_kernel(
    even_ref, length_ref, ids_ref, left_ref, right_ref, t_ref, w_ref, ct_ref,
    grad_ref, weights_ref, chunks_ref, hl0, hl1, both0, both1, d00, d01, d10, d11,
    ids_scr, bands_ref, *scratch,
):
    oh0, oh1, high_ref, low_ref = scratch
    oh_refs = (oh0, oh1)
    hl_refs, both_refs = (hl0, hl1), (both0, both1)
    ds = (Halves(d00, d01), Halves(d10, d11))
    count = ids_ref.shape[1] // 16
    chunks = count + 1
    vocab = t_ref.shape[1]
    even, length = even_ref[...], length_ref[...]
    ids_scr[...] = jnp.zeros_like(ids_scr)
    regroup(left_ref, ids_scr, 7, [count - 1])
    regroup(ids_ref, ids_scr, 8, list(range(count)))
    regroup(right_ref, ids_scr, 8 + count, [0])
    ids, weights = weigh(even, length, ids_scr, t_ref)
    for e in range(2):
        for b in range(4):
            weights_ref[e * 4 + b] = weights[e][b]
    bands = spread(weights, even)
    for r in RELS:
        bands[r] = jnp.where(alive(even + r, length), 0.5 * bands[r], 0.0)
    store_bands(bands, bands_ref, count)
    per = chunks_ref.shape[0] // 2
    for g in range(2):
        chunks_ref[g * per : g * per + per, :] = to_chunks(ids[0], ids[1], g)
    width = w_ref.shape[1]
    for d in ds:
        d.store(0, jnp.zeros((80, width), F32), slice(None))
        d.store(2 * d.size - 64, jnp.zeros((64, width), F32), slice(None))

    diagonal = diagonals()

    def grad_steps(g, w):
        made = []

        def step(n):
            if not made:
                made.append(banded(bands_ref, g, w, count, diagonal))
                hl_refs[g][w * 160 : w * 160 + 160, :] = made[0]
            window_grads(ct_ref.at[g * 8 : g * 8 + 8], both_refs[g], made[0], ds[g], w, n)

        return [functools.partial(step, n) for n in range(0, width, 256)]

    def part_steps(g, c, put):
        d, oh_ref = ds[g], oh_refs[g]
        to = c * 128
        size = 128 if c < count else 64

        def mark():
            ids = chunks_ref[g * per + c : g * per + c + 1, :]
            oh_ref[:, to : to + 128] = one_hot_t(ids, vocab)
            if size < 128:
                zero = jnp.zeros((128 - size, width), BF16)
                high_ref[put + size : put + 128, :] = zero
                low_ref[put + size : put + 128, :] = zero

        def step(n):
            cols = slice(n, n + 128)
            taps = [jnp.broadcast_to(w_ref[k : k + 1, cols], (64, 128)) for k in range(TAPS)]
            for i in range(0, size, 64):
                near = d.load(to + 24 + i, to + 112 + i, cols)
                total = sum(taps[3 - k] * near[8 * k : 8 * k + 64] for k in range(TAPS))
                high, low = split(total)
                high_ref[put + i : put + i + 64, cols] = high
                low_ref[put + i : put + i + 64, cols] = low

        return [mark] + [functools.partial(step, n) for n in range(0, width, 128)]

    def sum_steps(g, cs, put):
        held = slice(put, put + 128 * len(cs))
        at = slice(cs[0] * 128, cs[-1] * 128 + 128)

        def step(n):
            cols = slice(n, n + 256)
            oh = oh_refs[g][:, at]
            both = jnp.concatenate([high_ref[held, cols], low_ref[held, cols]], axis=0)
            total = dot(jnp.concatenate([oh, oh], axis=1), both)
            if g == 0 and cs[0] == 0:
                grad_ref[:, cols] = total
            else:
                grad_ref[:, cols] += total

        return [functools.partial(step, n) for n in range(0, width, 256)]

    stages = [[], [], []]
    for t, (g, ws) in enumerate(batches(count, min(TABLE_BATCH, count))):
        cs = ws + [count] * (ws[-1] == count - 1)
        put = t % 3 * (TABLE_BATCH + 1) * 128
        stages[0].append(sum((grad_steps(g, w) for w in ws), []))
        stages[1].append(sum((part_steps(g, c, put + 128 * i) for i, c in enumerate(cs)), []))
        stages[2].append(sum_steps(g, cs, put))
    run_stages(stages, (0, 1, 2))


def near_kernel(
    even_ref, length_ref, weights_ref, chunks_ref, e_high, e_low, w_ref, b_ref, s_ref, both0, both1, d00, d01, d10, d11,
    small_ref, high0, low0, high1, low1,
    near_ref, q_ref, sums_ref, oh0, oh1, x_ref,
):
    oh_refs, both_refs = (oh0, oh1), (both0, both1)
    ds = (Halves(d00, d01), Halves(d10, d11))
    high_refs, low_refs = (high0, high1), (low0, low1)
    padded = weights_ref.shape[1]
    count = both0.shape[0] // 128
    chunks = count + 1
    vocab, width = e_high.shape
    per = chunks_ref.shape[0] // 2
    small_ref[...] = jnp.zeros_like(small_ref)
    near_ref[...] = jnp.zeros_like(near_ref)
    sums_ref[...] = jnp.zeros_like(sums_ref)
    diagonal = diagonals()
    bias = line(b_ref)
    turned = chunks_ref[...].astype(F32).T

    def slot(g, c):
        return (g * chunks + c) % RING * 128

    def bytes_at(g, c, first, size, cols):
        here = min(128 - first, size)
        at = slot(g, c) + first
        x = x_ref[at : at + here, cols]
        if here == size:
            return x
        at = slot(g, c + 1)
        return jnp.concatenate([x, x_ref[at : at + size - here, cols]], axis=0)

    def look_up_steps(g, cs):
        at = slice(cs[0] * 128, cs[-1] * 128 + 128)

        def mark(c):
            column = turned[:, g * per + c : g * per + c + 1]
            column = jnp.broadcast_to(column, (128, 128)).astype(BF16)
            for v in range(0, vocab, 128):
                match = column == (lanes((128, 128)) + v).astype(F32).astype(BF16)
                found = jnp.where(match, jnp.ones((), BF16), jnp.zeros((), BF16))
                oh_refs[g][c * 128 : c * 128 + 128, v : v + 128] = found

        def step(n):
            cols = slice(n, n + 256)
            oh = oh_refs[g][at, :]
            table = jnp.concatenate([e_high[:, cols], e_low[:, cols]], axis=0)
            x = dot(jnp.concatenate([oh, oh], axis=1), table)
            for i, c in enumerate(cs):
                to = slot(g, c)
                x_ref[to : to + 128, cols] = x[i * 128 : i * 128 + 128]

        return [functools.partial(mark, c) for c in cs] + [
            functools.partial(step, n) for n in range(0, width, 256)
        ]

    def conv_steps(g, c):
        at = c * 128
        size = 128 if c < count else 32
        step_size = min(size, 64)

        def step(n):
            cols = slice(n, n + 128)
            taps = [jnp.broadcast_to(w_ref[k : k + 1, cols], (step_size, 128)) for k in range(TAPS)]
            first = jnp.broadcast_to(bias[:, cols], (step_size, 128))
            sums = [sums_ref[8 * k : 8 * k + 8, cols] for k in range(TAPS + 1)]
            for i in range(at, at + size, step_size):
                d = ds[g].load(i + 48, i + 48 + step_size, cols)
                x = bytes_at(g, c, i - at, step_size + 24, cols)
                total = first
                products = [d]
                for k in range(TAPS):
                    near = x[8 * k : 8 * k + step_size]
                    total = total + taps[k] * near
                    products.append(d * near)
                for k, p in enumerate(products):
                    sums[k] = sums[k] + p.reshape(step_size // 8, 8, 128).sum(0)
                high, low = split(total)
                high_refs[g][i : i + step_size, cols] = high
                low_refs[g][i : i + step_size, cols] = low
            for k in range(TAPS + 1):
                sums_ref[8 * k : 8 * k + 8, cols] = sums[k]

        return [functools.partial(step, n) for n in range(0, width, 128)]

    def meet_steps(g, w):
        at = slice(w * 128, w * 128 + 160)

        made = []

        def product(n):
            cols = slice(n, n + 256)
            ct = both_refs[g][128 * w : 128 * w + 128, cols]
            wide = jnp.concatenate([high_refs[g][at, cols], low_refs[g][at, cols]], axis=1)
            both = dot(wide, jnp.concatenate([ct, ct], axis=1), NT)
            made.append(both if n == 0 else made.pop() + both)

        def meet():
            product = made.pop()
            for i, r in enumerate(RELS):
                total = jnp.zeros((8, 128), F32)
                for u in range(8):
                    row = 8 * (2 * u + 2 + r)
                    total = total + jnp.where(diagonal[u], product[row : row + 8], 0.0)
                found = jnp.sum(total, axis=0, keepdims=True)
                found = found + pltpu.roll(found, 64, 1)
                near_ref[i, 8 + w : 9 + w, g * 64 : g * 64 + 64] = found[:, g * 64 : g * 64 + 64]

        return [functools.partial(product, n) for n in range(0, width, 256)] + [meet]

    stages = [[], [], []]
    for g, ws in batches(count, MIX_BATCH):
        cs = ws + [count] * (ws[-1] == count - 1)
        stages[0].append(look_up_steps(g, cs))
        stages[1].append(sum((conv_steps(g, c) for c in cs), []))
        stages[2].append(sum((meet_steps(g, w) for w in ws), []))
    run_stages(stages, (0, 2, 4))

    for k in range(TAPS + 1):
        total = jnp.sum(sums_ref[8 * k : 8 * k + 8, :], axis=0, keepdims=True)
        to = (k + TAPS) % (TAPS + 1)
        small_ref[to : to + 1, :] = total
    even, length = even_ref[...], length_ref[...]
    weights = [[weights_ref[e * 4 + b] for b in range(4)] for e in range(2)]
    near = {}
    for i, r in enumerate(RELS):
        near[r] = jnp.where(alive(even + r, length), 0.5 * near_ref[i], 0.0)
    d_scores = []
    for e in range(2):
        d_weights = []
        for b, cases in enumerate(members(even, e)):
            total = None
            for rels, where in cases:
                part = sum(near[r] for r in rels)
                total = part if total is None else jnp.where(where, part, total)
            d_weights.append(total * (1.0 / (b + 1)))
        mean = sum(weights[e][b] * d_weights[b] for b in range(4))
        d_scores.append([weights[e][b] * (d_weights[b] - mean) for b in range(4)])
    own = lax.broadcasted_iota(I32, (padded, 128), 0) - 8
    own = (own >= 0) & (own < count)
    q = spread(d_scores, even)
    for r in RELS:
        q[r] = jnp.where(own & alive(even + r, length), q[r], 0.0)
    qe = q[0] + behind(q[2]) + ahead(q[-2])
    qo = q[1] + behind(q[3]) + ahead(q[-1])
    q_sum = jnp.sum(jnp.sum(qe + qo, axis=0, keepdims=True), axis=1, keepdims=True)
    shifted = [
        (ahead(qe), ahead(qo)),
        (qo, ahead(qe)),
        (qe, qo),
        (behind(qo), qe),
    ]
    q_ref[...] = jnp.zeros_like(q_ref)
    for g in range(2):
        for k in range(TAPS):
            flat = to_chunks(*shifted[k], g)
            for c in range(chunks):
                at = (g * chunks + c) * 128
                q_ref[k : k + 1, at : at + 128] = flat[c : c + 1]
    q1, rest = q_ref[...].astype(BF16), q_ref[...]
    rest = rest - q1.astype(F32)
    q2 = rest.astype(BF16)
    q3 = (rest - q2.astype(F32)).astype(BF16)
    q = jnp.concatenate([q1, q2, q3], axis=0)
    xs = chunks * 128
    hist = dot(q[:, :xs], oh_refs[0][...]) + dot(q[:, xs:], oh_refs[1][...])
    hist = hist[:8] + hist[8:16] + hist[16:]
    h_high, h_low = split(hist)
    looked = dot(jnp.concatenate([h_high, h_low], axis=0), e_high[...])
    looked = looked[:8] + looked[8:] + dot(h_high, e_low[...])
    for k in range(TAPS):
        small_ref[k : k + 1, :] += looked[k : k + 1] * line(s_ref)
        at = k * vocab
        small_ref[6 + at // width : 7 + at // width, at % width : at % width + vocab] = hist[k : k + 1]
    small_ref[TAPS : TAPS + 1, :] += q_sum * line(s_ref)
    small_ref[5:6, :] = q_sum * bias + jnp.sum(
        looked[:TAPS] * w_ref[...], axis=0, keepdims=True
    )


def latent_kernel(high0, low0, high1, low1, hl0, hl1, out_ref, latent_ref, sems):
    half, width = latent_ref.shape[1:]
    size = min(LATENT_BATCH, half // 8)
    copies = []
    for g, (high_ref, low_ref, hl_ref) in enumerate(((high0, low0, hl0), (high1, low1, hl1))):
        for w in range(half // 8):
            band = hl_ref[w * 160 : w * 160 + 160, :].astype(F32).T.astype(BF16)
            at = slice(w * 128, w * 128 + 160)
            for n in range(0, width, 256):
                both = dot(band, high_ref[at, n : n + 256])
                rest = dot(band[:64], low_ref[at, n : n + 256])
                out = both[:64] + both[64:] + rest
                latent_ref[g * 8 : g * 8 + 8, 8 * w : 8 * w + 8, n : n + 256] = out.reshape(8, 8, 256)
            if (w + 1) % size == 0:
                done = (pl.ds(g * 8, 8), pl.ds(8 * (w + 1 - size), 8 * size))
                copy = pltpu.make_async_copy(
                    latent_ref.at[done], out_ref.at[done], sems.at[len(copies)]
                )
                copy.start()
                copies.append(copy)
    for copy in copies:
        copy.wait()


def final_kernel(stages, place_ref, mine_ref, theirs_ref, w_ref, s_ref, ge_ref, gw_ref, gb_ref, gs_ref):
    vocab, width = ge_ref.shape
    places = [(0, None)]
    size = vocab
    for i in reversed(range(len(stages))):
        places = [(low | m << 2 * i, None) for m in range(1 << stages[i][2]) for low, _ in places]
    for stage in stages:
        size >>= stage[2]
    half = len(places) // 2
    pieces = [(mine_ref, p * (size + 8)) for p in range(half)]
    pieces += [(theirs_ref, p * (size + 8)) for p in range(half)]
    small = sum(ref[at + size : at + size + 8, :] for ref, at in pieces)
    hist = []
    for k in range(TAPS):
        at = k * vocab
        hist.append(small[6 + at // width : 7 + at // width, at % width : at % width + vocab])
    hist = jnp.concatenate(hist + [jnp.zeros((8 - TAPS, vocab), F32)], axis=0).T
    scaled = w_ref[...] * line(s_ref)
    for v in range(0, vocab, 64):
        turned = [jnp.broadcast_to(hist[v : v + 64, k : k + 1], (64, 128)) for k in range(TAPS)]
        for n in range(0, width, 128):
            cols = slice(n, n + 128)
            ge_ref[v : v + 64, cols] = sum(turned[k] * scaled[k : k + 1, cols] for k in range(TAPS))
    for (mask, _), (ref, at) in zip(places, pieces):
        row, rest = 0, vocab
        for i, stage in enumerate(stages):
            rest >>= stage[2]
            row = row + (place_ref[i] ^ ((mask >> 2 * i) & 3)) * rest
        row = pl.multiple_of(row, 8)
        ge_ref[pl.ds(row, size), :] += ref[at : at + size, :]
    gw_ref[...] = small[:TAPS]
    gb_ref[...] = small[TAPS : TAPS + 1].reshape(width)
    gs_ref[...] = small[TAPS + 1 : TAPS + 2].reshape(width)


def in_vmem(*arrays):
    return [pltpu.with_memory_space_constraint(a, pltpu.VMEM) for a in arrays]


def in_hbm(*arrays):
    return [pltpu.with_memory_space_constraint(a, pltpu.HBM) for a in arrays]


def limit(megabytes):
    return pltpu.CompilerParams(vmem_limit_bytes=megabytes * 1024 * 1024)


def cost(flops, moved):
    return pl.CostEstimate(flops=flops, bytes_accessed=moved, transcendentals=0)


def vm(n):
    return [pl.BlockSpec(memory_space=pltpu.VMEM)] * n


def sm(n):
    return [pl.BlockSpec(memory_space=pltpu.SMEM)] * n


def sizes(span):
    count = span // 16
    chunks = count + 1
    per = -(-chunks // 8) * 8
    return count, chunks, per, (span + 16) * 8


def prep_call(start, lengths, ids, embedding, conv_weight, bias, scorer, cotangent):
    vocab, width = embedding.shape
    count, chunks, per, d_rows = sizes(ids.shape[1])
    return pl.pallas_call(
        prep_kernel,
        out_shape=(
            pltpu.VMEM((8, vocab), F32),
            pltpu.VMEM((vocab, width), BF16),
            pltpu.VMEM((vocab, width), BF16),
            pltpu.VMEM((8 + per, 128), I32),
            pltpu.VMEM((8 + per, 128), I32),
            pltpu.VMEM(ids.shape, I32),
            pltpu.VMEM(conv_weight.shape, F32),
            pltpu.VMEM(bias.shape, F32),
            pltpu.VMEM(scorer.shape, F32),
            pltpu.VMEM(cotangent.shape, F32),
        ),
        in_specs=[pl.BlockSpec(memory_space=pl.ANY)] * 8,
        out_specs=vm(10),
        scratch_shapes=[
            pltpu.SMEM((1,), I32),
            pltpu.SMEM(lengths.shape, I32),
            pltpu.VMEM((vocab, width), F32),
            pltpu.SemaphoreType.DMA((7 + ROWS // 2,)),
        ],
        compiler_params=limit(4),
        cost_estimate=cost(10**8, 10**6),
        name="prep",
    )(*in_hbm(start, lengths, ids, embedding, conv_weight, bias, scorer, cotangent))


def table_call(even, length, ids, left, right, table_scores, conv_weight, cotangent):
    rows, half, width = cotangent.shape
    count, chunks, per, d_rows = sizes(2 * half)
    vocab = table_scores.shape[1]
    return pl.pallas_call(
        table_kernel,
        out_shape=(
            pltpu.VMEM((vocab, width), F32),
            pltpu.VMEM((8, 8 + per, 128), F32),
            pltpu.VMEM((2 * per, 128), I32),
            pltpu.VMEM((160 * count, 128), BF16),
            pltpu.VMEM((160 * count, 128), BF16),
            pltpu.VMEM((128 * count, width), BF16),
            pltpu.VMEM((128 * count, width), BF16),
        )
        + (pltpu.VMEM((d_rows // 2, width), F32),) * 4,
        in_specs=vm(8),
        out_specs=vm(11),
        scratch_shapes=[
            pltpu.VMEM((8 + per, 256), I32),
            pltpu.VMEM((12 * count, 128), F32),
        ]
        + [pltpu.VMEM((vocab, chunks * 128), BF16)] * 2
        + [pltpu.VMEM((3 * (TABLE_BATCH + 1) * 128, width), BF16)] * 2,
        compiler_params=limit(12),
        cost_estimate=cost(8 * 10**9, 2 * 10**7),
        name="table_grad",
    )(*in_vmem(even, length, ids, left, right, table_scores, conv_weight, cotangent))


def near_call(even, length, weights, id_chunks, e_high, e_low, conv_weight, bias, scorer, *grads):
    count, chunks, per, d_rows = sizes(grads[0].shape[0] // 8)
    vocab, width = e_high.shape
    return pl.pallas_call(
        near_kernel,
        out_shape=[pltpu.VMEM((8, width), F32)] + [pltpu.VMEM((chunks * 128, width), BF16)] * 4,
        in_specs=vm(15),
        out_specs=vm(5),
        scratch_shapes=[
            pltpu.VMEM((6, 8 + per, 128), F32),
            pltpu.VMEM((8, 2 * chunks * 128), F32),
            pltpu.VMEM((8 * (TAPS + 1), width), F32),
        ]
        + [pltpu.VMEM((chunks * 128, vocab), BF16)] * 2
        + [pltpu.VMEM((RING * 128, width), F32)],
        compiler_params=limit(12),
        cost_estimate=cost(16 * 10**9, 4 * 10**7),
        name="near",
    )(*in_vmem(even, length, weights, id_chunks, e_high, e_low, conv_weight, bias, scorer, *grads))


def latent_call(kept, shape):
    rows, half, width = shape
    count = half // 8
    return pl.pallas_call(
        latent_kernel,
        out_shape=jax.ShapeDtypeStruct(shape, F32),
        in_specs=vm(6),
        out_specs=pl.BlockSpec(memory_space=pl.ANY),
        scratch_shapes=[
            pltpu.VMEM(shape, F32),
            pltpu.SemaphoreType.DMA((2 * (count // min(LATENT_BATCH, count)),)),
        ],
        compiler_params=limit(8),
        cost_estimate=cost(4 * 10**9, 10**7),
        name="latent",
    )(*in_vmem(*kept))


def partners(axis, mask):
    return [(i, i ^ mask) for i in range(lax.axis_size(axis))]


U32 = jnp.uint32


def offsets(axis, low, bits, size):
    me = (lax.axis_index(axis).astype(U32) >> low) & ((1 << bits) - 1)
    return [(me ^ m) * U32(size) for m in range(1 << bits)]


def part(v, at, size):
    return lax.dynamic_slice(v, (at, U32(0)), (size, v.shape[1]))


def scatter_sum(v, places, size, axis, low):
    total = part(v, places[0], size)
    for m in range(1, len(places)):
        total = total + lax.ppermute(part(v, places[m], size), axis, partners(axis, m << low))
    return total


def exchange_sum(v, axis, low, bits):
    return v + sum(
        lax.ppermute(v, axis, partners(axis, m << low)) for m in range(1, 1 << bits)
    )


def own_place(axis, low, bits):
    return (lax.axis_index(axis) >> low) & ((1 << bits) - 1)


def per_device(byte_ids, lengths, embedding, conv_weight, conv_bias, score_weight, cotangent):
    rows, span = byte_ids.shape
    vocab, width = embedding.shape
    count = span // 16
    seq = lax.axis_size("seq")
    start = (lax.axis_index("seq") * span).reshape(1)

    bits = seq.bit_length() - 1
    groups = [("seq", low, min(2, bits - low)) for low in range(0, bits, 2)]
    stages = [("dp", 0, lax.axis_size("dp").bit_length() - 1)] + groups[:-1]
    parts, places = [], []
    for axis, low, wide in stages:
        parts.append((parts[-1] if parts else vocab) >> wide)
        places.append(offsets(axis, low, wide, parts[-1]))
    here = jnp.stack([own_place(*stage) for stage in stages])
    byte_ids, start, here, places = lax.optimization_barrier((byte_ids, start, here, places))
    up = [(i, i + 1) for i in range(seq - 1)]
    left = lax.ppermute(byte_ids, "seq", up)
    right = lax.ppermute(byte_ids, "seq", [(j, i) for i, j in up])
    table_scores, e_high, e_low, even, length, ids, taps, bias, scorer, ct = prep_call(
        start, lengths, byte_ids, embedding, conv_weight, conv_bias, score_weight, cotangent
    )
    grad_table, weights, id_chunks, hl0, hl1, *grads = table_call(
        even, length, ids, left, right, table_scores, taps, ct
    )
    small, *kept = near_call(
        even, length, weights, id_chunks, e_high, e_low, taps, bias, scorer, *grads
    )
    latent = latent_call(kept + [hl0, hl1], cotangent.shape)

    total = grad_table
    for (axis, low, bits), size, at in zip(stages, parts, places):
        total = scatter_sum(total, at, size, axis, low)
    both = exchange_sum(jnp.concatenate([total, small], axis=0), *groups[-1])
    both, latent = lax.optimization_barrier((both, latent))
    for axis, low, wide in reversed(stages[1:]):
        got = [lax.ppermute(both, axis, partners(axis, m << low)) for m in range(1, 1 << wide)]
        both = jnp.concatenate([both] + got, axis=0)
    theirs = lax.ppermute(both, "dp", partners("dp", 1))

    grad_e, grad_w, grad_b, grad_s = pl.pallas_call(
        functools.partial(final_kernel, stages),
        out_shape=(
            jax.ShapeDtypeStruct((vocab, width), F32),
            jax.ShapeDtypeStruct((TAPS, width), F32),
            jax.ShapeDtypeStruct((width,), F32),
            jax.ShapeDtypeStruct((width,), F32),
        ),
        in_specs=sm(1) + vm(4),
        out_specs=vm(4),
        compiler_params=limit(4),
        name="final",
    )(here, *in_vmem(both, theirs, taps, scorer))
    return latent, grad_e, grad_w, grad_b, grad_s


def solution(mesh):
    placed = (P("dp", "seq"), P("dp"), P(), P(), P(), P(), P("dp", "seq", None))
    return jax.shard_map(
        per_device,
        mesh=mesh,
        in_specs=placed,
        out_specs=(P("dp", "seq", None), P(), P(), P(), P()),
        check_vma=False,
    )
```

```python
import functools

import jax
import jax.numpy as jnp
from jax import lax
from jax.experimental import pallas as pl
from jax.experimental.pallas import tpu as pltpu
from jax.sharding import PartitionSpec as P

F32, BF16, I32 = jnp.float32, jnp.bfloat16, jnp.int32
HIGH = lax.Precision.HIGHEST
ROWS = 16
TAPS = 4
TABLE_BATCH, MIX_BATCH, LATENT_BATCH = 1, 4, 4
RING = 18
RELS = (-2, -1, 0, 1, 2, 3)
NT = (((1,), (1,)), ((), ()))
TN = (((0,), (0,)), ((), ()))


def lanes(shape):
    return lax.broadcasted_iota(I32, shape, 1)


def line(ref):
    return ref[...].reshape(1, ref.shape[0])


def pick(x, index):
    return jnp.take_along_axis(x, index, axis=1, mode="promise_in_bounds")


def split(x):
    high = x.astype(BF16)
    return high, (x - high.astype(F32)).astype(BF16)


def dot(a, b, dims=(((1,), (0,)), ((), ()))):
    return lax.dot_general(a, b, dims, preferred_element_type=F32)


def ahead(x):
    lane = lanes(x.shape) % 8
    below = pltpu.roll(x, x.shape[0] - 1, 0)
    return jnp.where(lane == 7, pltpu.roll(below, 7, 1), pltpu.roll(x, 127, 1))


def behind(x):
    lane = lanes(x.shape) % 8
    above = pltpu.roll(x, 1, 0)
    return jnp.where(lane == 0, pltpu.roll(above, 121, 1), pltpu.roll(x, 1, 1))


def geometry(shape, start, len_ref):
    lane = lanes(shape)
    window = lax.broadcasted_iota(I32, shape, 0) - 8
    even = start + 16 * window + 2 * (lane % 8)
    length = jnp.zeros(shape, I32)
    for r in range(ROWS):
        length = jnp.where(lane // 8 == r, len_ref[r], length)
    return even, length


def alive(pos, length):
    return (pos >= 0) & (pos < length)


def members(even, parity):
    offset = (even + parity) % 3
    left = (even // 2) % 2 == 0
    out = [[((parity,), None)], [((0, 1), None)], [], []]
    for o in range(3):
        out[2].append((tuple(parity - o + i for i in range(3)), offset == o))
    out[3] = [((0, 1, 2, 3), left), ((-2, -1, 0, 1), ~left)]
    return out


def to_chunks(xe, xo, g):
    lane = lanes(xe.shape)
    place = (lane // 8 + 12) % 16
    index = g * 64 + (lane % 8) * 8 + place // 2
    y = jnp.where(place % 2 == 0, pick(xe, index), pick(xo, index))
    return jnp.where(lane < 32, pltpu.roll(y, 1, 0), y)[8:]


def prep_kernel(
    start_hbm, len_hbm, ids_hbm, e_hbm, w_hbm, b_hbm, s_hbm, ct_hbm,
    t_ref, high_ref, low_ref, even_ref, length_ref, ids_ref, w_ref, b_ref, s_ref, ct_ref,
    start_ref, len_ref, e_ref, sems,
):
    pairs = [
        (w_hbm, w_ref), (b_hbm, b_ref), (s_hbm, s_ref), (e_hbm, e_ref),
        (start_hbm, start_ref), (len_hbm, len_ref), (ids_hbm, ids_ref),
    ]
    copies = [pltpu.make_async_copy(a, b, sems.at[i]) for i, (a, b) in enumerate(pairs)]
    for r in range(0, ROWS, 2):
        rows = pl.ds(r, 2)
        copies.append(pltpu.make_async_copy(ct_hbm.at[rows], ct_ref.at[rows], sems.at[len(copies)]))
    for copy in copies:
        copy.start()
    for copy in copies[:4]:
        copy.wait()
    scaled = w_ref[...] * line(s_ref)
    wide = jnp.concatenate([scaled, jnp.zeros_like(scaled)], axis=0)
    t = lax.dot_general(wide, e_ref[...], NT, precision=HIGH, preferred_element_type=F32)
    b0 = jnp.sum(line(b_ref) * line(s_ref), axis=1, keepdims=True)
    row = lax.broadcasted_iota(I32, t.shape, 0)
    t_ref[...] = jnp.where(row == TAPS, b0, t)
    high_ref[...], low_ref[...] = split(e_ref[...])
    for copy in copies[4:]:
        copy.wait()
    even_ref[...], length_ref[...] = geometry(even_ref.shape, start_ref[0], len_ref)


def regroup(ids_ref, ids_scr, first, windows):
    for a in range(0, len(windows), 8):
        some = windows[a : a + 8]
        shape = (8, 128)
        lane = lanes(shape)
        window = lax.broadcasted_iota(I32, shape, 0) + some[0]
        column = 16 * some[0] // 128 * 128
        width = min(128, ids_ref.shape[1] - column)
        index = jnp.clip(16 * window + lane % 16 - column, 0, width - 1)
        for g in range(2):
            out = jnp.zeros(shape, I32)
            for r in range(8):
                row = ids_ref[g * 8 + r : g * 8 + r + 1, column : column + width]
                if width < 128:
                    row = jnp.concatenate([row, jnp.zeros((1, 128 - width), I32)], axis=1)
                found = pick(jnp.broadcast_to(row, shape), index)
                out = jnp.where(lane // 16 == r, found, out)
            at = first + a
            ids_scr[at : at + len(some), g * 128 : g * 128 + 128] = out[: len(some)]


def weigh(even, length, ids_scr, t_ref):
    shape = (ids_scr.shape[0], 128)
    lane = lanes(shape)
    live = [alive(even, length), alive(even + 1, length)]
    ids, terms = [], []
    for e in range(2):
        index = ((lane // 8) % 8) * 16 + 2 * (lane % 8) + e
        found = jnp.where(
            lane < 64, pick(ids_scr[:, :128], index), pick(ids_scr[:, 128:], index)
        )
        taps = []
        for k in range(TAPS):
            value = jnp.zeros(shape, F32)
            for half in range(t_ref.shape[1] // 128):
                row = jnp.broadcast_to(t_ref[k : k + 1, half * 128 : half * 128 + 128], shape)
                here = (found >= half * 128) & (found < half * 128 + 128)
                value = jnp.where(here, pick(row, found & 127), value)
            taps.append(jnp.where(live[e], value, 0.0))
        terms.append(taps)
        ids.append(jnp.where(live[e], found, -1))
    b0 = t_ref[TAPS : TAPS + 1, :128]
    (ae, ao) = terms
    ce = jnp.where(live[0], b0 + behind(ae[0] + ao[1]) + ae[2] + ao[3], 0.0)
    co = jnp.where(live[1], b0 + behind(ao[0]) + ae[1] + ao[2] + ahead(ae[3]), 0.0)
    at = {-2: behind(ce), -1: behind(co), 0: ce, 1: co, 2: ahead(ce), 3: ahead(co)}
    weights = []
    for e in range(2):
        scores = []
        for b, cases in enumerate(members(even, e)):
            total = None
            for rels, where in cases:
                part = sum(at[r] for r in rels)
                total = part if total is None else jnp.where(where, part, total)
            scores.append(total * (1.0 / (b + 1)))
        top = functools.reduce(jnp.maximum, scores)
        parts = [jnp.exp(s - top) for s in scores]
        norm = sum(parts)
        weights.append([p / norm for p in parts])
    return ids, weights


def spread(values, even):
    out = {r: 0.0 for r in RELS}
    for e in range(2):
        for b, cases in enumerate(members(even, e)):
            share = values[e][b] * (1.0 / (b + 1))
            for rels, where in cases:
                part = share if where is None else jnp.where(where, share, 0.0)
                for r in rels:
                    out[r] = out[r] + part
    return out


def diagonals():
    shape = (8, 128)
    row, lane = lax.broadcasted_iota(I32, shape, 0), lanes(shape)
    same = row == (lane % 64) // 8
    return [same & (lane % 8 == u) for u in range(8)]


def banded(bands_ref, g, w, count, diagonal):
    lane = lanes((8, 128))
    tiles = [jnp.zeros((8, 128), F32) for _ in range(20)]
    for i, r in enumerate(RELS):
        line = bands_ref[pl.ds((g * len(RELS) + i) * count + w, 1), :]
        high = line.astype(BF16).astype(F32)
        line = jnp.where(lanes((1, 128)) < 64, high, line - high)
        line = jnp.broadcast_to(line, (8, 128))
        for u in range(8):
            at = 2 * u + 2 + r
            tiles[at] = jnp.where(diagonal[u], line, tiles[at])
    return jnp.concatenate(tiles, axis=0).astype(BF16)


def store_bands(bands, bands_ref, count):
    lane = lanes(bands[0].shape)
    for i, r in enumerate(RELS):
        turned = pltpu.roll(bands[r], 64, 1)
        for g in range(2):
            both = jnp.where((lane < 64) == (g == 0), bands[r], turned)
            at = (g * len(RELS) + i) * count
            bands_ref[at : at + count, :] = both[8 : 8 + count]


def one_hot_t(ids, vocab):
    value = lax.broadcasted_iota(I32, (vocab, 128), 0).astype(F32).astype(BF16)
    match = value == jnp.broadcast_to(ids.astype(F32), (16, 128)).astype(BF16)[:1]
    return jnp.where(match, jnp.ones((), BF16), jnp.zeros((), BF16))


def weave(*parts):
    late = [0.9 if k == len(parts) - 2 else 0.0 for k in range(len(parts))]
    order = [((i + late[k]) / len(p), k, s) for k, p in enumerate(parts) for i, s in enumerate(p)]
    for _, _, step in sorted(order, key=lambda item: item[:2]):
        step()


def run_stages(stages, lags):
    for slot in range(len(stages[0]) + max(lags)):
        now = [(items, slot - lag) for items, lag in zip(stages, lags)]
        weave(*[items[t] for items, t in now if 0 <= t < len(items)])


def batches(count, size):
    return [(g, list(range(b, b + size))) for g in range(2) for b in range(0, count, size)]


class Halves:
    def __init__(self, first, second):
        self.refs, self.size = (first, second), first.shape[0]

    def parts(self, lo, hi):
        for ref, base in zip(self.refs, (0, self.size)):
            a, b = max(lo, base), min(hi, base + self.size)
            if a < b:
                yield ref, a - base, b - base, a - lo, b - lo

    def load(self, lo, hi, cols):
        found = [ref[a:b, cols] for ref, a, b, _, _ in self.parts(lo, hi)]
        return found[0] if len(found) == 1 else jnp.concatenate(found, axis=0)

    def store(self, lo, value, cols):
        for ref, a, b, i, j in self.parts(lo, lo + value.shape[0]):
            ref[a:b, cols] = value[i:j]


def window_grads(ct_ref, both_ref, hl, d, w, n):
    wide = jnp.concatenate([hl, hl], axis=1)
    at = 128 * w + 48
    cols = slice(n, n + 256)
    high, low = split(ct_ref[:, 8 * w : 8 * w + 8, cols].reshape(64, 256))
    both_ref[128 * w : 128 * w + 64, cols] = high
    both_ref[128 * w + 64 : 128 * w + 128, cols] = low
    grads = dot(wide, jnp.concatenate([high, high, low, low], axis=0))
    d.store(at, d.load(at, at + 32, cols) + grads[:32], cols)
    d.store(at + 32, grads[32:], cols)


def table_kernel(
    even_ref, length_ref, ids_ref, left_ref, right_ref, t_ref, w_ref, ct_ref,
    grad_ref, weights_ref, chunks_ref, hl0, hl1, both0, both1, d00, d01, d10, d11,
    ids_scr, bands_ref, *scratch,
):
    oh0, oh1, high_ref, low_ref = scratch
    oh_refs = (oh0, oh1)
    hl_refs, both_refs = (hl0, hl1), (both0, both1)
    ds = (Halves(d00, d01), Halves(d10, d11))
    count = ids_ref.shape[1] // 16
    chunks = count + 1
    vocab = t_ref.shape[1]
    even, length = even_ref[...], length_ref[...]
    ids_scr[...] = jnp.zeros_like(ids_scr)
    regroup(left_ref, ids_scr, 7, [count - 1])
    regroup(ids_ref, ids_scr, 8, list(range(count)))
    regroup(right_ref, ids_scr, 8 + count, [0])
    ids, weights = weigh(even, length, ids_scr, t_ref)
    for e in range(2):
        for b in range(4):
            weights_ref[e * 4 + b] = weights[e][b]
    bands = spread(weights, even)
    for r in RELS:
        bands[r] = jnp.where(alive(even + r, length), 0.5 * bands[r], 0.0)
    store_bands(bands, bands_ref, count)
    per = chunks_ref.shape[0] // 2
    for g in range(2):
        chunks_ref[g * per : g * per + per, :] = to_chunks(ids[0], ids[1], g)
    width = w_ref.shape[1]
    for d in ds:
        d.store(0, jnp.zeros((80, width), F32), slice(None))
        d.store(2 * d.size - 64, jnp.zeros((64, width), F32), slice(None))

    diagonal = diagonals()

    def grad_steps(g, w):
        made = []

        def step(n):
            if not made:
                made.append(banded(bands_ref, g, w, count, diagonal))
                hl_refs[g][w * 160 : w * 160 + 160, :] = made[0]
            window_grads(ct_ref.at[g * 8 : g * 8 + 8], both_refs[g], made[0], ds[g], w, n)

        return [functools.partial(step, n) for n in range(0, width, 256)]

    def part_steps(g, c, put):
        d, oh_ref = ds[g], oh_refs[g]
        to = c * 128
        size = 128 if c < count else 64

        def mark():
            ids = chunks_ref[g * per + c : g * per + c + 1, :]
            oh_ref[:, to : to + 128] = one_hot_t(ids, vocab)
            if size < 128:
                zero = jnp.zeros((128 - size, width), BF16)
                high_ref[put + size : put + 128, :] = zero
                low_ref[put + size : put + 128, :] = zero

        def step(n):
            cols = slice(n, n + 128)
            taps = [jnp.broadcast_to(w_ref[k : k + 1, cols], (64, 128)) for k in range(TAPS)]
            for i in range(0, size, 64):
                near = d.load(to + 24 + i, to + 112 + i, cols)
                total = sum(taps[3 - k] * near[8 * k : 8 * k + 64] for k in range(TAPS))
                high, low = split(total)
                high_ref[put + i : put + i + 64, cols] = high
                low_ref[put + i : put + i + 64, cols] = low

        return [mark] + [functools.partial(step, n) for n in range(0, width, 128)]

    def sum_steps(g, cs, put):
        held = slice(put, put + 128 * len(cs))
        at = slice(cs[0] * 128, cs[-1] * 128 + 128)

        def step(n):
            cols = slice(n, n + 256)
            oh = oh_refs[g][:, at]
            both = jnp.concatenate([high_ref[held, cols], low_ref[held, cols]], axis=0)
            total = dot(jnp.concatenate([oh, oh], axis=1), both)
            if g == 0 and cs[0] == 0:
                grad_ref[:, cols] = total
            else:
                grad_ref[:, cols] += total

        return [functools.partial(step, n) for n in range(0, width, 256)]

    stages = [[], [], []]
    for t, (g, ws) in enumerate(batches(count, min(TABLE_BATCH, count))):
        cs = ws + [count] * (ws[-1] == count - 1)
        put = t % 3 * (TABLE_BATCH + 1) * 128
        stages[0].append(sum((grad_steps(g, w) for w in ws), []))
        stages[1].append(sum((part_steps(g, c, put + 128 * i) for i, c in enumerate(cs)), []))
        stages[2].append(sum_steps(g, cs, put))
    run_stages(stages, (0, 1, 2))


def near_kernel(
    even_ref, length_ref, weights_ref, chunks_ref, e_high, e_low, w_ref, b_ref, s_ref, both0, both1, d00, d01, d10, d11,
    small_ref, high0, low0, high1, low1,
    near_ref, q_ref, sums_ref, oh0, oh1, x_ref,
):
    oh_refs, both_refs = (oh0, oh1), (both0, both1)
    ds = (Halves(d00, d01), Halves(d10, d11))
    high_refs, low_refs = (high0, high1), (low0, low1)
    padded = weights_ref.shape[1]
    count = both0.shape[0] // 128
    chunks = count + 1
    vocab, width = e_high.shape
    per = chunks_ref.shape[0] // 2
    small_ref[...] = jnp.zeros_like(small_ref)
    near_ref[...] = jnp.zeros_like(near_ref)
    sums_ref[...] = jnp.zeros_like(sums_ref)
    diagonal = diagonals()
    bias = line(b_ref)
    turned = chunks_ref[...].astype(F32).T

    def slot(g, c):
        return (g * chunks + c) % RING * 128

    def bytes_at(g, c, first, size, cols):
        here = min(128 - first, size)
        at = slot(g, c) + first
        x = x_ref[at : at + here, cols]
        if here == size:
            return x
        at = slot(g, c + 1)
        return jnp.concatenate([x, x_ref[at : at + size - here, cols]], axis=0)

    def look_up_steps(g, cs):
        at = slice(cs[0] * 128, cs[-1] * 128 + 128)

        def mark(c):
            column = turned[:, g * per + c : g * per + c + 1]
            column = jnp.broadcast_to(column, (128, 128)).astype(BF16)
            for v in range(0, vocab, 128):
                match = column == (lanes((128, 128)) + v).astype(F32).astype(BF16)
                found = jnp.where(match, jnp.ones((), BF16), jnp.zeros((), BF16))
                oh_refs[g][c * 128 : c * 128 + 128, v : v + 128] = found

        def step(n):
            cols = slice(n, n + 256)
            oh = oh_refs[g][at, :]
            table = jnp.concatenate([e_high[:, cols], e_low[:, cols]], axis=0)
            x = dot(jnp.concatenate([oh, oh], axis=1), table)
            for i, c in enumerate(cs):
                to = slot(g, c)
                x_ref[to : to + 128, cols] = x[i * 128 : i * 128 + 128]

        return [functools.partial(mark, c) for c in cs] + [
            functools.partial(step, n) for n in range(0, width, 256)
        ]

    def conv_steps(g, c):
        at = c * 128
        size = 128 if c < count else 32
        step_size = min(size, 64)

        def step(n):
            cols = slice(n, n + 128)
            taps = [jnp.broadcast_to(w_ref[k : k + 1, cols], (step_size, 128)) for k in range(TAPS)]
            first = jnp.broadcast_to(bias[:, cols], (step_size, 128))
            sums = [sums_ref[8 * k : 8 * k + 8, cols] for k in range(TAPS + 1)]
            for i in range(at, at + size, step_size):
                d = ds[g].load(i + 48, i + 48 + step_size, cols)
                x = bytes_at(g, c, i - at, step_size + 24, cols)
                total = first
                products = [d]
                for k in range(TAPS):
                    near = x[8 * k : 8 * k + step_size]
                    total = total + taps[k] * near
                    products.append(d * near)
                for k, p in enumerate(products):
                    sums[k] = sums[k] + p.reshape(step_size // 8, 8, 128).sum(0)
                high, low = split(total)
                high_refs[g][i : i + step_size, cols] = high
                low_refs[g][i : i + step_size, cols] = low
            for k in range(TAPS + 1):
                sums_ref[8 * k : 8 * k + 8, cols] = sums[k]

        return [functools.partial(step, n) for n in range(0, width, 128)]

    def meet_steps(g, w):
        at = slice(w * 128, w * 128 + 160)

        made = []

        def product(n):
            cols = slice(n, n + 256)
            ct = both_refs[g][128 * w : 128 * w + 128, cols]
            wide = jnp.concatenate([high_refs[g][at, cols], low_refs[g][at, cols]], axis=1)
            both = dot(wide, jnp.concatenate([ct, ct], axis=1), NT)
            made.append(both if n == 0 else made.pop() + both)

        def meet():
            product = made.pop()
            for i, r in enumerate(RELS):
                total = jnp.zeros((8, 128), F32)
                for u in range(8):
                    row = 8 * (2 * u + 2 + r)
                    total = total + jnp.where(diagonal[u], product[row : row + 8], 0.0)
                found = jnp.sum(total, axis=0, keepdims=True)
                found = found + pltpu.roll(found, 64, 1)
                near_ref[i, 8 + w : 9 + w, g * 64 : g * 64 + 64] = found[:, g * 64 : g * 64 + 64]

        return [functools.partial(product, n) for n in range(0, width, 256)] + [meet]

    stages = [[], [], []]
    for g, ws in batches(count, MIX_BATCH):
        cs = ws + [count] * (ws[-1] == count - 1)
        stages[0].append(look_up_steps(g, cs))
        stages[1].append(sum((conv_steps(g, c) for c in cs), []))
        stages[2].append(sum((meet_steps(g, w) for w in ws), []))
    run_stages(stages, (0, 2, 4))

    for k in range(TAPS + 1):
        total = jnp.sum(sums_ref[8 * k : 8 * k + 8, :], axis=0, keepdims=True)
        to = (k + TAPS) % (TAPS + 1)
        small_ref[to : to + 1, :] = total
    even, length = even_ref[...], length_ref[...]
    weights = [[weights_ref[e * 4 + b] for b in range(4)] for e in range(2)]
    near = {}
    for i, r in enumerate(RELS):
        near[r] = jnp.where(alive(even + r, length), 0.5 * near_ref[i], 0.0)
    d_scores = []
    for e in range(2):
        d_weights = []
        for b, cases in enumerate(members(even, e)):
            total = None
            for rels, where in cases:
                part = sum(near[r] for r in rels)
                total = part if total is None else jnp.where(where, part, total)
            d_weights.append(total * (1.0 / (b + 1)))
        mean = sum(weights[e][b] * d_weights[b] for b in range(4))
        d_scores.append([weights[e][b] * (d_weights[b] - mean) for b in range(4)])
    own = lax.broadcasted_iota(I32, (padded, 128), 0) - 8
    own = (own >= 0) & (own < count)
    q = spread(d_scores, even)
    for r in RELS:
        q[r] = jnp.where(own & alive(even + r, length), q[r], 0.0)
    qe = q[0] + behind(q[2]) + ahead(q[-2])
    qo = q[1] + behind(q[3]) + ahead(q[-1])
    q_sum = jnp.sum(jnp.sum(qe + qo, axis=0, keepdims=True), axis=1, keepdims=True)
    shifted = [
        (ahead(qe), ahead(qo)),
        (qo, ahead(qe)),
        (qe, qo),
        (behind(qo), qe),
    ]
    q_ref[...] = jnp.zeros_like(q_ref)
    for g in range(2):
        for k in range(TAPS):
            flat = to_chunks(*shifted[k], g)
            for c in range(chunks):
                at = (g * chunks + c) * 128
                q_ref[k : k + 1, at : at + 128] = flat[c : c + 1]
    q1, rest = q_ref[...].astype(BF16), q_ref[...]
    rest = rest - q1.astype(F32)
    q2 = rest.astype(BF16)
    q3 = (rest - q2.astype(F32)).astype(BF16)
    q = jnp.concatenate([q1, q2, q3], axis=0)
    xs = chunks * 128
    hist = dot(q[:, :xs], oh_refs[0][...]) + dot(q[:, xs:], oh_refs[1][...])
    hist = hist[:8] + hist[8:16] + hist[16:]
    h_high, h_low = split(hist)
    looked = dot(jnp.concatenate([h_high, h_low], axis=0), e_high[...])
    looked = looked[:8] + looked[8:] + dot(h_high, e_low[...])
    for k in range(TAPS):
        small_ref[k : k + 1, :] += looked[k : k + 1] * line(s_ref)
        at = k * vocab
        small_ref[6 + at // width : 7 + at // width, at % width : at % width + vocab] = hist[k : k + 1]
    small_ref[TAPS : TAPS + 1, :] += q_sum * line(s_ref)
    small_ref[5:6, :] = q_sum * bias + jnp.sum(
        looked[:TAPS] * w_ref[...], axis=0, keepdims=True
    )


def latent_kernel(high0, low0, high1, low1, hl0, hl1, out_ref, latent_ref, sems):
    half, width = latent_ref.shape[1:]
    size = min(LATENT_BATCH, half // 8)
    copies = []
    for g, (high_ref, low_ref, hl_ref) in enumerate(((high0, low0, hl0), (high1, low1, hl1))):
        for w in range(half // 8):
            band = hl_ref[w * 160 : w * 160 + 160, :].astype(F32).T.astype(BF16)
            at = slice(w * 128, w * 128 + 160)
            for n in range(0, width, 256):
                both = dot(band, high_ref[at, n : n + 256])
                rest = dot(band[:64], low_ref[at, n : n + 256])
                out = both[:64] + both[64:] + rest
                latent_ref[g * 8 : g * 8 + 8, 8 * w : 8 * w + 8, n : n + 256] = out.reshape(8, 8, 256)
            if (w + 1) % size == 0:
                done = (pl.ds(g * 8, 8), pl.ds(8 * (w + 1 - size), 8 * size))
                copy = pltpu.make_async_copy(
                    latent_ref.at[done], out_ref.at[done], sems.at[len(copies)]
                )
                copy.start()
                copies.append(copy)
    for copy in copies:
        copy.wait()


def final_kernel(stages, place_ref, mine_ref, theirs_ref, w_ref, s_ref, ge_ref, gw_ref, gb_ref, gs_ref):
    vocab, width = ge_ref.shape
    places = [(0, None)]
    size = vocab
    for i in reversed(range(len(stages))):
        places = [(low | m << 2 * i, None) for m in range(1 << stages[i][2]) for low, _ in places]
    for stage in stages:
        size >>= stage[2]
    half = len(places) // 2
    pieces = [(mine_ref, p * (size + 8)) for p in range(half)]
    pieces += [(theirs_ref, p * (size + 8)) for p in range(half)]
    small = sum(ref[at + size : at + size + 8, :] for ref, at in pieces)
    hist = []
    for k in range(TAPS):
        at = k * vocab
        hist.append(small[6 + at // width : 7 + at // width, at % width : at % width + vocab])
    hist = jnp.concatenate(hist + [jnp.zeros((8 - TAPS, vocab), F32)], axis=0).T
    scaled = w_ref[...] * line(s_ref)
    for v in range(0, vocab, 64):
        turned = [jnp.broadcast_to(hist[v : v + 64, k : k + 1], (64, 128)) for k in range(TAPS)]
        for n in range(0, width, 128):
            cols = slice(n, n + 128)
            ge_ref[v : v + 64, cols] = sum(turned[k] * scaled[k : k + 1, cols] for k in range(TAPS))
    for (mask, _), (ref, at) in zip(places, pieces):
        row, rest = 0, vocab
        for i, stage in enumerate(stages):
            rest >>= stage[2]
            row = row + (place_ref[i] ^ ((mask >> 2 * i) & 3)) * rest
        row = pl.multiple_of(row, 8)
        ge_ref[pl.ds(row, size), :] += ref[at : at + size, :]
    gw_ref[...] = small[:TAPS]
    gb_ref[...] = small[TAPS : TAPS + 1].reshape(width)
    gs_ref[...] = small[TAPS + 1 : TAPS + 2].reshape(width)


def in_vmem(*arrays):
    return [pltpu.with_memory_space_constraint(a, pltpu.VMEM) for a in arrays]


def in_hbm(*arrays):
    return [pltpu.with_memory_space_constraint(a, pltpu.HBM) for a in arrays]


def limit(megabytes):
    return pltpu.CompilerParams(vmem_limit_bytes=megabytes * 1024 * 1024)


def cost(flops, moved):
    return pl.CostEstimate(flops=flops, bytes_accessed=moved, transcendentals=0)


def vm(n):
    return [pl.BlockSpec(memory_space=pltpu.VMEM)] * n


def sm(n):
    return [pl.BlockSpec(memory_space=pltpu.SMEM)] * n


def sizes(span):
    count = span // 16
    chunks = count + 1
    per = -(-chunks // 8) * 8
    return count, chunks, per, (span + 16) * 8


def prep_call(start, lengths, ids, embedding, conv_weight, bias, scorer, cotangent):
    vocab, width = embedding.shape
    count, chunks, per, d_rows = sizes(ids.shape[1])
    return pl.pallas_call(
        prep_kernel,
        out_shape=(
            pltpu.VMEM((8, vocab), F32),
            pltpu.VMEM((vocab, width), BF16),
            pltpu.VMEM((vocab, width), BF16),
            pltpu.VMEM((8 + per, 128), I32),
            pltpu.VMEM((8 + per, 128), I32),
            pltpu.VMEM(ids.shape, I32),
            pltpu.VMEM(conv_weight.shape, F32),
            pltpu.VMEM(bias.shape, F32),
            pltpu.VMEM(scorer.shape, F32),
            pltpu.VMEM(cotangent.shape, F32),
        ),
        in_specs=[pl.BlockSpec(memory_space=pl.ANY)] * 8,
        out_specs=vm(10),
        scratch_shapes=[
            pltpu.SMEM((1,), I32),
            pltpu.SMEM(lengths.shape, I32),
            pltpu.VMEM((vocab, width), F32),
            pltpu.SemaphoreType.DMA((7 + ROWS // 2,)),
        ],
        compiler_params=limit(4),
        cost_estimate=cost(10**8, 10**6),
        name="prep",
    )(*in_hbm(start, lengths, ids, embedding, conv_weight, bias, scorer, cotangent))


def table_call(even, length, ids, left, right, table_scores, conv_weight, cotangent):
    rows, half, width = cotangent.shape
    count, chunks, per, d_rows = sizes(2 * half)
    vocab = table_scores.shape[1]
    return pl.pallas_call(
        table_kernel,
        out_shape=(
            pltpu.VMEM((vocab, width), F32),
            pltpu.VMEM((8, 8 + per, 128), F32),
            pltpu.VMEM((2 * per, 128), I32),
            pltpu.VMEM((160 * count, 128), BF16),
            pltpu.VMEM((160 * count, 128), BF16),
            pltpu.VMEM((128 * count, width), BF16),
            pltpu.VMEM((128 * count, width), BF16),
        )
        + (pltpu.VMEM((d_rows // 2, width), F32),) * 4,
        in_specs=vm(8),
        out_specs=vm(11),
        scratch_shapes=[
            pltpu.VMEM((8 + per, 256), I32),
            pltpu.VMEM((12 * count, 128), F32),
        ]
        + [pltpu.VMEM((vocab, chunks * 128), BF16)] * 2
        + [pltpu.VMEM((3 * (TABLE_BATCH + 1) * 128, width), BF16)] * 2,
        compiler_params=limit(12),
        cost_estimate=cost(8 * 10**9, 2 * 10**7),
        name="table_grad",
    )(*in_vmem(even, length, ids, left, right, table_scores, conv_weight, cotangent))


def near_call(even, length, weights, id_chunks, e_high, e_low, conv_weight, bias, scorer, *grads):
    count, chunks, per, d_rows = sizes(grads[0].shape[0] // 8)
    vocab, width = e_high.shape
    return pl.pallas_call(
        near_kernel,
        out_shape=[pltpu.VMEM((8, width), F32)] + [pltpu.VMEM((chunks * 128, width), BF16)] * 4,
        in_specs=vm(15),
        out_specs=vm(5),
        scratch_shapes=[
            pltpu.VMEM((6, 8 + per, 128), F32),
            pltpu.VMEM((8, 2 * chunks * 128), F32),
            pltpu.VMEM((8 * (TAPS + 1), width), F32),
        ]
        + [pltpu.VMEM((chunks * 128, vocab), BF16)] * 2
        + [pltpu.VMEM((RING * 128, width), F32)],
        compiler_params=limit(12),
        cost_estimate=cost(16 * 10**9, 4 * 10**7),
        name="near",
    )(*in_vmem(even, length, weights, id_chunks, e_high, e_low, conv_weight, bias, scorer, *grads))


def latent_call(kept, shape):
    rows, half, width = shape
    count = half // 8
    return pl.pallas_call(
        latent_kernel,
        out_shape=jax.ShapeDtypeStruct(shape, F32),
        in_specs=vm(6),
        out_specs=pl.BlockSpec(memory_space=pl.ANY),
        scratch_shapes=[
            pltpu.VMEM(shape, F32),
            pltpu.SemaphoreType.DMA((2 * (count // min(LATENT_BATCH, count)),)),
        ],
        compiler_params=limit(8),
        cost_estimate=cost(4 * 10**9, 10**7),
        name="latent",
    )(*in_vmem(*kept))


def partners(axis, mask):
    return [(i, i ^ mask) for i in range(lax.axis_size(axis))]


U32 = jnp.uint32


def offsets(axis, low, bits, size):
    me = (lax.axis_index(axis).astype(U32) >> low) & ((1 << bits) - 1)
    return [(me ^ m) * U32(size) for m in range(1 << bits)]


def part(v, at, size):
    return lax.dynamic_slice(v, (at, U32(0)), (size, v.shape[1]))


def scatter_sum(v, places, size, axis, low):
    total = part(v, places[0], size)
    for m in range(1, len(places)):
        total = total + lax.ppermute(part(v, places[m], size), axis, partners(axis, m << low))
    return total


def exchange_sum(v, axis, low, bits):
    return v + sum(
        lax.ppermute(v, axis, partners(axis, m << low)) for m in range(1, 1 << bits)
    )


def own_place(axis, low, bits):
    return (lax.axis_index(axis) >> low) & ((1 << bits) - 1)


def per_device(byte_ids, lengths, embedding, conv_weight, conv_bias, score_weight, cotangent):
    rows, span = byte_ids.shape
    vocab, width = embedding.shape
    count = span // 16
    seq = lax.axis_size("seq")
    start = (lax.axis_index("seq") * span).reshape(1)

    bits = seq.bit_length() - 1
    groups = [("seq", low, min(2, bits - low)) for low in range(0, bits, 2)]
    stages = [("dp", 0, lax.axis_size("dp").bit_length() - 1)] + groups[:-1]
    parts, places = [], []
    for axis, low, wide in stages:
        parts.append((parts[-1] if parts else vocab) >> wide)
        places.append(offsets(axis, low, wide, parts[-1]))
    here = jnp.stack([own_place(*stage) for stage in stages])
    byte_ids, start, here, places = lax.optimization_barrier((byte_ids, start, here, places))
    up = [(i, i + 1) for i in range(seq - 1)]
    left = lax.ppermute(byte_ids, "seq", up)
    right = lax.ppermute(byte_ids, "seq", [(j, i) for i, j in up])
    table_scores, e_high, e_low, even, length, ids, taps, bias, scorer, ct = prep_call(
        start, lengths, byte_ids, embedding, conv_weight, conv_bias, score_weight, cotangent
    )
    grad_table, weights, id_chunks, hl0, hl1, *grads = table_call(
        even, length, ids, left, right, table_scores, taps, ct
    )
    small, *kept = near_call(
        even, length, weights, id_chunks, e_high, e_low, taps, bias, scorer, *grads
    )
    latent = latent_call(kept + [hl0, hl1], cotangent.shape)

    total = grad_table
    for (axis, low, bits), size, at in zip(stages, parts, places):
        total = scatter_sum(total, at, size, axis, low)
    both = exchange_sum(jnp.concatenate([total, small], axis=0), *groups[-1])
    both, latent = lax.optimization_barrier((both, latent))
    for axis, low, wide in reversed(stages[1:]):
        got = [lax.ppermute(both, axis, partners(axis, m << low)) for m in range(1, 1 << wide)]
        both = jnp.concatenate([both] + got, axis=0)
    theirs = lax.ppermute(both, "dp", partners("dp", 1))

    grad_e, grad_w, grad_b, grad_s = pl.pallas_call(
        functools.partial(final_kernel, stages),
        out_shape=(
            jax.ShapeDtypeStruct((vocab, width), F32),
            jax.ShapeDtypeStruct((TAPS, width), F32),
            jax.ShapeDtypeStruct((width,), F32),
            jax.ShapeDtypeStruct((width,), F32),
        ),
        in_specs=sm(1) + vm(4),
        out_specs=vm(4),
        compiler_params=limit(4),
        name="final",
    )(here, *in_vmem(both, theirs, taps, scorer))
    return latent, grad_e, grad_w, grad_b, grad_s


def solution(mesh):
    placed = (P("dp", "seq"), P("dp"), P(), P(), P(), P(), P("dp", "seq", None))
    return jax.shard_map(
        per_device,
        mesh=mesh,
        in_specs=placed,
        out_specs=(P("dp", "seq", None), P(), P(), P(), P()),
        check_vma=False,
    )
```
